128 devices in a mesh: row: 8 (over y, z_lo), col: 8 (over x, core), feat: 2 (over z_hi).
Axes of the slice: x: 4, y: 4, z: 4 (z_hi: 2, z_lo: 2; z = z_hi * 2 + z_lo), core: 2. Of those that a mesh axis runs over, the one named last changes fastest.
Arguments:
- features: bfloat16 [32768, 128], P(('col', 'row')), may hold values from -6 to 6
- weight: bfloat16 [128, 256], P(None, 'feat'), may hold values from -0.5 to 0.5
- hidden_bias: float32 [256], P('feat'), may hold values from -4 to 4
- adjacency_tiles: bfloat16 [8, 8, 640, 128, 128], P('row', 'col'), may hold values from -0.078125 to 0.078125
- tile_rows: int32 [8, 8, 640], P('row', 'col'), may hold values from 0 to 31
- tile_columns: int32 [8, 8, 640], P('row', 'col'), may hold values from 0 to 31
- tile_count: int32 [8, 8], P('row', 'col'), may hold values from 1 to 640, as said below
- cotangent: bfloat16 [32768, 256], P(('row', 'col'), 'feat'), may hold values from -6 to 6
Outputs:
- activations: bfloat16 [32768, 256], P(('row', 'col'), 'feat')
- grad_features: float32 [32768, 128], P(('col', 'row'))
- grad_weight: float32 [128, 256], P(None, 'feat')
- grad_bias: float32 [256], P('feat')
The draws below stay inside these ranges and needn't reach their ends.
Inputs may be any that keep to these rules, and one draw needn't show every extreme that they name: `tile_count`: tiles at or past this count on a device are ignored; some device uses all 640.
All inputs are finite; a program needn't handle non-finite values.
Results may differ from the reference program's by a relative error of at most 0.024.
Values may be sent and summed in bfloat16 or wider, within the bound.
No kernel may reach another device: no remote copies, remote signals or barrier semaphores. Data moves between devices by JAX's collectives and lax.ppermute only.
A program may use at most 128 MiB of HBM per device.

```python
import jax
import jax.numpy as jnp
from jax import lax

FIN = 128
HID = 256
TILE = 128
RB = 4
MAXT = 640
NODES = 32768
N_ROW = 8
N_COL = 8


def draw_tile_rows(key, part):
    key = jax.random.fold_in(key, 11)
    first_key, second_key = jax.random.split(key)
    shape = (N_ROW, N_COL, MAXT)
    first = jax.random.randint(first_key, shape, 0, RB * N_COL, dtype=jnp.int32)
    second = jax.random.randint(second_key, shape, 0, RB * N_COL, dtype=jnp.int32)
    return jnp.minimum(first, second)


def draw_tile_columns(key, part):
    key = jax.random.fold_in(key, 23)
    return jax.random.randint(key, (N_ROW, N_COL, MAXT), 0, RB * N_ROW, dtype=jnp.int32)


def draw_tile_count(key, part):
    key = jax.random.fold_in(key, 37)
    base_key, heavy_key, pick_key = jax.random.split(key, 3)
    lowest = max(1, MAXT // 8)
    highest = max(lowest + 1, MAXT // 4 + 1)
    base = jax.random.randint(base_key, (N_ROW, N_COL), lowest, highest, dtype=jnp.int32)
    heavy = jax.random.randint(heavy_key, (N_ROW, N_COL), 0, 8, dtype=jnp.int32) == 0
    chosen = jax.random.randint(pick_key, (), 0, N_ROW * N_COL, dtype=jnp.int32)
    flat_index = jnp.arange(N_ROW * N_COL, dtype=jnp.int32).reshape(N_ROW, N_COL)
    heavy = heavy | (flat_index == chosen)
    return jnp.where(heavy, jnp.int32(MAXT), base)


def level_of(own_key, dims, cuts, least, top_value):
    factor_of = 1.0
    for axis_at, shards_of in cuts:
        heights = jax.random.uniform(jax.random.fold_in(jax.random.fold_in(own_key, 6), axis_at), (shards_of,), jnp.float32, least / len(cuts), top_value / len(cuts))
        factor_of = factor_of * jnp.repeat(jnp.exp(heights), dims[axis_at] // shards_of).reshape((-1,) + (1,) * (len(dims) - 1 - axis_at))
    return factor_of


def gaussian(rng, extent, spread, reach, pieces=(), held_as=jnp.bfloat16):
    loudness = level_of(rng, extent, pieces, -0.22, 0.18) if pieces else 1.0
    result = jax.random.normal(rng, extent, jnp.float32) * spread * loudness
    return jnp.minimum(jnp.maximum(result, -reach), reach).astype(held_as)


def setup_inputs(seed: int = 0) -> dict:
    key_of = jax.random.split(jax.random.key(seed), 9)
    return {
        "features": gaussian(key_of[0], (NODES, FIN), 1.0, 6.0, ((0, 64),)),
        "weight": gaussian(key_of[1], (FIN, HID), FIN ** -0.5, 0.5, ((1, 2),)),
        "hidden_bias": gaussian(key_of[2], (HID,), 1.0, 4.0, ((0, 2),), jnp.float32),
        "adjacency_tiles": gaussian(key_of[3], (N_ROW, N_COL, MAXT, TILE, TILE), (TILE * MAXT // (3 * RB)) ** -0.5, 0.078125, ((0, 8), (1, 8))),
        "tile_rows": draw_tile_rows(jax.random.fold_in(key_of[8], 71), 0),
        "tile_columns": draw_tile_columns(jax.random.fold_in(key_of[8], 71), 0),
        "tile_count": draw_tile_count(jax.random.fold_in(key_of[8], 71), 0),
        "cotangent": gaussian(key_of[7], (NODES, HID), 1.0, 6.0, ((0, 64), (1, 2))),
    }


def silu_slope(values):
    sigma = jax.nn.sigmoid(values)
    return sigma * (1.0 + values * (1.0 - sigma))


def rounded(values):
    return lax.optimization_barrier(values.astype(jnp.bfloat16)).astype(jnp.float32)


def block_terms(tile_block, take_rows, put_rows, count, source, out_blocks, flipped):
    picked = source[take_rows].astype(jnp.float32)
    dense = tile_block.astype(jnp.float32)
    if flipped:
        products = jnp.einsum('tab,taw->tbw', dense, picked)
    else:
        products = jnp.einsum('tab,tbw->taw', dense, picked)
    in_range = jnp.arange(take_rows.shape[0], dtype=jnp.int32) < count
    onehot = ((put_rows[None, :] == jnp.arange(out_blocks, dtype=jnp.int32)[:, None]) & in_range[None, :]).astype(jnp.float32)
    return jnp.einsum('nt,taw->naw', onehot, products, precision=lax.Precision.HIGHEST)


def reference(features, weight, hidden_bias, adjacency_tiles, tile_rows, tile_columns, tile_count, cotangent):
    projected = jnp.dot(features, weight, preferred_element_type=jnp.float32).astype(jnp.bfloat16)
    panel_blocks = RB * N_ROW
    range_blocks = RB * N_COL
    panels = projected.reshape(N_COL, panel_blocks, TILE, HID)

    def forward_row(row_index):
        def add_column(running, col_index):
            partial_term = block_terms(adjacency_tiles[row_index, col_index], tile_columns[row_index, col_index], tile_rows[row_index, col_index], tile_count[row_index, col_index], panels[col_index], range_blocks, False)
            return running + rounded(partial_term), None
        running, unused = lax.scan(add_column, jnp.zeros((range_blocks, TILE, HID), jnp.float32), jnp.arange(N_COL, dtype=jnp.int32))
        return running

    row_sums = lax.map(forward_row, jnp.arange(N_ROW, dtype=jnp.int32))
    preact = row_sums.reshape(NODES, HID) + hidden_bias
    activations = jax.nn.silu(preact).astype(jnp.bfloat16)
    grad_pre = (cotangent.astype(jnp.float32) * silu_slope(preact)).astype(jnp.bfloat16)
    grad_blocks = grad_pre.reshape(N_ROW, range_blocks, TILE, HID)

    def backward_column(col_index):
        def add_row(running, row_index):
            partial_term = block_terms(adjacency_tiles[row_index, col_index], tile_rows[row_index, col_index], tile_columns[row_index, col_index], tile_count[row_index, col_index], grad_blocks[row_index], panel_blocks, True)
            return running + rounded(partial_term), None
        running, unused = lax.scan(add_row, jnp.zeros((panel_blocks, TILE, HID), jnp.float32), jnp.arange(N_ROW, dtype=jnp.int32))
        return running

    column_sums = lax.map(backward_column, jnp.arange(N_COL, dtype=jnp.int32))
    grad_projected = column_sums.reshape(NODES, HID).astype(jnp.bfloat16)
    grad_weight = jnp.dot(features.T, grad_projected, preferred_element_type=jnp.float32)
    grad_bias = jnp.sum(grad_pre.astype(jnp.float32), axis=0)
    grad_features = jnp.dot(grad_projected, weight.T, preferred_element_type=jnp.float32)
    return (activations, grad_features, grad_weight, grad_bias)
```

```python
import functools

import jax
import jax.numpy as jnp
from jax import lax
from jax.experimental import pallas as pl
from jax.experimental.pallas import tpu as pltpu
from jax.sharding import PartitionSpec as P

F32 = jnp.float32
BF16 = jnp.bfloat16
TILE = 128
GROUP = 8
AHEAD = 8
SLOTS = AHEAD + 1
VMEM = pl.BlockSpec(memory_space=pltpu.VMEM)
SMEM = pl.BlockSpec(memory_space=pltpu.SMEM)
ANY = pl.BlockSpec(memory_space=pl.ANY)
PARAMS = pltpu.CompilerParams(vmem_limit_bytes=24 * 1024 * 1024)


def swap(values, axis, mask):
    size = lax.axis_size(axis)
    return lax.ppermute(values, axis, [(i, i ^ mask) for i in range(size)])


def exchange(parts, axis):
    return lax.all_to_all(parts, axis, 0, 0)


def pick_kernel(n_out, n_back, meta, rows, columns, forward, backward, groups):
    half = meta[1]

    def step(t, n):
        column = columns[t]
        row = rows[t]
        place = (column >> 2) * 2 + (column & 1)
        forward[n] = t + place * 1024 + row * 65536
        backward[n] = t + row * 1024 + place * 65536
        return n + ((column >> 1) & 1 == half).astype(jnp.int32)

    n = lax.fori_loop(0, meta[0], step, jnp.int32(0))
    for j in range(GROUP):
        forward[n + j] = n_out * 65536
        backward[n + j] = n_back * 65536
    groups[0] = (n + GROUP - 1) // GROUP


def pick(meta, rows, columns, n_out, n_back):
    length = rows.shape[0] + GROUP
    return pl.pallas_call(
        functools.partial(pick_kernel, n_out, n_back),
        out_shape=[
            jax.ShapeDtypeStruct((length,), jnp.int32),
            jax.ShapeDtypeStruct((length,), jnp.int32),
            jax.ShapeDtypeStruct((1,), jnp.int32),
        ],
        in_specs=[SMEM] * 3,
        out_specs=[SMEM] * 3,
        name="pick_tiles",
    )(meta, rows, columns)


def tiles_kernel(flipped, n_out, groups, picked, tiles, source, out, held, total, arrived):
    count = groups[0]

    def fetch(g):
        slot = lax.rem(g, SLOTS)
        for j in range(GROUP):
            t = picked[g * GROUP + j] & 1023
            pltpu.make_async_copy(tiles.at[t], held.at[slot * GROUP + j], arrived.at[slot]).start()

    def first(g, carry):
        fetch(g)
        return carry

    lax.fori_loop(0, jnp.minimum(count, AHEAD), first, 0)
    total[...] = jnp.zeros_like(total)

    def step(g, carry):
        @pl.when(g + AHEAD < count)
        def _():
            fetch(g + AHEAD)

        slot = lax.rem(g, SLOTS)
        block = held.at[pl.ds(slot * GROUP, GROUP)]
        pltpu.make_async_copy(tiles.at[pl.ds(0, GROUP)], block, arrived.at[slot]).wait()
        places = []
        products = []
        for j in range(GROUP):
            code = picked[g * GROUP + j]
            places.append(code >> 16)
            tile = held[slot * GROUP + j]
            other = source[(code >> 10) & 63]
            pair = (other, tile) if flipped else (tile, other)
            products.append(jnp.dot(*pair, preferred_element_type=F32))
        for place, product in zip(places, products):
            total[place] += product
        return carry

    lax.fori_loop(0, count, step, 0)
    out[...] = total[:n_out].astype(BF16)


def tile_sums(groups, picked, tiles, source, n_out, flipped):
    return pl.pallas_call(
        functools.partial(tiles_kernel, flipped, n_out),
        out_shape=jax.ShapeDtypeStruct((n_out, TILE, TILE), BF16),
        in_specs=[SMEM, SMEM, ANY, VMEM],
        out_specs=VMEM,
        scratch_shapes=[
            pltpu.VMEM((SLOTS * GROUP, TILE, TILE), BF16),
            pltpu.VMEM((n_out + 1, TILE, TILE), F32),
            pltpu.SemaphoreType.DMA((SLOTS,)),
        ],
        compiler_params=PARAMS,
        cost_estimate=pl.CostEstimate(
            flops=320 * 2 * TILE**3, bytes_accessed=320 * 2 * TILE**2, transcendentals=0
        ),
        name="tiles_backward" if flipped else "tiles_forward",
    )(groups, picked, tiles, source)


def gather_sum_kernel(parts, total, sent):
    value = jnp.sum(parts[...].astype(F32), axis=0)
    total[...] = value
    sent[...] = value.astype(BF16)


def gather_sum(parts):
    shape = parts.shape[1:]
    return pl.pallas_call(
        gather_sum_kernel,
        out_shape=[jax.ShapeDtypeStruct(shape, F32), jax.ShapeDtypeStruct(shape, BF16)],
        in_specs=[VMEM],
        out_specs=[VMEM] * 2,
        compiler_params=PARAMS,
        name="sum_parts",
    )(parts)


def middle_kernel(own, other, weight, bias, cotangent, activations, back_source, grad_weight, grad_bias):
    sums = (own[...] + other[...].astype(F32)).astype(BF16)
    preact = jnp.dot(sums, weight[...], preferred_element_type=F32) + bias[...]
    sigma = jax.nn.sigmoid(preact)
    activations[...] = (preact * sigma).astype(BF16)
    grad = cotangent[...].astype(F32) * (sigma * (1.0 + preact * (1.0 - sigma)))
    grad_pre = grad.astype(BF16)
    grad_bias[...] = jnp.sum(grad_pre.astype(F32), axis=0, keepdims=True)
    grad_weight[...] = lax.dot_general(
        sums, grad_pre, (((0,), (0,)), ((), ())), preferred_element_type=F32
    )
    for b in range(back_source.shape[0]):
        back_source[b] = lax.dot_general(
            weight[...],
            grad_pre[b * TILE : (b + 1) * TILE],
            (((1,), (1,)), ((), ())),
            preferred_element_type=F32,
        )


def middle(own, other, weight, bias, cotangent):
    rows, width = cotangent.shape
    return pl.pallas_call(
        middle_kernel,
        out_shape=[
            jax.ShapeDtypeStruct((rows, width), BF16),
            jax.ShapeDtypeStruct((rows // TILE, weight.shape[0], TILE), F32),
            jax.ShapeDtypeStruct(weight.shape, F32),
            jax.ShapeDtypeStruct((1, width), F32),
        ],
        in_specs=[VMEM] * 5,
        out_specs=[VMEM] * 4,
        compiler_params=PARAMS,
        name="middle",
    )(own, other, weight, bias, cotangent)


def final_kernel(parts, total, sent):
    for b in range(parts.shape[1]):
        value = jnp.sum(parts[:, b].astype(F32), axis=0).T
        total[b] = value
        sent[b] = value.astype(BF16)


def final_sum(parts):
    shape = parts.shape[1:]
    return pl.pallas_call(
        final_kernel,
        out_shape=[jax.ShapeDtypeStruct(shape, F32), jax.ShapeDtypeStruct(shape, BF16)],
        in_specs=[VMEM],
        out_specs=[VMEM] * 2,
        compiler_params=PARAMS,
        name="final_sum",
    )(parts)


def local(
    features, weight, hidden_bias, adjacency_tiles, tile_rows, tile_columns, tile_count, cotangent
):
    tiles = adjacency_tiles[0, 0]
    n_row, n_col = lax.axis_size("row"), lax.axis_size("col")
    half = lax.axis_index("feat")
    own_rows, fin = features.shape
    blocks = own_rows // TILE
    n_out, n_back = blocks * n_col, blocks // 2 * n_row
    meta = jnp.stack([tile_count[0, 0], half.astype(jnp.int32)])
    forward, backward, groups = pick(meta, tile_rows[0, 0], tile_columns[0, 0], n_out, n_back)

    mine = lax.dynamic_slice_in_dim(features, half * (own_rows // 2), own_rows // 2, 0)
    panel = exchange(jnp.broadcast_to(mine[None], (n_row,) + mine.shape), "row")
    panel = panel.reshape(n_back, TILE, fin)
    partial_sums = tile_sums(groups, forward, tiles, panel, n_out, False)
    parts = exchange(partial_sums.reshape(n_col, own_rows, fin), "col")
    own, sent = gather_sum(parts)
    other = swap(sent, "feat", 1)
    activations, back_own, local_weight, local_bias = middle(
        own, other, weight, hidden_bias[None], cotangent
    )
    back_source = (back_own + swap(back_own.astype(BF16), "feat", 1).astype(F32)).astype(BF16)
    back_range = lax.all_gather(back_source, "col", axis=0, tiled=False)
    back_range = back_range.reshape(n_out, fin, TILE)

    grads = jnp.concatenate([local_weight, jnp.broadcast_to(local_bias, (8, local_bias.shape[1]))], 0)
    for axis in ("col", "row"):
        for mask in (1, 2, 4):
            grads = grads + swap(grads, axis, mask)

    back = tile_sums(groups, backward, tiles, back_range, n_back, True)
    back_parts = exchange(back.reshape(n_row, blocks // 2, fin, TILE), "row")
    own_grad, sent_grad = final_sum(back_parts)
    other_grad = swap(sent_grad, "feat", 1).astype(F32)
    own_grad = own_grad.reshape(own_rows // 2, fin)
    other_grad = other_grad.reshape(own_rows // 2, fin)
    grad_features = jnp.where(
        half == 0,
        jnp.concatenate([own_grad, other_grad], 0),
        jnp.concatenate([other_grad, own_grad], 0),
    )
    return (activations, grad_features, grads[:fin], grads[fin])


def solution(mesh):
    placed = (
        P(("col", "row"), None),
        P(None, "feat"),
        P("feat"),
        P("row", "col", None, None, None),
        P("row", "col", None),
        P("row", "col", None),
        P("row", "col"),
        P(("row", "col"), "feat"),
    )
    return jax.shard_map(
        local,
        mesh=mesh,
        in_specs=placed,
        out_specs=(P(("row", "col"), "feat"), P(("col", "row"), None), P(None, "feat"), P("feat")),
        check_vma=False,
    )
```

```python
import functools

import jax
import jax.numpy as jnp
from jax import lax
from jax.experimental import pallas as pl
from jax.experimental.pallas import tpu as pltpu
from jax.sharding import PartitionSpec as P

F32 = jnp.float32
BF16 = jnp.bfloat16
TILE = 128
QUAD = 4
STEP = 8
PER = QUAD * STEP
VMEM = pl.BlockSpec(memory_space=pltpu.VMEM)
SMEM = pl.BlockSpec(memory_space=pltpu.SMEM)
ANY = pl.BlockSpec(memory_space=pl.ANY)
PARAMS = pltpu.CompilerParams(vmem_limit_bytes=8 * 1024 * 1024)
PICK_PARAMS = pltpu.CompilerParams(vmem_limit_bytes=16 * 1024 * 1024)


def swap(values, axis, mask):
    size = lax.axis_size(axis)
    return lax.ppermute(values, axis, [(i, i ^ mask) for i in range(size)])


def near(values):
    return pltpu.with_memory_space_constraint(values, pltpu.VMEM)


def iota(shape, dim):
    return lax.broadcasted_iota(jnp.int32, shape, dim)


def order(key, used, source, item, n_keys, length):
    n = key.shape[1]
    hit = ((iota((n_keys, n), 0) == key) & used).astype(F32)
    upto = (iota((n, n), 0) <= iota((n, n), 1)).astype(BF16)
    rank = jnp.dot(hit.astype(BF16), upto, preferred_element_type=F32)
    quads = jnp.floor((rank[:, n - 1 :] + (QUAD - 1)) * (1.0 / QUAD))
    below = (iota((n_keys, n_keys), 0) >= iota((n_keys, n_keys), 1)).astype(BF16)
    wide = jnp.broadcast_to(quads, (n_keys, TILE)).astype(BF16)
    end = jnp.dot(below, wide, preferred_element_type=F32)[:, :1]
    first = (end - quads) * QUAD
    slot = jnp.sum(hit * (first + rank - 1.0), axis=0, keepdims=True)
    slot = jnp.where(used, slot.astype(jnp.int32), -1)
    at = (iota((length, n), 0) == slot).astype(F32).astype(BF16)
    line = iota((8, n), 0)
    values = jnp.where(line == 2, source, 1)
    values = jnp.where(line == 0, item & 255, jnp.where(line == 1, item >> 8, values))
    found = lax.dot_general(
        values.astype(F32).astype(BF16), at, (((1,), (1,)), ((), ())), preferred_element_type=F32
    ).astype(jnp.int32)
    passed = (end * QUAD).astype(jnp.int32) <= iota((n_keys, length), 1)
    target = jnp.sum(passed.astype(F32), axis=0, keepdims=True).astype(jnp.int32)
    items = jnp.where(found[3:4] > 0, found[0:1] + found[1:2] * 256, -1)
    steps = (jnp.max(end).astype(jnp.int32) + STEP - 1) // STEP
    return items, found[2:3], target, steps, slot


def pick_kernel(n_out, n_back, count, ids, rows, columns, fetched, forward, backward, steps):
    row, column = rows[0], columns[0]
    index = iota(row.shape, 1)
    length = forward.shape[1]
    used = (index < count[0, 0]) & (((column >> 1) & 1) == ids[0])
    place = (column >> 2) * 2 + (column & 1)
    owner = jnp.bitwise_xor(row >> 2, ids[1])
    items, source, target, steps[0], slot = order(row, used, place, index, n_out, length)
    fetched[...] = jnp.maximum(items, 0)
    here = jnp.where(items >= 0, iota(items.shape, 1), length)
    forward[...] = here + source * 1024 + target * 65536
    items, source, target, steps[1], slot = order(
        place, used, owner * 4 + (row & 3), slot, n_back, length
    )
    here = jnp.where(items >= 0, items, length)
    backward[...] = here + source * 1024 + target * 65536


def pick(count, ids, rows, columns, n_out, n_back):
    length = rows.shape[-1] + max(n_out, n_back) * (QUAD - 1) + PER
    length = -(-length // TILE) * TILE
    slots = jax.ShapeDtypeStruct((1, length), jnp.int32)
    return pl.pallas_call(
        functools.partial(pick_kernel, n_out, n_back),
        out_shape=[slots, slots, slots, jax.ShapeDtypeStruct((2,), jnp.int32)],
        in_specs=[SMEM, SMEM, VMEM, VMEM],
        out_specs=[VMEM, VMEM, VMEM, SMEM],
        compiler_params=PICK_PARAMS,
        name="pick_tiles",
    )(count, ids, rows, columns)


def stage_kernel(steps, fetched, tiles, held, arrived):
    held[held.shape[0] - 1] = jnp.zeros((TILE, TILE), BF16)

    def start(g, carry):
        for j in range(PER):
            source = tiles.at[fetched[0, g * PER + j]]
            pltpu.make_async_copy(source, held.at[g * PER + j], arrived.at[g]).start()
        return carry

    def finish(g, carry):
        block = held.at[pl.ds(g * PER, PER)]
        pltpu.make_async_copy(tiles.at[pl.ds(0, PER)], block, arrived.at[g]).wait()
        return carry

    lax.fori_loop(0, steps[0], start, 0)
    lax.fori_loop(0, steps[0], finish, 0)


def stage(steps, fetched, tiles):
    length = fetched.shape[1]
    return pl.pallas_call(
        stage_kernel,
        out_shape=pltpu.VMEM((length + 1, TILE, TILE), BF16),
        in_specs=[SMEM, SMEM, ANY],
        out_specs=VMEM,
        scratch_shapes=[pltpu.SemaphoreType.DMA((length // PER,))],
        compiler_params=PARAMS,
        name="stage_tiles",
    )(steps, fetched, pltpu.with_memory_space_constraint(tiles, pltpu.HBM))


def add_products(flipped, count, picked, held, source, total):
    total[...] = jnp.zeros_like(total)

    def step(g, carry):
        places = []
        products = []
        for q in range(STEP):
            codes = [picked[0, g * PER + q * QUAD + j] for j in range(QUAD)]
            places.append(codes[0] >> 16)
            mine = [held[code & 1023] for code in codes]
            other = [source[(code >> 10) & 63] for code in codes]
            left, right = (other, mine) if flipped else (mine, other)
            products.append(
                jnp.dot(
                    jnp.concatenate(left, 1),
                    jnp.concatenate(right, 0),
                    preferred_element_type=F32,
                )
            )
        for place, product in zip(places, products):
            total[place] += product
        return carry

    lax.fori_loop(0, count, step, 0)


def forward_kernel(steps, ids, picked, held, source, kept, sent, total):
    add_products(False, steps[0], picked, held, source, total)
    for k in range(kept.shape[0]):
        own = jnp.bitwise_xor(ids[1], 2 * k)
        kept[k] = total[pl.ds(own * 4, 4)]
        sent[k] = total[pl.ds(jnp.bitwise_xor(own, 1) * 4, 4)].astype(BF16)


def tiles_forward(steps, ids, picked, held, source, n_out):
    shape = (n_out // 8, 4, TILE, TILE)
    return pl.pallas_call(
        forward_kernel,
        out_shape=[pltpu.VMEM(shape, F32), pltpu.VMEM(shape, BF16)],
        in_specs=[SMEM, SMEM, SMEM, VMEM, VMEM],
        out_specs=[VMEM] * 2,
        scratch_shapes=[pltpu.VMEM((n_out + 1, TILE, TILE), F32)],
        compiler_params=PARAMS,
        name="tiles_forward",
    )(steps, ids, picked, near(held), near(source))


def backward_kernel(n_back, steps, picked, held, *refs):
    sources, (out, gathered, total) = refs[:-3], refs[-3:]
    for m, source in enumerate(sources):
        gathered[4 * m : 4 * m + 4] = source[...]
    add_products(True, steps[1], picked, held, gathered, total)
    out[...] = total[:n_back].astype(BF16)


def tiles_backward(steps, picked, held, sources, n_back):
    return pl.pallas_call(
        functools.partial(backward_kernel, n_back),
        out_shape=pltpu.VMEM((n_back, TILE, TILE), BF16),
        in_specs=[SMEM, SMEM] + [VMEM] * (1 + len(sources)),
        out_specs=VMEM,
        scratch_shapes=[
            pltpu.VMEM((4 * len(sources), TILE, TILE), BF16),
            pltpu.VMEM((n_back + 1, TILE, TILE), F32),
        ],
        compiler_params=PARAMS,
        name="tiles_backward",
    )(steps, picked, near(held), *[near(values) for values in sources])


def pair_kernel(kept, got, first, *others):
    first[...] = kept[0] + got[0].astype(F32)
    for k, other in enumerate(others):
        other[...] = (kept[k + 1] + got[k + 1].astype(F32)).astype(BF16)


def pair_sum(kept, got):
    shape = kept.shape[1:]
    n = kept.shape[0] - 1
    return pl.pallas_call(
        pair_kernel,
        out_shape=[pltpu.VMEM(shape, F32)] + [pltpu.VMEM(shape, BF16)] * n,
        in_specs=[VMEM] * 2,
        out_specs=[VMEM] * (n + 1),
        compiler_params=PARAMS,
        name="pair_sum",
    )(near(kept), near(got))


def own_kernel(first, a, b, c, total, sent):
    value = first[...] + a[...].astype(F32) + b[...].astype(F32) + c[...].astype(F32)
    total[...] = value
    sent[...] = value.astype(BF16)


def own_sum(first, others):
    return pl.pallas_call(
        own_kernel,
        out_shape=[pltpu.VMEM(first.shape, F32), pltpu.VMEM(first.shape, BF16)],
        in_specs=[VMEM] * 4,
        out_specs=[VMEM] * 2,
        compiler_params=PARAMS,
        name="own_sum",
    )(near(first), *[near(values) for values in others])


def middle_kernel(own, other, weight, bias, cotangent, activations, back, back_sent, grads):
    blocks = own.shape[0]
    rows = blocks * TILE
    sums = (own[...] + other[...].astype(F32)).astype(BF16).reshape(rows, TILE)
    preact = jnp.dot(sums, weight[...], preferred_element_type=F32) + bias[...]
    sigma = jax.nn.sigmoid(preact)
    activations[...] = (preact * sigma).astype(BF16)
    grad = cotangent[...].astype(F32) * (sigma * (1.0 + preact * (1.0 - sigma)))
    grad_pre = grad.astype(BF16)
    grads[0:TILE] = lax.dot_general(
        sums, grad_pre, (((0,), (0,)), ((), ())), preferred_element_type=F32
    )
    total = jnp.sum(grad_pre.astype(F32), axis=0, keepdims=True)
    grads[TILE : TILE + 8] = jnp.broadcast_to(total, (8, TILE))
    for b in range(blocks):
        value = lax.dot_general(
            weight[...],
            grad_pre[b * TILE : (b + 1) * TILE],
            (((1,), (1,)), ((), ())),
            preferred_element_type=F32,
        )
        back[b] = value
        back_sent[b] = value.astype(BF16)


def middle(own, other, weight, bias, cotangent):
    return pl.pallas_call(
        middle_kernel,
        out_shape=[
            jax.ShapeDtypeStruct(cotangent.shape, BF16),
            pltpu.VMEM(own.shape, F32),
            pltpu.VMEM(own.shape, BF16),
            pltpu.VMEM((TILE + 8, TILE), F32),
        ],
        in_specs=[VMEM] * 5,
        out_specs=[VMEM] * 4,
        compiler_params=PARAMS,
        name="middle",
    )(near(own), near(other), weight, bias, cotangent)


def last_kernel(parts, total, sent):
    for b in range(parts.shape[1]):
        value = jnp.sum(parts[:, b].astype(F32), axis=0).T
        total[b * TILE : (b + 1) * TILE] = value
        sent[b * TILE : (b + 1) * TILE] = value.astype(BF16)


def last_sum(parts):
    shape = (parts.shape[1] * TILE, TILE)
    return pl.pallas_call(
        last_kernel,
        out_shape=[pltpu.VMEM(shape, F32), pltpu.VMEM(shape, BF16)],
        in_specs=[VMEM],
        out_specs=[VMEM] * 2,
        compiler_params=PARAMS,
        name="last_sum",
    )(near(parts))


def finish_kernel(ids, own, other, grads, more, features, weight, bias):
    rows = own.shape[0]
    features[pl.ds(ids[0] * rows, rows)] = own[...]
    features[pl.ds((1 - ids[0]) * rows, rows)] = other[...].astype(F32)
    weight[...] = grads[0:TILE] + more[0:TILE]
    bias[...] = grads[TILE : TILE + 1] + more[TILE : TILE + 1]


def finish(ids, own, other, grads, more):
    return pl.pallas_call(
        finish_kernel,
        out_shape=[
            jax.ShapeDtypeStruct((2 * own.shape[0], TILE), F32),
            jax.ShapeDtypeStruct((TILE, TILE), F32),
            jax.ShapeDtypeStruct((1, TILE), F32),
        ],
        in_specs=[SMEM] + [VMEM] * 4,
        out_specs=[VMEM] * 3,
        compiler_params=PARAMS,
        name="finish",
    )(ids, near(own), near(other), near(grads), near(more))


def local(
    features, weight, hidden_bias, adjacency_tiles, tile_rows, tile_columns, tile_count, cotangent
):
    tiles = adjacency_tiles[0, 0]
    n_row, n_col = lax.axis_size("row"), lax.axis_size("col")
    own_rows, fin = features.shape
    blocks = own_rows // TILE
    n_out, n_back = blocks * n_col, blocks // 2 * n_row
    half = lax.axis_index("feat")
    ids = jnp.stack([half, lax.axis_index("col")]).astype(jnp.int32)

    mine = lax.dynamic_slice_in_dim(features, half * (own_rows // 2), own_rows // 2, 0)
    panel = lax.all_to_all(jnp.broadcast_to(mine[None], (n_row,) + mine.shape), "row", 0, 0)
    fetched, forward, backward, steps = pick(tile_count, ids, tile_rows, tile_columns, n_out, n_back)
    held = stage(steps, fetched, tiles)
    held, panel = lax.optimization_barrier((held, panel))

    kept, sent = tiles_forward(steps, ids, forward, held, panel.reshape(n_back, TILE, fin), n_out)
    first, *others = pair_sum(kept, swap(sent, "col", 1))
    others = [swap(other, "col", 2 * k + 2) for k, other in enumerate(others)]
    own, sent = own_sum(first, others)
    other = swap(sent, "feat", 1)
    activations, back, back_sent, grads = middle(own, other, weight, hidden_bias[None], cotangent)

    back_other, more = lax.optimization_barrier((swap(back_sent, "feat", 1), swap(grads, "row", 1)))
    source = (back + back_other.astype(F32)).astype(BF16)
    grads = grads + more
    far = [swap(source, "col", mask) for mask in (2, 6, 4)]
    beside = swap(source, "col", 1)
    *far, more = lax.optimization_barrier((*far, swap(grads, "row", 2)))
    grads = grads + more
    across = [swap(values, "col", 1) for values in far]
    *across, more = lax.optimization_barrier((*across, swap(grads, "row", 4)))
    grads = grads + more
    sources = [source, beside, far[0], across[0], far[2], across[2], far[1], across[1]]
    out = tiles_backward(steps, backward, held, sources, n_back)
    out, more = lax.optimization_barrier((out, swap(grads, "col", 1)))
    grads = grads + more
    parts = lax.all_to_all(out.reshape(n_row, blocks // 2, fin, TILE), "row", 0, 0)
    parts, more = lax.optimization_barrier((parts, swap(grads, "col", 2)))
    grads = grads + more
    own, sent = last_sum(parts)
    other, more = lax.optimization_barrier((swap(sent, "feat", 1), swap(grads, "col", 4)))
    grad_features, grad_weight, grad_bias = finish(ids, own, other, grads, more)
    return (activations, grad_features, grad_weight, grad_bias[0])


def solution(mesh):
    placed = (
        P(("col", "row"), None),
        P(None, "feat"),
        P("feat"),
        P("row", "col", None, None, None),
        P("row", "col", None),
        P("row", "col", None),
        P("row", "col"),
        P(("row", "col"), "feat"),
    )
    return jax.shard_map(
        local,
        mesh=mesh,
        in_specs=placed,
        out_specs=(P(("row", "col"), "feat"), P(("col", "row"), None), P(None, "feat"), P("feat")),
        check_vma=False,
    )
```

```python
import functools

import jax
import jax.numpy as jnp
from jax import lax
from jax.experimental import pallas as pl
from jax.experimental.pallas import tpu as pltpu
from jax.sharding import PartitionSpec as P

F32 = jnp.float32
BF16 = jnp.bfloat16
TILE = 128
QUAD = 4
STEP = 8
PER = QUAD * STEP
VMEM = pl.BlockSpec(memory_space=pltpu.VMEM)
SMEM = pl.BlockSpec(memory_space=pltpu.SMEM)
ANY = pl.BlockSpec(memory_space=pl.ANY)
PARAMS = pltpu.CompilerParams(vmem_limit_bytes=8 * 1024 * 1024)
PICK_PARAMS = pltpu.CompilerParams(vmem_limit_bytes=16 * 1024 * 1024)


def swap(values, axis, mask):
    size = lax.axis_size(axis)
    return lax.ppermute(values, axis, [(i, i ^ mask) for i in range(size)])


def near(values):
    return pltpu.with_memory_space_constraint(values, pltpu.VMEM)


def iota(shape, dim):
    return lax.broadcasted_iota(jnp.int32, shape, dim)


def order(key, used, source, item, n_keys, length):
    n = key.shape[1]
    hit = ((iota((n_keys, n), 0) == key) & used).astype(F32)
    upto = (iota((n, n), 0) <= iota((n, n), 1)).astype(BF16)
    rank = jnp.dot(hit.astype(BF16), upto, preferred_element_type=F32)
    quads = jnp.floor((rank[:, n - 1 :] + (QUAD - 1)) * (1.0 / QUAD))
    below = (iota((n_keys, n_keys), 0) >= iota((n_keys, n_keys), 1)).astype(BF16)
    wide = jnp.broadcast_to(quads, (n_keys, TILE)).astype(BF16)
    end = jnp.dot(below, wide, preferred_element_type=F32)[:, :1]
    first = (end - quads) * QUAD
    slot = jnp.sum(hit * (first + rank - 1.0), axis=0, keepdims=True)
    slot = jnp.where(used, slot.astype(jnp.int32), -1)
    at = (iota((length, n), 0) == slot).astype(F32).astype(BF16)
    line = iota((8, n), 0)
    values = jnp.where(line == 2, source, 1)
    values = jnp.where(line == 0, item & 255, jnp.where(line == 1, item >> 8, values))
    found = lax.dot_general(
        values.astype(F32).astype(BF16), at, (((1,), (1,)), ((), ())), preferred_element_type=F32
    ).astype(jnp.int32)
    passed = (end * QUAD).astype(jnp.int32) <= iota((n_keys, length), 1)
    target = jnp.sum(passed.astype(F32), axis=0, keepdims=True).astype(jnp.int32)
    items = jnp.where(found[3:4] > 0, found[0:1] + found[1:2] * 256, -1)
    steps = (jnp.max(end).astype(jnp.int32) + STEP - 1) // STEP
    return items, found[2:3], target, steps, slot


def pick_kernel(n_out, n_back, count, ids, rows, columns, fetched, forward, backward, steps):
    row, column = rows[0], columns[0]
    index = iota(row.shape, 1)
    length = forward.shape[1]
    used = (index < count[0, 0]) & (((column >> 1) & 1) == ids[0])
    place = (column >> 2) * 2 + (column & 1)
    near_place = jnp.bitwise_xor(column >> 2, ids[2]) * 2 + (column & 1)
    near_row = jnp.bitwise_xor(row >> 2, ids[1]) * 4 + (row & 3)
    items, source, target, steps[0], slot = order(row, used, near_place, index, n_out, length)
    fetched[...] = jnp.maximum(items, 0)
    here = jnp.where(items >= 0, iota(items.shape, 1), length)
    forward[...] = here + source * 1024 + target * 65536
    items, source, target, steps[1], slot = order(place, used, near_row, slot, n_back, length)
    here = jnp.where(items >= 0, items, length)
    backward[...] = here + source * 1024 + target * 65536


def pick(count, ids, rows, columns, n_out, n_back):
    length = rows.shape[-1] + max(n_out, n_back) * (QUAD - 1) + PER
    length = -(-length // TILE) * TILE
    slots = jax.ShapeDtypeStruct((1, length), jnp.int32)
    return pl.pallas_call(
        functools.partial(pick_kernel, n_out, n_back),
        out_shape=[slots, slots, slots, jax.ShapeDtypeStruct((2,), jnp.int32)],
        in_specs=[SMEM, SMEM, VMEM, VMEM],
        out_specs=[VMEM, VMEM, VMEM, SMEM],
        compiler_params=PICK_PARAMS,
        name="pick_tiles",
    )(count, ids, rows, columns)


def stage_kernel(steps, fetched, tiles, held, arrived):
    held[held.shape[0] - 1] = jnp.zeros((TILE, TILE), BF16)

    def start(g, carry):
        for j in range(PER):
            source = tiles.at[fetched[0, g * PER + j]]
            pltpu.make_async_copy(source, held.at[g * PER + j], arrived.at[g]).start()
        return carry

    def finish(g, carry):
        block = held.at[pl.ds(g * PER, PER)]
        pltpu.make_async_copy(tiles.at[pl.ds(0, PER)], block, arrived.at[g]).wait()
        return carry

    lax.fori_loop(0, steps[0], start, 0)
    lax.fori_loop(0, steps[0], finish, 0)


def stage(steps, fetched, tiles):
    length = fetched.shape[1]
    return pl.pallas_call(
        stage_kernel,
        out_shape=pltpu.VMEM((length + 1, TILE, TILE), BF16),
        in_specs=[SMEM, SMEM, ANY],
        out_specs=VMEM,
        scratch_shapes=[pltpu.SemaphoreType.DMA((length // PER,))],
        compiler_params=PARAMS,
        name="stage_tiles",
    )(steps, fetched, pltpu.with_memory_space_constraint(tiles, pltpu.HBM))


def add_products(flipped, count, picked, held, source, total):
    total[...] = jnp.zeros_like(total)

    def step(g, carry):
        places = []
        products = []
        for q in range(STEP):
            codes = [picked[0, g * PER + q * QUAD + j] for j in range(QUAD)]
            places.append(codes[0] >> 16)
            mine = [held[code & 1023] for code in codes]
            other = [source[(code >> 10) & 63] for code in codes]
            left, right = (other, mine) if flipped else (mine, other)
            products.append(
                jnp.dot(
                    jnp.concatenate(left, 1),
                    jnp.concatenate(right, 0),
                    preferred_element_type=F32,
                )
            )
        for place, product in zip(places, products):
            total[place] += product
        return carry

    lax.fori_loop(0, count, step, 0)


def forward_kernel(n_out, steps, ids, picked, held, *refs):
    sources, (kept, sent, gathered, total) = refs[:-4], refs[-4:]
    for m, source in enumerate(sources):
        gathered[2 * m : 2 * m + 2] = source[...].reshape(2, TILE, TILE)
    add_products(False, steps[0], picked, held, gathered, total)
    for k in range(kept.shape[0]):
        own = jnp.bitwise_xor(ids[1], 2 * k)
        kept[k] = total[pl.ds(own * 4, 4)]
        sent[k] = total[pl.ds(jnp.bitwise_xor(own, 1) * 4, 4)].astype(BF16)


def tiles_forward(steps, ids, picked, held, sources, n_out):
    shape = (n_out // 8, 4, TILE, TILE)
    return pl.pallas_call(
        functools.partial(forward_kernel, n_out),
        out_shape=[pltpu.VMEM(shape, F32), pltpu.VMEM(shape, BF16)],
        in_specs=[SMEM, SMEM, SMEM] + [VMEM] * (1 + len(sources)),
        out_specs=[VMEM] * 2,
        scratch_shapes=[
            pltpu.VMEM((2 * len(sources), TILE, TILE), BF16),
            pltpu.VMEM((n_out + 1, TILE, TILE), F32),
        ],
        compiler_params=PARAMS,
        name="tiles_forward",
    )(steps, ids, picked, near(held), *[near(values) for values in sources])


def backward_kernel(n_back, steps, picked, held, *refs):
    sources, (out, gathered, total) = refs[:-3], refs[-3:]
    for m, source in enumerate(sources):
        gathered[4 * m : 4 * m + 4] = source[0 : 4 * TILE].reshape(4, TILE, TILE)
    add_products(True, steps[1], picked, held, gathered, total)
    out[...] = total[:n_back].astype(BF16)


def tiles_backward(steps, picked, held, sources, n_back):
    return pl.pallas_call(
        functools.partial(backward_kernel, n_back),
        out_shape=pltpu.VMEM((n_back, TILE, TILE), BF16),
        in_specs=[SMEM, SMEM] + [VMEM] * (1 + len(sources)),
        out_specs=VMEM,
        scratch_shapes=[
            pltpu.VMEM((4 * len(sources), TILE, TILE), BF16),
            pltpu.VMEM((n_back + 1, TILE, TILE), F32),
        ],
        compiler_params=PARAMS,
        name="tiles_backward",
    )(steps, picked, near(held), *[near(values) for values in sources])


def pair_kernel(kept, got, first, *others):
    first[...] = kept[0] + got[0].astype(F32)
    for k, other in enumerate(others):
        other[...] = (kept[k + 1] + got[k + 1].astype(F32)).astype(BF16)


def pair_sum(kept, got):
    shape = kept.shape[1:]
    n = kept.shape[0] - 1
    return pl.pallas_call(
        pair_kernel,
        out_shape=[pltpu.VMEM(shape, F32)] + [pltpu.VMEM(shape, BF16)] * n,
        in_specs=[VMEM] * 2,
        out_specs=[VMEM] * (n + 1),
        compiler_params=PARAMS,
        name="pair_sum",
    )(near(kept), near(got))


def own_kernel(first, a, b, c, total, sent):
    value = first[...] + a[...].astype(F32) + b[...].astype(F32) + c[...].astype(F32)
    total[...] = value
    sent[...] = value.astype(BF16)


def own_sum(first, others):
    return pl.pallas_call(
        own_kernel,
        out_shape=[pltpu.VMEM(first.shape, F32), pltpu.VMEM(first.shape, BF16)],
        in_specs=[VMEM] * 4,
        out_specs=[VMEM] * 2,
        compiler_params=PARAMS,
        name="own_sum",
    )(near(first), *[near(values) for values in others])


def middle_kernel(own, other, weight, bias, cotangent, activations, back, back_sent, grads):
    blocks = own.shape[0]
    rows = blocks * TILE
    sums = (own[...] + other[...].astype(F32)).astype(BF16).reshape(rows, TILE)
    preact = jnp.dot(sums, weight[...], preferred_element_type=F32) + bias[...]
    sigma = jax.nn.sigmoid(preact)
    activations[...] = (preact * sigma).astype(BF16)
    grad = cotangent[...].astype(F32) * (sigma * (1.0 + preact * (1.0 - sigma)))
    grad_pre = grad.astype(BF16)
    grads[0:TILE] = lax.dot_general(
        sums, grad_pre, (((0,), (0,)), ((), ())), preferred_element_type=F32
    )
    total = jnp.sum(grad_pre.astype(F32), axis=0, keepdims=True)
    grads[TILE : TILE + 8] = jnp.broadcast_to(total, (8, TILE))
    for b in range(blocks):
        value = lax.dot_general(
            weight[...],
            grad_pre[b * TILE : (b + 1) * TILE],
            (((1,), (1,)), ((), ())),
            preferred_element_type=F32,
        )
        back[b] = value
        back_sent[b] = value.astype(BF16)


def middle(own, other, weight, bias, cotangent):
    return pl.pallas_call(
        middle_kernel,
        out_shape=[
            jax.ShapeDtypeStruct(cotangent.shape, BF16),
            pltpu.VMEM(own.shape, F32),
            pltpu.VMEM(own.shape, BF16),
            pltpu.VMEM((TILE + 8, TILE), F32),
        ],
        in_specs=[VMEM] * 5,
        out_specs=[VMEM] * 4,
        compiler_params=PARAMS,
        name="middle",
    )(near(own), near(other), weight, bias, cotangent)


def message_kernel(back, other, grads, message):
    blocks = back.shape[0]
    value = back[...] + other[...].astype(F32)
    message[0 : blocks * TILE] = value.astype(BF16).reshape(blocks * TILE, TILE)
    message[blocks * TILE : (blocks + 1) * TILE] = grads[0:TILE].astype(BF16)
    rest = jnp.concatenate([grads[TILE : TILE + 8]] * 2, 0)
    line = iota(rest.shape, 0)
    terms = jnp.zeros(rest.shape, F32)
    for k in range(3):
        term = rest.astype(BF16).astype(F32)
        terms = jnp.where(line == k, term, terms)
        rest = rest - term
    message[(blocks + 1) * TILE : (blocks + 1) * TILE + 16] = terms.astype(BF16)


def message(back, other, grads):
    rows = (back.shape[0] + 1) * TILE + 16
    return pl.pallas_call(
        message_kernel,
        out_shape=pltpu.VMEM((rows, TILE), BF16),
        in_specs=[VMEM] * 3,
        out_specs=VMEM,
        compiler_params=PARAMS,
        name="message",
    )(near(back), near(other), near(grads))


def grad_kernel(*refs):
    messages, grads = refs[:-1], refs[-1]
    last = messages[0].shape[0] - 16
    weight = jnp.zeros((TILE, TILE), F32)
    bias = jnp.zeros((16, TILE), F32)
    for one in messages:
        weight = weight + one[last - TILE : last].astype(F32)
        bias = bias + one[last : last + 16].astype(F32)
    grads[0:TILE] = weight
    grads[TILE : TILE + 8] = jnp.broadcast_to(jnp.sum(bias, axis=0, keepdims=True), (8, TILE))


def grad_sum(messages):
    return pl.pallas_call(
        grad_kernel,
        out_shape=pltpu.VMEM((TILE + 8, TILE), F32),
        in_specs=[VMEM] * len(messages),
        out_specs=VMEM,
        compiler_params=PARAMS,
        name="grad_sum",
    )(*[near(one) for one in messages])


def last_kernel(parts, total, sent):
    for b in range(parts.shape[1]):
        value = jnp.sum(parts[:, b].astype(F32), axis=0).T
        total[b * TILE : (b + 1) * TILE] = value
        sent[b * TILE : (b + 1) * TILE] = value.astype(BF16)


def last_sum(parts):
    shape = (parts.shape[1] * TILE, TILE)
    return pl.pallas_call(
        last_kernel,
        out_shape=[pltpu.VMEM(shape, F32), pltpu.VMEM(shape, BF16)],
        in_specs=[VMEM],
        out_specs=[VMEM] * 2,
        compiler_params=PARAMS,
        name="last_sum",
    )(near(parts))


def finish_kernel(ids, own, other, grads, more, features, weight, bias):
    rows = own.shape[0]
    features[pl.ds(ids[0] * rows, rows)] = own[...]
    features[pl.ds((1 - ids[0]) * rows, rows)] = other[...].astype(F32)
    weight[...] = grads[0:TILE] + more[0:TILE]
    bias[...] = grads[TILE : TILE + 1] + more[TILE : TILE + 1]


def finish(ids, own, other, grads, more):
    return pl.pallas_call(
        finish_kernel,
        out_shape=[
            jax.ShapeDtypeStruct((2 * own.shape[0], TILE), F32),
            jax.ShapeDtypeStruct((TILE, TILE), F32),
            jax.ShapeDtypeStruct((1, TILE), F32),
        ],
        in_specs=[SMEM] + [VMEM] * 4,
        out_specs=[VMEM] * 3,
        compiler_params=PARAMS,
        name="finish",
    )(ids, near(own), near(other), near(grads), near(more))


def local(
    features, weight, hidden_bias, adjacency_tiles, tile_rows, tile_columns, tile_count, cotangent
):
    tiles = adjacency_tiles[0, 0]
    n_row, n_col = lax.axis_size("row"), lax.axis_size("col")
    own_rows, fin = features.shape
    blocks = own_rows // TILE
    n_out, n_back = blocks * n_col, blocks // 2 * n_row
    half = lax.axis_index("feat")
    ids = jnp.stack([half, lax.axis_index("col"), lax.axis_index("row")]).astype(jnp.int32)

    mine = lax.dynamic_slice_in_dim(features, half * (own_rows // 2), own_rows // 2, 0)
    far = [swap(mine, "row", mask) for mask in (2, 6, 4)]
    beside = swap(mine, "row", 1)
    lists = pick(tile_count, ids, tile_rows, tile_columns, n_out, n_back)
    lists, far, beside = lax.optimization_barrier((lists, far, beside))
    fetched, forward, backward, steps = lists
    across = [swap(values, "row", 1) for values in far]
    held = stage(steps, fetched, tiles)
    held, across = lax.optimization_barrier((held, across))
    sources = [mine, beside, far[0], across[0], far[2], across[2], far[1], across[1]]

    kept, sent = tiles_forward(steps, ids, forward, held, sources, n_out)
    first, *others = pair_sum(kept, swap(sent, "col", 1))
    others = [swap(other, "col", 2 * k + 2) for k, other in enumerate(others)]
    own, sent = own_sum(first, others)
    other = swap(sent, "feat", 1)
    activations, back, back_sent, grads = middle(own, other, weight, hidden_bias[None], cotangent)

    mine = message(back, swap(back_sent, "feat", 1), grads)
    far = [swap(mine, "col", mask) for mask in (2, 6, 4)]
    beside = swap(mine, "col", 1)
    far = lax.optimization_barrier(far)
    across = [swap(values, "col", 1) for values in far]
    sources = [mine, beside, far[0], across[0], far[2], across[2], far[1], across[1]]
    grads = grad_sum(sources)
    more = swap(grads, "row", 1)
    out = tiles_backward(steps, backward, held, sources, n_back)
    out, more = lax.optimization_barrier((out, more))
    grads = grads + more
    parts = lax.all_to_all(out.reshape(n_row, blocks // 2, fin, TILE), "row", 0, 0)
    parts, more = lax.optimization_barrier((parts, swap(grads, "row", 2)))
    grads = grads + more
    own, sent = last_sum(parts)
    other, more = lax.optimization_barrier((swap(sent, "feat", 1), swap(grads, "row", 4)))
    grad_features, grad_weight, grad_bias = finish(ids, own, other, grads, more)
    return (activations, grad_features, grad_weight, grad_bias[0])


def solution(mesh):
    placed = (
        P(("col", "row"), None),
        P(None, "feat"),
        P("feat"),
        P("row", "col", None, None, None),
        P("row", "col", None),
        P("row", "col", None),
        P("row", "col"),
        P(("row", "col"), "feat"),
    )
    return jax.shard_map(
        local,
        mesh=mesh,
        in_specs=placed,
        out_specs=(P(("row", "col"), "feat"), P(("col", "row"), None), P(None, "feat"), P("feat")),
        check_vma=False,
    )
```

```python
import functools

import jax
import jax.numpy as jnp
from jax import lax
from jax.experimental import pallas as pl
from jax.experimental.pallas import tpu as pltpu
from jax.sharding import PartitionSpec as P

F32 = jnp.float32
BF16 = jnp.bfloat16
TILE = 128
PER = 32
FORWARD = 2
BACKWARD = 4
VMEM = pl.BlockSpec(memory_space=pltpu.VMEM)
SMEM = pl.BlockSpec(memory_space=pltpu.SMEM)
ANY = pl.BlockSpec(memory_space=pl.ANY)
PARAMS = pltpu.CompilerParams(vmem_limit_bytes=8 * 1024 * 1024)
PICK_PARAMS = pltpu.CompilerParams(vmem_limit_bytes=16 * 1024 * 1024)


def swap(values, axis, mask):
    size = lax.axis_size(axis)
    return lax.ppermute(values, axis, [(i, i ^ mask) for i in range(size)])


def near(values):
    return pltpu.with_memory_space_constraint(values, pltpu.VMEM)


def iota(shape, dim):
    return lax.broadcasted_iota(jnp.int32, shape, dim)


def order(key, used, source, item, n_keys, length, width):
    n = key.shape[1]
    hit = ((iota((n_keys, n), 0) == key) & used).astype(F32)
    upto = (iota((n, n), 0) <= iota((n, n), 1)).astype(BF16)
    rank = jnp.dot(hit.astype(BF16), upto, preferred_element_type=F32)
    groups = jnp.floor((rank[:, n - 1 :] + (width - 1)) * (1.0 / width))
    below = (iota((n_keys, n_keys), 0) >= iota((n_keys, n_keys), 1)).astype(BF16)
    high = jnp.floor(groups * (1.0 / 128))
    lane = iota((n_keys, TILE), 1)
    parts = jnp.where(lane == 0, groups - high * 128, jnp.where(lane == 1, high, 0.0))
    ends = jnp.dot(below, parts.astype(BF16), preferred_element_type=F32)
    end = ends[:, 0:1] + ends[:, 1:2] * 128
    first = (end - groups) * width
    slot = jnp.sum(hit * (first + rank - 1.0), axis=0, keepdims=True)
    slot = jnp.where(used, slot.astype(jnp.int32), -1)
    at = (iota((length, n), 0) == slot).astype(F32).astype(BF16)
    line = iota((8, n), 0)
    values = jnp.where(line == 2, source, 1)
    values = jnp.where(line == 0, item & 255, jnp.where(line == 1, item >> 8, values))
    found = lax.dot_general(
        values.astype(F32).astype(BF16), at, (((1,), (1,)), ((), ())), preferred_element_type=F32
    ).astype(jnp.int32)
    passed = (end * width).astype(jnp.int32) <= iota((n_keys, length), 1)
    target = jnp.sum(passed.astype(F32), axis=0, keepdims=True).astype(jnp.int32)
    items = jnp.where(found[3:4] > 0, found[0:1] + found[1:2] * 256, -1)
    steps = (jnp.max(end).astype(jnp.int32) * width + PER - 1) // PER
    return items, found[2:3], target, steps, slot


def pick_kernel(n_out, n_back, count, ids, rows, columns, fetched, forward, backward, steps):
    row, column = rows[0], columns[0]
    index = iota(row.shape, 1)
    length = forward.shape[1]
    used = (index < count[0, 0]) & (((column >> 1) & 1) == ids[0])
    place = (column >> 2) * 2 + (column & 1)
    near_place = jnp.bitwise_xor(column >> 2, ids[2]) * 2 + (column & 1)
    near_row = jnp.bitwise_xor(row >> 2, ids[1]) * 4 + (row & 3)
    items, source, target, steps[0], slot = order(
        row, used, near_place, index, n_out, length, FORWARD
    )
    fetched[...] = jnp.maximum(items, 0)
    here = jnp.where(items >= 0, iota(items.shape, 1), length)
    forward[...] = here + source * 1024 + target * 65536
    items, source, target, steps[1], slot = order(
        place, used, near_row, slot, n_back, length, BACKWARD
    )
    here = jnp.where(items >= 0, items, length)
    backward[...] = here + source * 1024 + target * 65536


def pick(count, ids, rows, columns, n_out, n_back):
    length = rows.shape[-1] + max(n_out * (FORWARD - 1), n_back * (BACKWARD - 1)) + PER
    length = -(-length // TILE) * TILE
    slots = jax.ShapeDtypeStruct((1, length), jnp.int32)
    return pl.pallas_call(
        functools.partial(pick_kernel, n_out, n_back),
        out_shape=[slots, slots, slots, jax.ShapeDtypeStruct((2,), jnp.int32)],
        in_specs=[SMEM, SMEM, VMEM, VMEM],
        out_specs=[VMEM, VMEM, VMEM, SMEM],
        compiler_params=PICK_PARAMS,
        name="pick_tiles",
    )(count, ids, rows, columns)


def add_products(flipped, g, picked, held, source, total):
    width = BACKWARD if flipped else FORWARD
    places = []
    products = []
    for at in range(0, PER, width):
        codes = [picked[0, g * PER + at + j] for j in range(width)]
        places.append(codes[0] >> 16)
        mine = [held[code & 1023] for code in codes]
        other = [source[(code >> 10) & 63] for code in codes]
        left, right = (other, mine) if flipped else (mine, other)
        products.append(
            jnp.dot(
                jnp.concatenate(left, 1), jnp.concatenate(right, 0), preferred_element_type=F32
            )
        )
    for place, product in zip(places, products):
        total[place] += product


def forward_kernel(steps, ids, fetched, picked, tiles, *refs):
    sources, (held, kept, sent, gathered, total, arrived) = refs[:-6], refs[-6:]
    count = steps[0]

    def start(g, carry):
        for j in range(PER):
            source = tiles.at[fetched[0, g * PER + j]]
            pltpu.make_async_copy(source, held.at[g * PER + j], arrived.at[g]).start()
        return carry

    lax.fori_loop(0, count, start, 0)
    held[held.shape[0] - 1] = jnp.zeros((TILE, TILE), BF16)
    total[...] = jnp.zeros_like(total)
    for m, source in enumerate(sources):
        gathered[2 * m : 2 * m + 2] = source[...].reshape(2, TILE, TILE)

    def step(g, carry):
        block = held.at[pl.ds(g * PER, PER)]
        pltpu.make_async_copy(tiles.at[pl.ds(0, PER)], block, arrived.at[g]).wait()
        add_products(False, g, picked, held, gathered, total)
        return carry

    lax.fori_loop(0, count, step, 0)
    for k in range(kept.shape[0]):
        own = jnp.bitwise_xor(ids[1], 2 * k)
        kept[k] = total[pl.ds(own * 4, 4)]
        sent[k] = total[pl.ds(jnp.bitwise_xor(own, 1) * 4, 4)].astype(BF16)


def tiles_forward(steps, ids, fetched, picked, tiles, sources, n_out):
    shape = (n_out // 8, 4, TILE, TILE)
    length = fetched.shape[1]
    return pl.pallas_call(
        forward_kernel,
        out_shape=[
            pltpu.VMEM((length + 1, TILE, TILE), BF16),
            pltpu.VMEM(shape, F32),
            pltpu.VMEM(shape, BF16),
        ],
        in_specs=[SMEM, SMEM, SMEM, SMEM, ANY] + [VMEM] * len(sources),
        out_specs=[VMEM] * 3,
        scratch_shapes=[
            pltpu.VMEM((2 * len(sources), TILE, TILE), BF16),
            pltpu.VMEM((n_out + 1, TILE, TILE), F32),
            pltpu.SemaphoreType.DMA((length // PER,)),
        ],
        compiler_params=PARAMS,
        name="tiles_forward",
    )(
        steps,
        ids,
        fetched,
        picked,
        pltpu.with_memory_space_constraint(tiles, pltpu.HBM),
        *[near(values) for values in sources],
    )


def backward_kernel(steps, ids, picked, held, *refs):
    sources, (kept, first, second, third, gathered, total) = refs[:-6], refs[-6:]
    total[...] = jnp.zeros_like(total)
    for m, source in enumerate(sources):
        gathered[4 * m : 4 * m + 4] = source[0 : 4 * TILE].reshape(4, TILE, TILE)

    def step(g, carry):
        add_products(True, g, picked, held, gathered, total)
        return carry

    lax.fori_loop(0, steps[1], step, 0)
    across = ids[2] >> 1
    kept[...] = total[pl.ds(across * 4, 4)]
    for k, out in enumerate((first, second, third)):
        out[...] = total[pl.ds(jnp.bitwise_xor(across, k + 1) * 4, 4)].astype(BF16)


def tiles_backward(steps, ids, picked, held, sources, n_back):
    shape = (n_back // 4, TILE, TILE)
    return pl.pallas_call(
        backward_kernel,
        out_shape=[pltpu.VMEM(shape, F32)] + [pltpu.VMEM(shape, BF16)] * 3,
        in_specs=[SMEM, SMEM, SMEM] + [VMEM] * (1 + len(sources)),
        out_specs=[VMEM] * 4,
        scratch_shapes=[
            pltpu.VMEM((4 * len(sources), TILE, TILE), BF16),
            pltpu.VMEM((n_back + 1, TILE, TILE), F32),
        ],
        compiler_params=PARAMS,
        name="tiles_backward",
    )(steps, ids, picked, near(held), *[near(values) for values in sources])


def pair_kernel(kept, got, first, *others):
    first[...] = kept[0] + got[0].astype(F32)
    for k, other in enumerate(others):
        other[...] = (kept[k + 1] + got[k + 1].astype(F32)).astype(BF16)


def pair_sum(kept, got):
    shape = kept.shape[1:]
    n = kept.shape[0] - 1
    return pl.pallas_call(
        pair_kernel,
        out_shape=[pltpu.VMEM(shape, F32)] + [pltpu.VMEM(shape, BF16)] * n,
        in_specs=[VMEM] * 2,
        out_specs=[VMEM] * (n + 1),
        compiler_params=PARAMS,
        name="pair_sum",
    )(near(kept), near(got))


def own_kernel(first, a, b, c, total, sent):
    value = first[...] + a[...].astype(F32) + b[...].astype(F32) + c[...].astype(F32)
    total[...] = value
    sent[...] = value.astype(BF16)


def own_sum(first, others):
    return pl.pallas_call(
        own_kernel,
        out_shape=[pltpu.VMEM(first.shape, F32), pltpu.VMEM(first.shape, BF16)],
        in_specs=[VMEM] * 4,
        out_specs=[VMEM] * 2,
        compiler_params=PARAMS,
        name="own_sum",
    )(near(first), *[near(values) for values in others])


def middle_kernel(own, other, weight, bias, cotangent, activations, back, back_sent, grads):
    blocks = own.shape[0]
    rows = blocks * TILE
    sums = (own[...] + other[...].astype(F32)).astype(BF16).reshape(rows, TILE)
    preact = jnp.dot(sums, weight[...], preferred_element_type=F32) + bias[...]
    sigma = jax.nn.sigmoid(preact)
    activations[...] = (preact * sigma).astype(BF16)
    grad = cotangent[...].astype(F32) * (sigma * (1.0 + preact * (1.0 - sigma)))
    grad_pre = grad.astype(BF16)
    grads[0:TILE] = lax.dot_general(
        sums, grad_pre, (((0,), (0,)), ((), ())), preferred_element_type=F32
    )
    total = jnp.sum(grad_pre.astype(F32), axis=0, keepdims=True)
    grads[TILE : TILE + 8] = jnp.broadcast_to(total, (8, TILE))
    for b in range(blocks):
        value = lax.dot_general(
            weight[...],
            grad_pre[b * TILE : (b + 1) * TILE],
            (((1,), (1,)), ((), ())),
            preferred_element_type=F32,
        )
        back[b] = value
        back_sent[b] = value.astype(BF16)


def middle(own, other, weight, bias, cotangent):
    return pl.pallas_call(
        middle_kernel,
        out_shape=[
            jax.ShapeDtypeStruct(cotangent.shape, BF16),
            pltpu.VMEM(own.shape, F32),
            pltpu.VMEM(own.shape, BF16),
            pltpu.VMEM((TILE + 8, TILE), F32),
        ],
        in_specs=[VMEM] * 5,
        out_specs=[VMEM] * 4,
        compiler_params=PARAMS,
        name="middle",
    )(near(own), near(other), weight, bias, cotangent)


def message_kernel(back, other, grads, message):
    blocks = back.shape[0]
    value = back[...] + other[...].astype(F32)
    message[0 : blocks * TILE] = value.astype(BF16).reshape(blocks * TILE, TILE)
    message[blocks * TILE : (blocks + 1) * TILE] = grads[0:TILE].astype(BF16)
    rest = jnp.concatenate([grads[TILE : TILE + 8]] * 2, 0)
    line = iota(rest.shape, 0)
    terms = jnp.zeros(rest.shape, F32)
    for k in range(3):
        term = rest.astype(BF16).astype(F32)
        terms = jnp.where(line == k, term, terms)
        rest = rest - term
    message[(blocks + 1) * TILE : (blocks + 1) * TILE + 16] = terms.astype(BF16)


def message(back, other, grads):
    rows = (back.shape[0] + 1) * TILE + 16
    return pl.pallas_call(
        message_kernel,
        out_shape=pltpu.VMEM((rows, TILE), BF16),
        in_specs=[VMEM] * 3,
        out_specs=VMEM,
        compiler_params=PARAMS,
        name="message",
    )(near(back), near(other), near(grads))


def grad_kernel(*refs):
    messages, grads = refs[:-1], refs[-1]
    last = messages[0].shape[0] - 16
    weight = jnp.zeros((TILE, TILE), F32)
    bias = jnp.zeros((16, TILE), F32)
    for one in messages:
        weight = weight + one[last - TILE : last].astype(F32)
        bias = bias + one[last : last + 16].astype(F32)
    grads[0:TILE] = weight
    grads[TILE : TILE + 8] = jnp.broadcast_to(jnp.sum(bias, axis=0, keepdims=True), (8, TILE))


def grad_sum(messages):
    return pl.pallas_call(
        grad_kernel,
        out_shape=pltpu.VMEM((TILE + 8, TILE), F32),
        in_specs=[VMEM] * len(messages),
        out_specs=VMEM,
        compiler_params=PARAMS,
        name="grad_sum",
    )(*[near(one) for one in messages])


def line_kernel(ids, kept, a, b, c, own, own_sent, other_sent):
    value = kept[...] + a[...].astype(F32) + b[...].astype(F32) + c[...].astype(F32)
    blocks = own.shape[0]
    side = ids[2] & 1
    for z in range(2):
        half = value[z * blocks : (z + 1) * blocks]

        @pl.when(side == z)
        def _():
            own[...] = half
            own_sent[...] = half.astype(BF16)

        @pl.when(side != z)
        def _():
            other_sent[...] = half.astype(BF16)


def line_sum(ids, kept, others):
    shape = (kept.shape[0] // 2, TILE, TILE)
    return pl.pallas_call(
        line_kernel,
        out_shape=[pltpu.VMEM(shape, F32), pltpu.VMEM(shape, BF16), pltpu.VMEM(shape, BF16)],
        in_specs=[SMEM] + [VMEM] * 4,
        out_specs=[VMEM] * 3,
        compiler_params=PARAMS,
        name="line_sum",
    )(ids, near(kept), *[near(values) for values in others])


def finish_kernel(ids, own, beside, far, corner, grads, more, features, weight, bias):
    blocks = own.shape[0]
    for b in range(blocks):
        mine = own[b] + beside[b].astype(F32)
        other = far[b].astype(F32) + corner[b].astype(F32)
        features[pl.ds((ids[0] * blocks + b) * TILE, TILE)] = mine.T
        features[pl.ds(((1 - ids[0]) * blocks + b) * TILE, TILE)] = other.T
    weight[...] = grads[0:TILE] + more[0:TILE]
    bias[...] = grads[TILE : TILE + 1] + more[TILE : TILE + 1]


def finish(ids, own, beside, far, corner, grads, more):
    return pl.pallas_call(
        finish_kernel,
        out_shape=[
            jax.ShapeDtypeStruct((2 * own.shape[0] * TILE, TILE), F32),
            jax.ShapeDtypeStruct((TILE, TILE), F32),
            jax.ShapeDtypeStruct((1, TILE), F32),
        ],
        in_specs=[SMEM] + [VMEM] * 6,
        out_specs=[VMEM] * 3,
        compiler_params=PARAMS,
        name="finish",
    )(ids, near(own), near(beside), near(far), near(corner), near(grads), near(more))


def local(
    features, weight, hidden_bias, adjacency_tiles, tile_rows, tile_columns, tile_count, cotangent
):
    tiles = adjacency_tiles[0, 0]
    n_row, n_col = lax.axis_size("row"), lax.axis_size("col")
    own_rows, fin = features.shape
    blocks = own_rows // TILE
    n_out, n_back = blocks * n_col, blocks // 2 * n_row
    half = lax.axis_index("feat")
    ids = jnp.stack([half, lax.axis_index("col"), lax.axis_index("row")]).astype(jnp.int32)

    mine = lax.dynamic_slice_in_dim(features, half * (own_rows // 2), own_rows // 2, 0)
    sources = [swap(mine, "row", mask) for mask in range(1, n_row)]
    lists = pick(tile_count, ids, tile_rows, tile_columns, n_out, n_back)
    lists, sources = lax.optimization_barrier((lists, sources))
    fetched, forward, backward, steps = lists

    held, kept, sent = tiles_forward(steps, ids, fetched, forward, tiles, [mine, *sources], n_out)
    first, *others = pair_sum(kept, swap(sent, "col", 1))
    others = [swap(other, "col", 2 * k + 2) for k, other in enumerate(others)]
    own, sent = own_sum(first, others)
    other = swap(sent, "feat", 1)
    activations, back, back_sent, grads = middle(own, other, weight, hidden_bias[None], cotangent)

    mine = message(back, swap(back_sent, "feat", 1), grads)
    far = [swap(mine, "col", mask) for mask in (2, 6, 4)]
    beside = swap(mine, "col", 1)
    far = lax.optimization_barrier(far)
    across = [swap(values, "col", 1) for values in far]
    sources = [mine, beside, far[0], across[0], far[2], across[2], far[1], across[1]]
    grads = grad_sum(sources)
    more = swap(grads, "row", 1)
    kept, *others = tiles_backward(steps, ids, backward, held, sources, n_back)
    others, more = lax.optimization_barrier((others, more))
    grads = grads + more

    others = [swap(other, "row", 2 * k + 2) for k, other in enumerate(others)]
    others, more = lax.optimization_barrier((others, swap(grads, "row", 2)))
    grads = grads + more
    own, own_sent, other_sent = line_sum(ids, kept, others)
    far = swap(own_sent, "feat", 1)
    corner = swap(other_sent, ("row", "feat"), 3)
    beside = swap(other_sent, "row", 1)
    far, corner, beside, more = lax.optimization_barrier(
        (far, corner, beside, swap(grads, "row", 4))
    )
    grad_features, grad_weight, grad_bias = finish(ids, own, beside, far, corner, grads, more)
    return (activations, grad_features, grad_weight, grad_bias[0])


def solution(mesh):
    placed = (
        P(("col", "row"), None),
        P(None, "feat"),
        P("feat"),
        P("row", "col", None, None, None),
        P("row", "col", None),
        P("row", "col", None),
        P("row", "col"),
        P(("row", "col"), "feat"),
    )
    return jax.shard_map(
        local,
        mesh=mesh,
        in_specs=placed,
        out_specs=(P(("row", "col"), "feat"), P(("col", "row"), None), P(None, "feat"), P("feat")),
        check_vma=False,
    )
```

```python
import functools

import jax
import jax.numpy as jnp
from jax import lax
from jax.experimental import pallas as pl
from jax.experimental.pallas import tpu as pltpu
from jax.sharding import PartitionSpec as P

F32 = jnp.float32
BF16 = jnp.bfloat16
TILE = 128
PER = 32
FORWARD = 2
BACKWARD = 4
VMEM = pl.BlockSpec(memory_space=pltpu.VMEM)
SMEM = pl.BlockSpec(memory_space=pltpu.SMEM)
ANY = pl.BlockSpec(memory_space=pl.ANY)
PARAMS = pltpu.CompilerParams(vmem_limit_bytes=8 * 1024 * 1024)
PICK_PARAMS = pltpu.CompilerParams(vmem_limit_bytes=16 * 1024 * 1024)


def swap(values, axis, mask):
    size = lax.axis_size(axis)
    return lax.ppermute(values, axis, [(i, i ^ mask) for i in range(size)])


def near(values):
    return pltpu.with_memory_space_constraint(values, pltpu.VMEM)


def far(values):
    return pltpu.with_memory_space_constraint(values, pltpu.HBM)


def iota(shape, dim):
    return lax.broadcasted_iota(jnp.int32, shape, dim)


def order(key, used, source, item, n_keys, length, width):
    n = key.shape[1]
    hit = ((iota((n_keys, n), 0) == key) & used).astype(F32)
    upto = (iota((n, n), 0) <= iota((n, n), 1)).astype(BF16)
    rank = jnp.dot(hit.astype(BF16), upto, preferred_element_type=F32)
    groups = jnp.floor((rank[:, n - 1 :] + (width - 1)) * (1.0 / width))
    below = (iota((n_keys, n_keys), 0) >= iota((n_keys, n_keys), 1)).astype(BF16)
    high = jnp.floor(groups * (1.0 / 128))
    lane = iota((n_keys, TILE), 1)
    parts = jnp.where(lane == 0, groups - high * 128, jnp.where(lane == 1, high, 0.0))
    ends = jnp.dot(below, parts.astype(BF16), preferred_element_type=F32)
    end = ends[:, 0:1] + ends[:, 1:2] * 128
    first = (end - groups) * width
    slot = jnp.sum(hit * (first + rank - 1.0), axis=0, keepdims=True)
    slot = jnp.where(used, slot.astype(jnp.int32), -1)
    at = (iota((length, n), 0) == slot).astype(F32).astype(BF16)
    line = iota((8, n), 0)
    values = jnp.where(line == 2, source, 1)
    values = jnp.where(line == 0, item & 255, jnp.where(line == 1, item >> 8, values))
    found = lax.dot_general(
        values.astype(F32).astype(BF16), at, (((1,), (1,)), ((), ())), preferred_element_type=F32
    ).astype(jnp.int32)
    passed = (end * width).astype(jnp.int32) <= iota((n_keys, length), 1)
    target = jnp.sum(passed.astype(F32), axis=0, keepdims=True).astype(jnp.int32)
    items = jnp.where(found[3:4] > 0, found[0:1] + found[1:2] * 256, -1)
    steps = (jnp.max(end).astype(jnp.int32) * width + PER - 1) // PER
    return items, found[2:3], target, steps, slot


def pick_kernel(n_out, count, ids, rows, columns, fetched, forward, slots, steps, row_copy, column_copy, arrived):
    copies = [
        pltpu.make_async_copy(rows.at[0], row_copy, arrived.at[0]),
        pltpu.make_async_copy(columns.at[0], column_copy, arrived.at[1]),
    ]
    for copy in copies:
        copy.start()
    for copy in copies:
        copy.wait()
    row, column = row_copy[...], column_copy[...]
    index = iota(row.shape, 1)
    length = forward.shape[1]
    used = (index < count[0, 0]) & (((column >> 1) & 1) == ids[0])
    source = jnp.bitwise_xor(column >> 2, ids[2]) * 2 + (column & 1)
    items, source, target, steps[0], slot = order(row, used, source, index, n_out, length, FORWARD)
    fetched[...] = jnp.maximum(items, 0)
    here = jnp.where(items >= 0, iota(items.shape, 1), length)
    forward[...] = here + source * 1024 + target * 65536
    slots[...] = slot


def pick(count, ids, rows, columns, n_out, n_back):
    length = rows.shape[-1] + max(n_out * (FORWARD - 1), n_back * (BACKWARD - 1)) + PER
    length = -(-length // TILE) * TILE
    listed = jax.ShapeDtypeStruct((1, length), jnp.int32)
    return pl.pallas_call(
        functools.partial(pick_kernel, n_out),
        out_shape=[
            listed,
            listed,
            pltpu.VMEM(rows.shape[1:], jnp.int32),
            jax.ShapeDtypeStruct((1,), jnp.int32),
        ],
        in_specs=[SMEM, SMEM, ANY, ANY],
        out_specs=[VMEM, VMEM, VMEM, SMEM],
        scratch_shapes=[
            pltpu.VMEM(rows.shape[1:], jnp.int32),
            pltpu.VMEM(rows.shape[1:], jnp.int32),
            pltpu.SemaphoreType.DMA((2,)),
        ],
        compiler_params=PICK_PARAMS,
        name="pick_tiles",
    )(count, ids, far(rows), far(columns))


def prepare_kernel(
    n_back, ids, rows, columns, slots, weight, bias, cotangent, *refs
):
    backward, steps, weight_copy, bias_copy, cotangent_copy, row_copy, column_copy, arrived = refs
    pairs = [
        (rows.at[0], row_copy),
        (columns.at[0], column_copy),
        (weight, weight_copy),
        (bias, bias_copy),
        (cotangent, cotangent_copy),
    ]
    copies = [
        pltpu.make_async_copy(source, target, arrived.at[k])
        for k, (source, target) in enumerate(pairs)
    ]
    for copy in copies:
        copy.start()
    for copy in copies:
        copy.wait()
    row, column, slot = row_copy[...], column_copy[...], slots[...]
    length = backward.shape[1]
    place = (column >> 2) * 2 + (column & 1)
    source = jnp.bitwise_xor(row >> 2, ids[1]) * 4 + (row & 3)
    used = slot >= 0
    items, source, target, steps[0], slot = order(
        place, used, source, slot, n_back, length, BACKWARD
    )
    here = jnp.where(items >= 0, items, length)
    backward[...] = here + source * 1024 + target * 65536


def prepare(ids, rows, columns, slots, length, n_back, weight, bias, cotangent):
    return pl.pallas_call(
        functools.partial(prepare_kernel, n_back),
        out_shape=[
            jax.ShapeDtypeStruct((1, length), jnp.int32),
            jax.ShapeDtypeStruct((1,), jnp.int32),
            pltpu.VMEM(weight.shape, weight.dtype),
            pltpu.VMEM(bias.shape, bias.dtype),
            pltpu.VMEM(cotangent.shape, cotangent.dtype),
        ],
        in_specs=[SMEM, ANY, ANY, VMEM, ANY, ANY, ANY],
        out_specs=[VMEM, SMEM, VMEM, VMEM, VMEM],
        scratch_shapes=[
            pltpu.VMEM(rows.shape[1:], jnp.int32),
            pltpu.VMEM(rows.shape[1:], jnp.int32),
            pltpu.SemaphoreType.DMA((5,)),
        ],
        compiler_params=PICK_PARAMS,
        name="prepare",
    )(ids, far(rows), far(columns), near(slots), far(weight), far(bias), far(cotangent))


def join_kernel(a, b, out):
    rows = a.shape[0]
    out[0:rows] = a[...]
    out[rows : 2 * rows] = b[...]


def join(a, b):
    return pl.pallas_call(
        join_kernel,
        out_shape=pltpu.VMEM((2 * a.shape[0], a.shape[1]), a.dtype),
        in_specs=[VMEM] * 2,
        out_specs=VMEM,
        compiler_params=PARAMS,
        name="join",
    )(near(a), near(b))


def add_products(flipped, g, picked, held, source, total):
    width = BACKWARD if flipped else FORWARD
    places = []
    products = []
    for at in range(0, PER, width):
        codes = [picked[0, g * PER + at + j] for j in range(width)]
        places.append(codes[0] >> 16)
        mine = [held[code & 1023] for code in codes]
        other = [source[(code >> 10) & 63] for code in codes]
        left, right = (other, mine) if flipped else (mine, other)
        products.append(
            jnp.dot(
                jnp.concatenate(left, 1), jnp.concatenate(right, 0), preferred_element_type=F32
            )
        )
    for place, product in zip(places, products):
        total[place] += product


def forward_kernel(steps, ids, fetched, picked, tiles, *refs):
    sources, (held, kept, sent, gathered, total, arrived) = refs[:-6], refs[-6:]
    count = steps[0]

    def start(g, carry):
        for j in range(PER):
            source = tiles.at[fetched[0, g * PER + j]]
            pltpu.make_async_copy(source, held.at[g * PER + j], arrived.at[g]).start()
        return carry

    lax.fori_loop(0, count, start, 0)
    held[held.shape[0] - 1] = jnp.zeros((TILE, TILE), BF16)
    total[...] = jnp.zeros_like(total)
    for m, source in enumerate(sources):
        gathered[4 * m : 4 * m + 4] = source[...].reshape(4, TILE, TILE)

    def step(g, carry):
        block = held.at[pl.ds(g * PER, PER)]
        pltpu.make_async_copy(tiles.at[pl.ds(0, PER)], block, arrived.at[g]).wait()
        add_products(False, g, picked, held, gathered, total)
        return carry

    lax.fori_loop(0, count, step, 0)
    for k in range(kept.shape[0]):
        own = jnp.bitwise_xor(ids[1], 2 * k)
        kept[k] = total[pl.ds(own * 4, 4)]
        sent[k] = total[pl.ds(jnp.bitwise_xor(own, 1) * 4, 4)].astype(BF16)


def tiles_forward(steps, ids, fetched, picked, tiles, sources, n_out):
    shape = (n_out // 8, 4, TILE, TILE)
    length = fetched.shape[1]
    return pl.pallas_call(
        forward_kernel,
        out_shape=[
            pltpu.VMEM((length + 1, TILE, TILE), BF16),
            pltpu.VMEM(shape, F32),
            pltpu.VMEM(shape, BF16),
        ],
        in_specs=[SMEM, SMEM, SMEM, SMEM, ANY] + [VMEM] * len(sources),
        out_specs=[VMEM] * 3,
        scratch_shapes=[
            pltpu.VMEM((4 * len(sources), TILE, TILE), BF16),
            pltpu.VMEM((n_out + 1, TILE, TILE), F32),
            pltpu.SemaphoreType.DMA((length // PER,)),
        ],
        compiler_params=PARAMS,
        name="tiles_forward",
    )(
        steps,
        ids,
        fetched,
        picked,
        far(tiles),
        *[near(values) for values in sources],
    )


def backward_kernel(steps, ids, picked, held, *refs):
    sources, (kept, first, second, third, gathered, total) = refs[:-6], refs[-6:]
    total[...] = jnp.zeros_like(total)
    for m, source in enumerate(sources):
        gathered[4 * m : 4 * m + 4] = source[0 : 4 * TILE].reshape(4, TILE, TILE)

    def step(g, carry):
        add_products(True, g, picked, held, gathered, total)
        return carry

    lax.fori_loop(0, steps[0], step, 0)
    across = ids[2] >> 1
    kept[...] = total[pl.ds(across * 4, 4)]
    for k, out in enumerate((first, second, third)):
        out[...] = total[pl.ds(jnp.bitwise_xor(across, k + 1) * 4, 4)].astype(BF16)


def tiles_backward(steps, ids, picked, held, sources, n_back):
    shape = (n_back // 4, TILE, TILE)
    return pl.pallas_call(
        backward_kernel,
        out_shape=[pltpu.VMEM(shape, F32)] + [pltpu.VMEM(shape, BF16)] * 3,
        in_specs=[SMEM, SMEM, SMEM] + [VMEM] * (1 + len(sources)),
        out_specs=[VMEM] * 4,
        scratch_shapes=[
            pltpu.VMEM((4 * len(sources), TILE, TILE), BF16),
            pltpu.VMEM((n_back + 1, TILE, TILE), F32),
        ],
        compiler_params=PARAMS,
        name="tiles_backward",
    )(steps, ids, picked, near(held), *[near(values) for values in sources])


def pair_kernel(kept, got, first, *others):
    first[...] = kept[0] + got[0].astype(F32)
    for k, other in enumerate(others):
        other[...] = (kept[k + 1] + got[k + 1].astype(F32)).astype(BF16)


def pair_sum(kept, got):
    shape = kept.shape[1:]
    n = kept.shape[0] - 1
    return pl.pallas_call(
        pair_kernel,
        out_shape=[pltpu.VMEM(shape, F32)] + [pltpu.VMEM(shape, BF16)] * n,
        in_specs=[VMEM] * 2,
        out_specs=[VMEM] * (n + 1),
        compiler_params=PARAMS,
        name="pair_sum",
    )(near(kept), near(got))


def own_kernel(first, a, b, c, total, sent):
    value = first[...] + a[...].astype(F32) + b[...].astype(F32) + c[...].astype(F32)
    total[...] = value
    sent[...] = value.astype(BF16)


def own_sum(first, others):
    return pl.pallas_call(
        own_kernel,
        out_shape=[pltpu.VMEM(first.shape, F32), pltpu.VMEM(first.shape, BF16)],
        in_specs=[VMEM] * 4,
        out_specs=[VMEM] * 2,
        compiler_params=PARAMS,
        name="own_sum",
    )(near(first), *[near(values) for values in others])


def middle_kernel(own, other, weight, bias, cotangent, activations, back, back_sent, grads):
    blocks = own.shape[0]
    rows = blocks * TILE
    sums = (own[...] + other[...].astype(F32)).astype(BF16).reshape(rows, TILE)
    preact = jnp.dot(sums, weight[...], preferred_element_type=F32) + bias[...]
    sigma = jax.nn.sigmoid(preact)
    activations[...] = (preact * sigma).astype(BF16)
    grad = cotangent[...].astype(F32) * (sigma * (1.0 + preact * (1.0 - sigma)))
    grad_pre = grad.astype(BF16)
    grads[0:TILE] = lax.dot_general(
        sums, grad_pre, (((0,), (0,)), ((), ())), preferred_element_type=F32
    )
    total = jnp.sum(grad_pre.astype(F32), axis=0, keepdims=True)
    grads[TILE : TILE + 8] = jnp.broadcast_to(total, (8, TILE))
    for b in range(blocks):
        value = lax.dot_general(
            weight[...],
            grad_pre[b * TILE : (b + 1) * TILE],
            (((1,), (1,)), ((), ())),
            preferred_element_type=F32,
        )
        back[b] = value
        back_sent[b] = value.astype(BF16)


def middle(own, other, weight, bias, cotangent):
    return pl.pallas_call(
        middle_kernel,
        out_shape=[
            jax.ShapeDtypeStruct(cotangent.shape, BF16),
            pltpu.VMEM(own.shape, F32),
            pltpu.VMEM(own.shape, BF16),
            pltpu.VMEM((TILE + 8, TILE), F32),
        ],
        in_specs=[VMEM] * 5,
        out_specs=[VMEM] * 4,
        compiler_params=PARAMS,
        name="middle",
    )(near(own), near(other), near(weight), near(bias), near(cotangent))


def message_kernel(back, other, grads, message):
    blocks = back.shape[0]
    value = back[...] + other[...].astype(F32)
    message[0 : blocks * TILE] = value.astype(BF16).reshape(blocks * TILE, TILE)
    message[blocks * TILE : (blocks + 1) * TILE] = grads[0:TILE].astype(BF16)
    rest = jnp.concatenate([grads[TILE : TILE + 8]] * 2, 0)
    line = iota(rest.shape, 0)
    terms = jnp.zeros(rest.shape, F32)
    for k in range(3):
        term = rest.astype(BF16).astype(F32)
        terms = jnp.where(line == k, term, terms)
        rest = rest - term
    message[(blocks + 1) * TILE : (blocks + 1) * TILE + 16] = terms.astype(BF16)


def message(back, other, grads):
    rows = (back.shape[0] + 1) * TILE + 16
    return pl.pallas_call(
        message_kernel,
        out_shape=pltpu.VMEM((rows, TILE), BF16),
        in_specs=[VMEM] * 3,
        out_specs=VMEM,
        compiler_params=PARAMS,
        name="message",
    )(near(back), near(other), near(grads))


def grad_kernel(*refs):
    messages, grads = refs[:-1], refs[-1]
    last = messages[0].shape[0] - 16
    weight = jnp.zeros((TILE, TILE), F32)
    bias = jnp.zeros((16, TILE), F32)
    for one in messages:
        weight = weight + one[last - TILE : last].astype(F32)
        bias = bias + one[last : last + 16].astype(F32)
    grads[0:TILE] = weight
    grads[TILE : TILE + 8] = jnp.broadcast_to(jnp.sum(bias, axis=0, keepdims=True), (8, TILE))


def grad_sum(messages):
    return pl.pallas_call(
        grad_kernel,
        out_shape=pltpu.VMEM((TILE + 8, TILE), F32),
        in_specs=[VMEM] * len(messages),
        out_specs=VMEM,
        compiler_params=PARAMS,
        name="grad_sum",
    )(*[near(one) for one in messages])


def line_kernel(ids, kept, a, b, c, own, own_sent, other_sent):
    blocks = own.shape[0]
    side = ids[2] & 1

    def half(z):
        block = pl.ds(z * blocks, blocks)
        terms = [values[block].astype(F32) for values in (a, b, c)]
        return kept[block] + terms[0] + terms[1] + terms[2]

    mine = half(side)
    own[...] = mine
    own_sent[...] = mine.astype(BF16)
    other_sent[...] = half(1 - side).astype(BF16)


def line_sum(ids, kept, others):
    shape = (kept.shape[0] // 2, TILE, TILE)
    return pl.pallas_call(
        line_kernel,
        out_shape=[pltpu.VMEM(shape, F32), pltpu.VMEM(shape, BF16), pltpu.VMEM(shape, BF16)],
        in_specs=[SMEM] + [VMEM] * 4,
        out_specs=[VMEM] * 3,
        compiler_params=PARAMS,
        name="line_sum",
    )(ids, near(kept), *[near(values) for values in others])


def finish_kernel(ids, own, beside, opposite, corner, grads, more, features, weight, bias):
    blocks = own.shape[0]
    for b in range(blocks):
        mine = own[b] + beside[b].astype(F32)
        other = opposite[b].astype(F32) + corner[b].astype(F32)
        features[pl.ds((ids[0] * blocks + b) * TILE, TILE)] = mine.T
        features[pl.ds(((1 - ids[0]) * blocks + b) * TILE, TILE)] = other.T
    weight[...] = grads[0:TILE] + more[0:TILE]
    bias[...] = grads[TILE : TILE + 1] + more[TILE : TILE + 1]


def finish(ids, own, beside, opposite, corner, grads, more):
    return pl.pallas_call(
        finish_kernel,
        out_shape=[
            jax.ShapeDtypeStruct((2 * own.shape[0] * TILE, TILE), F32),
            jax.ShapeDtypeStruct((TILE, TILE), F32),
            jax.ShapeDtypeStruct((1, TILE), F32),
        ],
        in_specs=[SMEM] + [VMEM] * 6,
        out_specs=[VMEM] * 3,
        compiler_params=PARAMS,
        name="finish",
    )(ids, near(own), near(beside), near(opposite), near(corner), near(grads), near(more))


def local(
    features, weight, hidden_bias, adjacency_tiles, tile_rows, tile_columns, tile_count, cotangent
):
    tiles = adjacency_tiles[0, 0]
    n_row, n_col = lax.axis_size("row"), lax.axis_size("col")
    own_rows, fin = features.shape
    blocks = own_rows // TILE
    n_out, n_back = blocks * n_col, blocks // 2 * n_row
    half = lax.axis_index("feat")
    ids = jnp.stack([half, lax.axis_index("col"), lax.axis_index("row")]).astype(jnp.int32)

    mine = lax.dynamic_slice_in_dim(features, half * (own_rows // 2), own_rows // 2, 0)
    beside, ids = lax.optimization_barrier((swap(mine, "row", 1), ids))
    pair = join(mine, beside)
    sources = [swap(pair, "row", mask) for mask in range(2, n_row, 2)]
    lists = pick(tile_count, ids, tile_rows, tile_columns, n_out, n_back)
    lists, sources = lax.optimization_barrier((lists, sources))
    fetched, forward, slots, steps = lists

    held, kept, sent = tiles_forward(steps, ids, fetched, forward, tiles, [pair, *sources], n_out)
    first, *others = pair_sum(kept, swap(sent, "col", 1))
    others = [swap(other, "col", 2 * k + 2) for k, other in enumerate(others)]
    own, sent = own_sum(first, others)
    sent, slots = lax.optimization_barrier((sent, slots))
    ready = prepare(
        ids, tile_rows, tile_columns, slots, forward.shape[1], n_back, weight, hidden_bias[None], cotangent
    )
    other, ready = lax.optimization_barrier((swap(sent, "feat", 1), ready))
    backward, steps, weight, bias, cotangent = ready
    activations, back, back_sent, grads = middle(own, other, weight, bias, cotangent)

    mine = message(back, swap(back_sent, "feat", 1), grads)
    across = [swap(mine, "col", mask) for mask in (2, 6, 4)]
    beside = swap(mine, "col", 1)
    across = lax.optimization_barrier(across)
    corners = [swap(values, "col", 1) for values in across]
    sources = [mine, beside, across[0], corners[0], across[2], corners[2], across[1], corners[1]]
    grads = grad_sum(sources)
    more = swap(grads, "row", 1)
    kept, *others = tiles_backward(steps, ids, backward, held, sources, n_back)
    others, more = lax.optimization_barrier((others, more))
    grads = grads + more

    others = [swap(other, "row", 2 * k + 2) for k, other in enumerate(others)]
    others, more = lax.optimization_barrier((others, swap(grads, "row", 2)))
    grads = grads + more
    own, own_sent, other_sent = line_sum(ids, kept, others)
    opposite = swap(own_sent, "feat", 1)
    corner = swap(other_sent, ("row", "feat"), 3)
    beside = swap(other_sent, "row", 1)
    opposite, corner, beside, more = lax.optimization_barrier(
        (opposite, corner, beside, swap(grads, "row", 4))
    )
    grad_features, grad_weight, grad_bias = finish(ids, own, beside, opposite, corner, grads, more)
    return (activations, grad_features, grad_weight, grad_bias[0])


def solution(mesh):
    placed = (
        P(("col", "row"), None),
        P(None, "feat"),
        P("feat"),
        P("row", "col", None, None, None),
        P("row", "col", None),
        P("row", "col", None),
        P("row", "col"),
        P(("row", "col"), "feat"),
    )
    return jax.shard_map(
        local,
        mesh=mesh,
        in_specs=placed,
        out_specs=(P(("row", "col"), "feat"), P(("col", "row"), None), P(None, "feat"), P("feat")),
        check_vma=False,
    )
```

```python
import functools

import jax
import jax.numpy as jnp
from jax import lax
from jax.experimental import pallas as pl
from jax.experimental.pallas import tpu as pltpu
from jax.sharding import PartitionSpec as P

F32 = jnp.float32
BF16 = jnp.bfloat16
TILE = 128
PER = 32
FORWARD = 2
BACKWARD = 4
EARLY = 4
VMEM = pl.BlockSpec(memory_space=pltpu.VMEM)
SMEM = pl.BlockSpec(memory_space=pltpu.SMEM)
ANY = pl.BlockSpec(memory_space=pl.ANY)
PARAMS = pltpu.CompilerParams(vmem_limit_bytes=8 * 1024 * 1024)
PICK_PARAMS = pltpu.CompilerParams(vmem_limit_bytes=16 * 1024 * 1024)


def swap(values, axis, mask):
    size = lax.axis_size(axis)
    return lax.ppermute(values, axis, [(i, i ^ mask) for i in range(size)])


def near(values):
    return pltpu.with_memory_space_constraint(values, pltpu.VMEM)


def scalar(values):
    return pltpu.with_memory_space_constraint(values, pltpu.SMEM)


def far(values):
    return pltpu.with_memory_space_constraint(values, pltpu.HBM)


def iota(shape, dim):
    return lax.broadcasted_iota(jnp.int32, shape, dim)


def order(key, used, source, item, n_keys, length, width):
    n = key.shape[1]
    hit = ((iota((n_keys, n), 0) == key) & used).astype(F32)
    upto = (iota((n, n), 0) <= iota((n, n), 1)).astype(BF16)
    rank = jnp.dot(hit.astype(BF16), upto, preferred_element_type=F32)
    groups = jnp.floor((rank[:, n - 1 :] + (width - 1)) * (1.0 / width))
    below = (iota((n_keys, n_keys), 0) >= iota((n_keys, n_keys), 1)).astype(BF16)
    high = jnp.floor(groups * (1.0 / 128))
    lane = iota((n_keys, TILE), 1)
    parts = jnp.where(lane == 0, groups - high * 128, jnp.where(lane == 1, high, 0.0))
    ends = jnp.dot(below, parts.astype(BF16), preferred_element_type=F32)
    end = ends[:, 0:1] + ends[:, 1:2] * 128
    first = (end - groups) * width
    slot = jnp.sum(hit * (first + rank - 1.0), axis=0, keepdims=True)
    slot = jnp.where(used, slot.astype(jnp.int32), -1)
    at = (iota((length, n), 0) == slot).astype(F32).astype(BF16)
    line = iota((8, n), 0)
    values = jnp.where(line == 2, source, 1)
    values = jnp.where(line == 0, item & 255, jnp.where(line == 1, item >> 8, values))
    found = lax.dot_general(
        values.astype(F32).astype(BF16), at, (((1,), (1,)), ((), ())), preferred_element_type=F32
    ).astype(jnp.int32)
    passed = (end * width).astype(jnp.int32) <= iota((n_keys, length), 1)
    target = jnp.sum(passed.astype(F32), axis=0, keepdims=True).astype(jnp.int32)
    items = jnp.where(found[3:4] > 0, found[0:1] + found[1:2] * 256, -1)
    steps = (jnp.max(end).astype(jnp.int32) * width + PER - 1) // PER
    return items, found[2:3], target, steps, slot


def pick_kernel(
    n_out, count, ids, rows, columns, tiles,
    held, fetched, forward, steps, same_ids, slots,
    row_copy, column_copy, fetched_copy, forward_copy, arrived, early,
):
    copies = [
        pltpu.make_async_copy(rows.at[0], row_copy, arrived.at[0]),
        pltpu.make_async_copy(columns.at[0], column_copy, arrived.at[1]),
    ]
    for copy in copies:
        copy.start()
    for k in range(3):
        same_ids[k] = ids[k]
    for copy in copies:
        copy.wait()
    row, column = row_copy[...], column_copy[...]
    index = iota(row.shape, 1)
    length = forward.shape[1]
    used = (index < count[0, 0]) & (((column >> 1) & 1) == ids[0])
    source = jnp.bitwise_xor(column >> 2, ids[2]) * 2 + (column & 1)
    items, source, target, n_steps, slot = order(row, used, source, index, n_out, length, FORWARD)
    fetched_copy[...] = jnp.maximum(items, 0)
    first = pltpu.make_async_copy(fetched_copy, fetched, arrived.at[2])
    first.start()
    here = jnp.where(items >= 0, iota(items.shape, 1), length)
    forward_copy[...] = here + source * 1024 + target * 65536
    second = pltpu.make_async_copy(forward_copy, forward, arrived.at[3])
    second.start()
    slots[...] = slot
    steps[0] = n_steps
    first.wait()
    n_early = jnp.minimum(n_steps, EARLY)
    lax.fori_loop(0, n_early, functools.partial(start_fetch, tiles, fetched, held, early), 0)
    held[held.shape[0] - 1] = jnp.zeros((TILE, TILE), BF16)
    second.wait()
    lax.fori_loop(0, n_early, functools.partial(end_fetch, tiles, held, early), 0)


def start_fetch(tiles, fetched, held, arrived, g, carry):
    for j in range(PER):
        source = tiles.at[fetched[0, g * PER + j]]
        pltpu.make_async_copy(source, held.at[g * PER + j], arrived.at[g]).start()
    return carry


def end_fetch(tiles, held, arrived, g, carry):
    block = held.at[pl.ds(g * PER, PER)]
    pltpu.make_async_copy(tiles.at[pl.ds(0, PER)], block, arrived.at[g]).wait()
    return carry


def pick(count, ids, rows, columns, tiles, n_out, n_back):
    length = rows.shape[-1] + max(n_out * (FORWARD - 1), n_back * (BACKWARD - 1)) + PER
    length = -(-length // TILE) * TILE
    listed = (1, length)
    return pl.pallas_call(
        functools.partial(pick_kernel, n_out),
        out_shape=[
            pltpu.VMEM((EARLY * PER + 1, TILE, TILE), BF16),
            pltpu.SMEM(listed, jnp.int32),
            pltpu.SMEM(listed, jnp.int32),
            pltpu.SMEM((1,), jnp.int32),
            pltpu.SMEM((3,), jnp.int32),
            pltpu.VMEM(rows.shape[1:], jnp.int32),
        ],
        in_specs=[SMEM, SMEM, ANY, ANY, ANY],
        out_specs=[VMEM, SMEM, SMEM, SMEM, SMEM, VMEM],
        scratch_shapes=[
            pltpu.VMEM(rows.shape[1:], jnp.int32),
            pltpu.VMEM(rows.shape[1:], jnp.int32),
            pltpu.VMEM(listed, jnp.int32),
            pltpu.VMEM(listed, jnp.int32),
            pltpu.SemaphoreType.DMA((4,)),
            pltpu.SemaphoreType.DMA((EARLY,)),
        ],
        compiler_params=PICK_PARAMS,
        name="pick_tiles",
    )(count, ids, far(rows), far(columns), far(tiles))


def prepare_kernel(n_back, ids, rows, columns, slots, weight, bias, cotangent, *refs):
    backward, steps, weight_copy, bias_copy, cotangent_copy = refs[:5]
    row_copy, column_copy, backward_copy, arrived = refs[5:]
    pairs = [
        (rows.at[0], row_copy),
        (columns.at[0], column_copy),
        (weight, weight_copy),
        (bias, bias_copy),
        (cotangent, cotangent_copy),
    ]
    copies = [
        pltpu.make_async_copy(source, target, arrived.at[k])
        for k, (source, target) in enumerate(pairs)
    ]
    for copy in copies:
        copy.start()
    for copy in copies:
        copy.wait()
    row, column, slot = row_copy[...], column_copy[...], slots[...]
    length = backward.shape[1]
    place = (column >> 2) * 2 + (column & 1)
    source = jnp.bitwise_xor(row >> 2, ids[1]) * 4 + (row & 3)
    used = slot >= 0
    items, source, target, n_steps, slot = order(
        place, used, source, slot, n_back, length, BACKWARD
    )
    here = jnp.where(items >= 0, items, length)
    backward_copy[...] = here + source * 1024 + target * 65536
    copy = pltpu.make_async_copy(backward_copy, backward, arrived.at[5])
    copy.start()
    steps[0] = n_steps
    copy.wait()


def prepare(ids, rows, columns, slots, length, n_back, weight, bias, cotangent):
    return pl.pallas_call(
        functools.partial(prepare_kernel, n_back),
        out_shape=[
            pltpu.SMEM((1, length), jnp.int32),
            pltpu.SMEM((1,), jnp.int32),
            pltpu.VMEM(weight.shape, weight.dtype),
            pltpu.VMEM(bias.shape, bias.dtype),
            pltpu.VMEM(cotangent.shape, cotangent.dtype),
        ],
        in_specs=[SMEM, ANY, ANY, VMEM, ANY, ANY, ANY],
        out_specs=[SMEM, SMEM, VMEM, VMEM, VMEM],
        scratch_shapes=[
            pltpu.VMEM(rows.shape[1:], jnp.int32),
            pltpu.VMEM(rows.shape[1:], jnp.int32),
            pltpu.VMEM((1, length), jnp.int32),
            pltpu.SemaphoreType.DMA((6,)),
        ],
        compiler_params=PICK_PARAMS,
        name="prepare",
    )(scalar(ids), far(rows), far(columns), near(slots), far(weight), far(bias), far(cotangent))


def join_kernel(a, b, out):
    rows = a.shape[0]
    out[0:rows] = a[...]
    out[rows : 2 * rows] = b[...]


def join(a, b):
    return pl.pallas_call(
        join_kernel,
        out_shape=pltpu.VMEM((2 * a.shape[0], a.shape[1]), a.dtype),
        in_specs=[VMEM] * 2,
        out_specs=VMEM,
        compiler_params=PARAMS,
        name="join",
    )(near(a), near(b))


def add_products(flipped, g, picked, held, source, total):
    last = held.shape[0] - 1
    width = BACKWARD if flipped else FORWARD
    places = []
    products = []
    for at in range(0, PER, width):
        codes = [picked[0, g * PER + at + j] for j in range(width)]
        places.append(codes[0] >> 16)
        mine = [held[jnp.minimum(code & 1023, last)] for code in codes]
        other = [source[(code >> 10) & 63] for code in codes]
        left, right = (other, mine) if flipped else (mine, other)
        products.append(
            jnp.dot(
                jnp.concatenate(left, 1), jnp.concatenate(right, 0), preferred_element_type=F32
            )
        )
    for place, product in zip(places, products):
        total[place] += product


def forward_kernel(steps, ids, fetched, picked, tiles, early, *refs):
    sources, (held, kept, sent, gathered, total, arrived) = refs[:-6], refs[-6:]
    count = steps[0]
    start = functools.partial(start_fetch, tiles, fetched, held, arrived)
    lax.fori_loop(EARLY, jnp.maximum(count, EARLY), start, 0)
    moved = pltpu.make_async_copy(
        early.at[pl.ds(0, EARLY * PER)], held.at[pl.ds(0, EARLY * PER)], arrived.at[0]
    )
    moved.start()
    held[held.shape[0] - 1] = jnp.zeros((TILE, TILE), BF16)
    total[...] = jnp.zeros_like(total)
    for m, source in enumerate(sources):
        gathered[4 * m : 4 * m + 4] = source[...].reshape(4, TILE, TILE)

    def early_step(g, carry):
        add_products(False, g, picked, early, gathered, total)
        return carry

    def step(g, carry):
        end_fetch(tiles, held, arrived, g, 0)
        add_products(False, g, picked, held, gathered, total)
        return carry

    lax.fori_loop(0, jnp.minimum(count, EARLY), early_step, 0)
    lax.fori_loop(EARLY, jnp.maximum(count, EARLY), step, 0)
    moved.wait()
    for k in range(kept.shape[0]):
        own = jnp.bitwise_xor(ids[1], 2 * k)
        kept[k] = total[pl.ds(own * 4, 4)]
        sent[k] = total[pl.ds(jnp.bitwise_xor(own, 1) * 4, 4)].astype(BF16)


def tiles_forward(steps, ids, fetched, picked, tiles, early, sources, n_out):
    shape = (n_out // 8, 4, TILE, TILE)
    length = fetched.shape[1]
    return pl.pallas_call(
        forward_kernel,
        out_shape=[
            pltpu.VMEM((length + 1, TILE, TILE), BF16),
            pltpu.VMEM(shape, F32),
            pltpu.VMEM(shape, BF16),
        ],
        in_specs=[SMEM, SMEM, SMEM, SMEM, ANY, VMEM] + [VMEM] * len(sources),
        out_specs=[VMEM] * 3,
        scratch_shapes=[
            pltpu.VMEM((4 * len(sources), TILE, TILE), BF16),
            pltpu.VMEM((n_out + 1, TILE, TILE), F32),
            pltpu.SemaphoreType.DMA((length // PER,)),
        ],
        compiler_params=PARAMS,
        name="tiles_forward",
    )(
        scalar(steps),
        scalar(ids),
        scalar(fetched),
        scalar(picked),
        far(tiles),
        near(early),
        *[near(values) for values in sources],
    )


def backward_kernel(steps, ids, picked, held, *refs):
    sources, (kept, first, second, third, gathered, total) = refs[:-6], refs[-6:]
    total[...] = jnp.zeros_like(total)
    for m, source in enumerate(sources):
        gathered[4 * m : 4 * m + 4] = source[0 : 4 * TILE].reshape(4, TILE, TILE)

    def step(g, carry):
        add_products(True, g, picked, held, gathered, total)
        return carry

    lax.fori_loop(0, steps[0], step, 0)
    for k, out in enumerate((kept, first, second, third)):
        for z in range(2):
            block = pl.ds(jnp.bitwise_xor(ids[2], 2 * k + z) * 2, 2)
            out[2 * z : 2 * z + 2] = total[block].astype(out.dtype)


def tiles_backward(steps, ids, picked, held, sources, n_back):
    shape = (n_back // 4, TILE, TILE)
    return pl.pallas_call(
        backward_kernel,
        out_shape=[pltpu.VMEM(shape, F32)] + [pltpu.VMEM(shape, BF16)] * 3,
        in_specs=[SMEM, SMEM, SMEM] + [VMEM] * (1 + len(sources)),
        out_specs=[VMEM] * 4,
        scratch_shapes=[
            pltpu.VMEM((4 * len(sources), TILE, TILE), BF16),
            pltpu.VMEM((n_back + 1, TILE, TILE), F32),
        ],
        compiler_params=PARAMS,
        name="tiles_backward",
    )(scalar(steps), scalar(ids), scalar(picked), near(held), *[near(values) for values in sources])


def pair_kernel(kept, got, first, *others):
    first[...] = kept[0] + got[0].astype(F32)
    for k, other in enumerate(others):
        other[...] = (kept[k + 1] + got[k + 1].astype(F32)).astype(BF16)


def pair_sum(kept, got):
    shape = kept.shape[1:]
    n = kept.shape[0] - 1
    return pl.pallas_call(
        pair_kernel,
        out_shape=[pltpu.VMEM(shape, F32)] + [pltpu.VMEM(shape, BF16)] * n,
        in_specs=[VMEM] * 2,
        out_specs=[VMEM] * (n + 1),
        compiler_params=PARAMS,
        name="pair_sum",
    )(near(kept), near(got))


def own_kernel(first, a, b, c, total, sent):
    value = first[...] + a[...].astype(F32) + b[...].astype(F32) + c[...].astype(F32)
    total[...] = value
    sent[...] = value.astype(BF16)


def own_sum(first, others):
    return pl.pallas_call(
        own_kernel,
        out_shape=[pltpu.VMEM(first.shape, F32), pltpu.VMEM(first.shape, BF16)],
        in_specs=[VMEM] * 4,
        out_specs=[VMEM] * 2,
        compiler_params=PARAMS,
        name="own_sum",
    )(near(first), *[near(values) for values in others])


def middle_kernel(own, other, weight, bias, cotangent, activations, back, back_sent, grads):
    blocks = own.shape[0]
    rows = blocks * TILE
    sums = (own[...] + other[...].astype(F32)).astype(BF16).reshape(rows, TILE)
    preact = jnp.dot(sums, weight[...], preferred_element_type=F32) + bias[...]
    sigma = jax.nn.sigmoid(preact)
    activations[...] = (preact * sigma).astype(BF16)
    grad = cotangent[...].astype(F32) * (sigma * (1.0 + preact * (1.0 - sigma)))
    grad_pre = grad.astype(BF16)
    grads[0:TILE] = lax.dot_general(
        sums, grad_pre, (((0,), (0,)), ((), ())), preferred_element_type=F32
    )
    total = jnp.sum(grad_pre.astype(F32), axis=0, keepdims=True)
    grads[TILE : TILE + 8] = jnp.broadcast_to(total, (8, TILE))
    for b in range(blocks):
        value = lax.dot_general(
            weight[...],
            grad_pre[b * TILE : (b + 1) * TILE],
            (((1,), (1,)), ((), ())),
            preferred_element_type=F32,
        )
        back[b] = value
        back_sent[b] = value.astype(BF16)


def middle(own, other, weight, bias, cotangent):
    return pl.pallas_call(
        middle_kernel,
        out_shape=[
            jax.ShapeDtypeStruct(cotangent.shape, BF16),
            pltpu.VMEM(own.shape, F32),
            pltpu.VMEM(own.shape, BF16),
            pltpu.VMEM((TILE + 8, TILE), F32),
        ],
        in_specs=[VMEM] * 5,
        out_specs=[VMEM] * 4,
        compiler_params=PARAMS,
        name="middle",
    )(near(own), near(other), near(weight), near(bias), near(cotangent))


def message_kernel(ids, back, other, grads, more, message):
    rows = back.shape[0] * TILE
    value = back[...] + other[...].astype(F32)
    message[0:rows] = value.astype(BF16).reshape(rows, TILE)
    half = pl.ds((ids[1] & 1) * (TILE // 2), TILE // 2)
    message[rows : rows + TILE // 2] = (grads[half] + more[half]).astype(BF16)
    rest = grads[TILE : TILE + 8] + more[TILE : TILE + 8]
    rest = jnp.concatenate([rest, rest], 0)
    line = iota(rest.shape, 0)
    terms = jnp.zeros(rest.shape, F32)
    for k in range(3):
        term = rest.astype(BF16).astype(F32)
        terms = jnp.where(line == k, term, terms)
        rest = rest - term
    message[rows + TILE // 2 : rows + TILE // 2 + 16] = terms.astype(BF16)


def message(ids, back, other, grads, more):
    rows = back.shape[0] * TILE + TILE // 2 + 16
    return pl.pallas_call(
        message_kernel,
        out_shape=pltpu.VMEM((rows, TILE), BF16),
        in_specs=[SMEM] + [VMEM] * 4,
        out_specs=VMEM,
        compiler_params=PARAMS,
        name="message",
    )(scalar(ids), near(back), near(other), near(grads), near(more))


def grad_kernel(ids, *refs):
    messages, grads = refs[:-1], refs[-1]
    last = messages[0].shape[0] - 16
    for k in range(2):
        weight = jnp.zeros((TILE // 2, TILE), F32)
        for one in messages[k::2]:
            weight = weight + one[last - TILE // 2 : last].astype(F32)
        grads[pl.ds(jnp.bitwise_xor(ids[1] & 1, k) * (TILE // 2), TILE // 2)] = weight
    bias = jnp.zeros((16, TILE), F32)
    for one in messages[0::2]:
        bias = bias + one[last : last + 16].astype(F32)
    grads[TILE : TILE + 8] = jnp.broadcast_to(jnp.sum(bias, axis=0, keepdims=True), (8, TILE))


def grad_sum(ids, messages):
    return pl.pallas_call(
        grad_kernel,
        out_shape=pltpu.VMEM((TILE + 8, TILE), F32),
        in_specs=[SMEM] + [VMEM] * len(messages),
        out_specs=VMEM,
        compiler_params=PARAMS,
        name="grad_sum",
    )(scalar(ids), *[near(one) for one in messages])


def line_kernel(kept, a, b, c, own, own_sent, other_sent):
    blocks = own.shape[0]
    value = kept[...] + a[...].astype(F32) + b[...].astype(F32) + c[...].astype(F32)
    own[...] = value[:blocks]
    own_sent[...] = value[:blocks].astype(BF16)
    other_sent[...] = value[blocks:].astype(BF16)


def line_sum(kept, others):
    shape = (kept.shape[0] // 2, TILE, TILE)
    return pl.pallas_call(
        line_kernel,
        out_shape=[pltpu.VMEM(shape, F32), pltpu.VMEM(shape, BF16), pltpu.VMEM(shape, BF16)],
        in_specs=[VMEM] * 4,
        out_specs=[VMEM] * 3,
        compiler_params=PARAMS,
        name="line_sum",
    )(near(kept), *[near(values) for values in others])


def finish_kernel(ids, own, beside, opposite, corner, grads, more, features, weight, bias):
    blocks = own.shape[0]
    for b in range(blocks):
        mine = own[b] + beside[b].astype(F32)
        other = opposite[b].astype(F32) + corner[b].astype(F32)
        features[pl.ds((ids[0] * blocks + b) * TILE, TILE)] = mine.T
        features[pl.ds(((1 - ids[0]) * blocks + b) * TILE, TILE)] = other.T
    weight[...] = grads[0:TILE] + more[0:TILE]
    bias[...] = grads[TILE : TILE + 1] + more[TILE : TILE + 1]


def finish(ids, own, beside, opposite, corner, grads, more):
    return pl.pallas_call(
        finish_kernel,
        out_shape=[
            jax.ShapeDtypeStruct((2 * own.shape[0] * TILE, TILE), F32),
            jax.ShapeDtypeStruct((TILE, TILE), F32),
            jax.ShapeDtypeStruct((1, TILE), F32),
        ],
        in_specs=[SMEM] + [VMEM] * 6,
        out_specs=[VMEM] * 3,
        compiler_params=PARAMS,
        name="finish",
    )(scalar(ids), near(own), near(beside), near(opposite), near(corner), near(grads), near(more))


def local(
    features, weight, hidden_bias, adjacency_tiles, tile_rows, tile_columns, tile_count, cotangent
):
    tiles = adjacency_tiles[0, 0]
    n_row, n_col = lax.axis_size("row"), lax.axis_size("col")
    own_rows, fin = features.shape
    blocks = own_rows // TILE
    n_out, n_back = blocks * n_col, blocks // 2 * n_row
    half = lax.axis_index("feat")
    ids = jnp.stack([half, lax.axis_index("col"), lax.axis_index("row")]).astype(jnp.int32)

    mine = lax.dynamic_slice_in_dim(features, half * (own_rows // 2), own_rows // 2, 0)
    beside, ids = lax.optimization_barrier((swap(mine, "row", 1), ids))
    pair = join(mine, beside)
    sources = [swap(pair, "row", mask) for mask in range(2, n_row, 2)]
    lists = pick(tile_count, ids, tile_rows, tile_columns, tiles, n_out, n_back)
    lists, sources = lax.optimization_barrier((lists, sources))
    early, fetched, forward, steps, ids, slots = lists

    held, kept, sent = tiles_forward(steps, ids, fetched, forward, tiles, early, [pair, *sources], n_out)
    first, *others = pair_sum(kept, swap(sent, "col", 1))
    others = [swap(other, "col", 2 * k + 2) for k, other in enumerate(others)]
    own, sent = own_sum(first, others)
    sent, slots = lax.optimization_barrier((sent, slots))
    ready = prepare(
        ids, tile_rows, tile_columns, slots, forward.shape[1], n_back, weight, hidden_bias[None], cotangent
    )
    other, ready = lax.optimization_barrier((swap(sent, "feat", 1), ready))
    backward, steps, weight, bias, cotangent = ready
    activations, back, back_sent, grads = middle(own, other, weight, bias, cotangent)

    back_other, more = lax.optimization_barrier((swap(back_sent, "feat", 1), swap(grads, "col", 1)))
    mine = message(ids, back, back_other, grads, more)
    across = [swap(mine, "col", mask) for mask in (2, 6, 4)]
    beside = swap(mine, "col", 1)
    across = lax.optimization_barrier(across)
    corners = [swap(values, "col", 1) for values in across]
    sources = [mine, beside, across[0], corners[0], across[2], corners[2], across[1], corners[1]]
    grads = grad_sum(ids, sources)
    more = swap(grads, "row", 1)
    kept, *others = tiles_backward(steps, ids, backward, held, sources, n_back)
    others, more = lax.optimization_barrier((others, more))
    grads = grads + more

    others = [swap(other, "row", 2 * k + 2) for k, other in enumerate(others)]
    others, more = lax.optimization_barrier((others, swap(grads, "row", 2)))
    grads = grads + more
    own, own_sent, other_sent = line_sum(kept, others)
    own_sent, other_sent, grads = lax.optimization_barrier((own_sent, other_sent, grads))
    opposite = swap(own_sent, "feat", 1)
    corner = swap(other_sent, ("row", "feat"), 3)
    beside = swap(other_sent, "row", 1)
    opposite, corner, beside, more = lax.optimization_barrier(
        (opposite, corner, beside, swap(grads, "row", 4))
    )
    grad_features, grad_weight, grad_bias = finish(ids, own, beside, opposite, corner, grads, more)
    return (activations, grad_features, grad_weight, grad_bias[0])


def solution(mesh):
    placed = (
        P(("col", "row"), None),
        P(None, "feat"),
        P("feat"),
        P("row", "col", None, None, None),
        P("row", "col", None),
        P("row", "col", None),
        P("row", "col"),
        P(("row", "col"), "feat"),
    )
    return jax.shard_map(
        local,
        mesh=mesh,
        in_specs=placed,
        out_specs=(P(("row", "col"), "feat"), P(("col", "row"), None), P(None, "feat"), P("feat")),
        check_vma=False,
    )
```

```python
import functools

import jax
import jax.numpy as jnp
from jax import lax
from jax.experimental import pallas as pl
from jax.experimental.pallas import tpu as pltpu
from jax.sharding import PartitionSpec as P

F32 = jnp.float32
BF16 = jnp.bfloat16
TILE = 128
PER = 32
FORWARD = 2
BACKWARD = 4
SPARE = 1023
EARLY = 4
VMEM = pl.BlockSpec(memory_space=pltpu.VMEM)
SMEM = pl.BlockSpec(memory_space=pltpu.SMEM)
ANY = pl.BlockSpec(memory_space=pl.ANY)
PARAMS = pltpu.CompilerParams(vmem_limit_bytes=8 * 1024 * 1024)
PICK_PARAMS = pltpu.CompilerParams(vmem_limit_bytes=16 * 1024 * 1024)


def swap(values, axis, mask):
    size = lax.axis_size(axis)
    return lax.ppermute(values, axis, [(i, i ^ mask) for i in range(size)])


def near(values):
    return pltpu.with_memory_space_constraint(values, pltpu.VMEM)


def scalar(values):
    return pltpu.with_memory_space_constraint(values, pltpu.SMEM)


def far(values):
    return pltpu.with_memory_space_constraint(values, pltpu.HBM)


def iota(shape, dim):
    return lax.broadcasted_iota(jnp.int32, shape, dim)


def order(key, used, source, item, n_keys, length, width):
    n = key.shape[1]
    hit = ((iota((n_keys, n), 0) == key) & used).astype(F32)
    upto = (iota((n, n), 0) <= iota((n, n), 1)).astype(BF16)
    rank = jnp.dot(hit.astype(BF16), upto, preferred_element_type=F32)
    groups = jnp.floor((rank[:, n - 1 :] + (width - 1)) * (1.0 / width))
    below = (iota((n_keys, n_keys), 0) >= iota((n_keys, n_keys), 1)).astype(BF16)
    high = jnp.floor(groups * (1.0 / 128))
    lane = iota((n_keys, TILE), 1)
    parts = jnp.where(lane == 0, groups - high * 128, jnp.where(lane == 1, high, 0.0))
    ends = jnp.dot(below, parts.astype(BF16), preferred_element_type=F32)
    end = ends[:, 0:1] + ends[:, 1:2] * 128
    first = (end - groups) * width
    slot = jnp.sum(hit * (first + rank - 1.0), axis=0, keepdims=True)
    slot = jnp.where(used, slot.astype(jnp.int32), -1)
    at = (iota((length, n), 0) == slot).astype(F32).astype(BF16)
    line = iota((8, n), 0)
    values = jnp.where(line == 2, source, 1)
    values = jnp.where(line == 0, item & 255, jnp.where(line == 1, item >> 8, values))
    found = lax.dot_general(
        values.astype(F32).astype(BF16), at, (((1,), (1,)), ((), ())), preferred_element_type=F32
    ).astype(jnp.int32)
    passed = (end * width).astype(jnp.int32) <= iota((n_keys, length), 1)
    target = jnp.sum(passed.astype(F32), axis=0, keepdims=True).astype(jnp.int32)
    items = jnp.where(found[3:4] > 0, found[0:1] + found[1:2] * 256, -1)
    steps = (jnp.max(end).astype(jnp.int32) * width + PER - 1) // PER
    return items, found[2:3], target, steps, slot


def pick_kernel(n_out, count, ids, rows, columns, *refs):
    fetched, forward, steps, same_ids, slots = refs[:5]
    row_copy, column_copy, fetched_copy, forward_copy, arrived = refs[5:]
    copies = [
        pltpu.make_async_copy(rows.at[0], row_copy, arrived.at[0]),
        pltpu.make_async_copy(columns.at[0], column_copy, arrived.at[1]),
    ]
    for copy in copies:
        copy.start()
    for k in range(3):
        same_ids[k] = ids[k]
    for copy in copies:
        copy.wait()
    row, column = row_copy[...], column_copy[...]
    index = iota(row.shape, 1)
    length = forward.shape[1]
    used = (index < count[0, 0]) & (((column >> 1) & 1) == ids[0])
    source = jnp.bitwise_xor(column >> 2, ids[2]) * 2 + (column & 1)
    items, source, target, n_steps, slot = order(row, used, source, index, n_out, length, FORWARD)
    fetched_copy[...] = jnp.maximum(items, 0)
    here = jnp.where(items >= 0, iota(items.shape, 1), SPARE)
    forward_copy[...] = here + source * 1024 + target * 65536
    copies = [
        pltpu.make_async_copy(fetched_copy, fetched, arrived.at[0]),
        pltpu.make_async_copy(forward_copy, forward, arrived.at[1]),
    ]
    for copy in copies:
        copy.start()
    slots[...] = slot
    steps[0] = n_steps
    for copy in copies:
        copy.wait()


def pick(count, ids, rows, columns, n_out, n_back):
    length = rows.shape[-1] + max(n_out * (FORWARD - 1), n_back * (BACKWARD - 1)) + PER
    length = -(-length // TILE) * TILE
    listed = (1, length)
    return pl.pallas_call(
        functools.partial(pick_kernel, n_out),
        out_shape=[
            pltpu.SMEM(listed, jnp.int32),
            pltpu.SMEM(listed, jnp.int32),
            pltpu.SMEM((1,), jnp.int32),
            pltpu.SMEM((3,), jnp.int32),
            pltpu.VMEM(rows.shape[1:], jnp.int32),
        ],
        in_specs=[SMEM, SMEM, ANY, ANY],
        out_specs=[SMEM, SMEM, SMEM, SMEM, VMEM],
        scratch_shapes=[
            pltpu.VMEM(rows.shape[1:], jnp.int32),
            pltpu.VMEM(rows.shape[1:], jnp.int32),
            pltpu.VMEM(listed, jnp.int32),
            pltpu.VMEM(listed, jnp.int32),
            pltpu.SemaphoreType.DMA((2,)),
        ],
        compiler_params=PICK_PARAMS,
        name="pick_tiles",
    )(count, ids, far(rows), far(columns))


def start_fetch(tiles, fetched, held, arrived, g, carry):
    for j in range(PER):
        source = tiles.at[fetched[0, g * PER + j]]
        pltpu.make_async_copy(source, held.at[g * PER + j], arrived.at[g]).start()
    return carry


def end_fetch(tiles, held, arrived, g, carry):
    block = held.at[pl.ds(g * PER, PER)]
    pltpu.make_async_copy(tiles.at[pl.ds(0, PER)], block, arrived.at[g]).wait()
    return carry


def early_kernel(steps, fetched, tiles, early, arrived):
    count = jnp.minimum(steps[0], EARLY)
    lax.fori_loop(0, count, functools.partial(start_fetch, tiles, fetched, early, arrived), 0)
    early[early.shape[0] - 1] = jnp.zeros((TILE, TILE), BF16)
    lax.fori_loop(0, count, functools.partial(end_fetch, tiles, early, arrived), 0)


def early_tiles(steps, fetched, tiles):
    return pl.pallas_call(
        early_kernel,
        out_shape=pltpu.VMEM((EARLY * PER + 1, TILE, TILE), BF16),
        in_specs=[SMEM, SMEM, ANY],
        out_specs=VMEM,
        scratch_shapes=[pltpu.SemaphoreType.DMA((EARLY,))],
        compiler_params=PARAMS,
        name="early_tiles",
    )(scalar(steps), scalar(fetched), far(tiles))


def prepare_kernel(n_back, ids, rows, columns, slots, weight, bias, cotangent, *refs):
    backward, steps, weight_copy, bias_copy, cotangent_copy = refs[:5]
    row_copy, column_copy, backward_copy, arrived = refs[5:]
    pairs = [
        (rows.at[0], row_copy),
        (columns.at[0], column_copy),
        (weight, weight_copy),
        (bias, bias_copy),
        (cotangent, cotangent_copy),
    ]
    copies = [
        pltpu.make_async_copy(source, target, arrived.at[k])
        for k, (source, target) in enumerate(pairs)
    ]
    for copy in copies:
        copy.start()
    for copy in copies:
        copy.wait()
    row, column, slot = row_copy[...], column_copy[...], slots[...]
    length = backward.shape[1]
    place = (column >> 2) * 2 + (column & 1)
    source = jnp.bitwise_xor(row >> 2, ids[1]) * 4 + (row & 3)
    used = slot >= 0
    items, source, target, n_steps, slot = order(
        place, used, source, slot, n_back, length, BACKWARD
    )
    here = jnp.where(items >= 0, items, SPARE)
    backward_copy[...] = here + source * 1024 + target * 65536
    copy = pltpu.make_async_copy(backward_copy, backward, arrived.at[5])
    copy.start()
    steps[0] = n_steps
    copy.wait()


def prepare(ids, rows, columns, slots, length, n_back, weight, bias, cotangent):
    return pl.pallas_call(
        functools.partial(prepare_kernel, n_back),
        out_shape=[
            pltpu.SMEM((1, length), jnp.int32),
            pltpu.SMEM((1,), jnp.int32),
            pltpu.VMEM(weight.shape, weight.dtype),
            pltpu.VMEM(bias.shape, bias.dtype),
            pltpu.VMEM(cotangent.shape, cotangent.dtype),
        ],
        in_specs=[SMEM, ANY, ANY, VMEM, ANY, ANY, ANY],
        out_specs=[SMEM, SMEM, VMEM, VMEM, VMEM],
        scratch_shapes=[
            pltpu.VMEM(rows.shape[1:], jnp.int32),
            pltpu.VMEM(rows.shape[1:], jnp.int32),
            pltpu.VMEM((1, length), jnp.int32),
            pltpu.SemaphoreType.DMA((6,)),
        ],
        compiler_params=PICK_PARAMS,
        name="prepare",
    )(scalar(ids), far(rows), far(columns), near(slots), far(weight), far(bias), far(cotangent))


def join_kernel(a, b, out):
    rows = a.shape[0]
    out[0:rows] = a[...]
    out[rows : 2 * rows] = b[...]


def join(a, b):
    return pl.pallas_call(
        join_kernel,
        out_shape=pltpu.VMEM((2 * a.shape[0], a.shape[1]), a.dtype),
        in_specs=[VMEM] * 2,
        out_specs=VMEM,
        compiler_params=PARAMS,
        name="join",
    )(near(a), near(b))


def add_products(flipped, g, picked, held, source, total):
    last = held.shape[0] - 1
    width = BACKWARD if flipped else FORWARD
    places = []
    products = []
    for at in range(0, PER, width):
        codes = [picked[0, g * PER + at + j] for j in range(width)]
        places.append(codes[0] >> 16)
        mine = [held[jnp.minimum(code & 1023, last)] for code in codes]
        other = [source[(code >> 10) & 63] for code in codes]
        left, right = (other, mine) if flipped else (mine, other)
        products.append(
            jnp.dot(
                jnp.concatenate(left, 1), jnp.concatenate(right, 0), preferred_element_type=F32
            )
        )
    for place, product in zip(places, products):
        total[place] += product


def forward_kernel(steps, ids, fetched, picked, tiles, early, *refs):
    sources, (held, kept, sent, gathered, total, arrived) = refs[:-6], refs[-6:]
    count = steps[0]
    start = functools.partial(start_fetch, tiles, fetched, held, arrived)
    lax.fori_loop(EARLY, jnp.maximum(count, EARLY), start, 0)
    moved = pltpu.make_async_copy(
        early.at[pl.ds(0, EARLY * PER)], held.at[pl.ds(0, EARLY * PER)], arrived.at[0]
    )
    moved.start()
    held[held.shape[0] - 1] = jnp.zeros((TILE, TILE), BF16)
    total[...] = jnp.zeros_like(total)
    for m, source in enumerate(sources):
        gathered[4 * m : 4 * m + 4] = source[...].reshape(4, TILE, TILE)

    def early_step(g, carry):
        add_products(False, g, picked, early, gathered, total)
        return carry

    def step(g, carry):
        end_fetch(tiles, held, arrived, g, 0)
        add_products(False, g, picked, held, gathered, total)
        return carry

    lax.fori_loop(0, jnp.minimum(count, EARLY), early_step, 0)
    lax.fori_loop(EARLY, jnp.maximum(count, EARLY), step, 0)
    moved.wait()
    for k in range(kept.shape[0]):
        own = jnp.bitwise_xor(ids[1], 2 * k)
        kept[k] = total[pl.ds(own * 4, 4)]
        sent[k] = total[pl.ds(jnp.bitwise_xor(own, 1) * 4, 4)].astype(BF16)


def tiles_forward(steps, ids, fetched, picked, tiles, early, sources, n_out):
    shape = (n_out // 8, 4, TILE, TILE)
    length = -(-(tiles.shape[0] + n_out * (FORWARD - 1)) // PER) * PER
    return pl.pallas_call(
        forward_kernel,
        out_shape=[
            pltpu.VMEM((length + 1, TILE, TILE), BF16),
            pltpu.VMEM(shape, F32),
            pltpu.VMEM(shape, BF16),
        ],
        in_specs=[SMEM, SMEM, SMEM, SMEM, ANY, VMEM] + [VMEM] * len(sources),
        out_specs=[VMEM] * 3,
        scratch_shapes=[
            pltpu.VMEM((4 * len(sources), TILE, TILE), BF16),
            pltpu.VMEM((n_out + 1, TILE, TILE), F32),
            pltpu.SemaphoreType.DMA((length // PER,)),
        ],
        compiler_params=PARAMS,
        name="tiles_forward",
    )(
        scalar(steps),
        scalar(ids),
        scalar(fetched),
        scalar(picked),
        far(tiles),
        near(early),
        *[near(values) for values in sources],
    )


def backward_kernel(steps, ids, picked, held, *refs):
    sources, (kept, first, second, third, gathered, total) = refs[:-6], refs[-6:]
    total[...] = jnp.zeros_like(total)
    for m, source in enumerate(sources):
        gathered[4 * m : 4 * m + 4] = source[0 : 4 * TILE].reshape(4, TILE, TILE)

    def step(g, carry):
        add_products(True, g, picked, held, gathered, total)
        return carry

    lax.fori_loop(0, steps[0], step, 0)
    for k, out in enumerate((kept, first, second, third)):
        for z in range(2):
            block = pl.ds(jnp.bitwise_xor(ids[2], 2 * k + z) * 2, 2)
            out[2 * z : 2 * z + 2] = total[block].astype(out.dtype)


def tiles_backward(steps, ids, picked, held, sources, n_back):
    shape = (n_back // 4, TILE, TILE)
    return pl.pallas_call(
        backward_kernel,
        out_shape=[pltpu.VMEM(shape, F32)] + [pltpu.VMEM(shape, BF16)] * 3,
        in_specs=[SMEM, SMEM, SMEM] + [VMEM] * (1 + len(sources)),
        out_specs=[VMEM] * 4,
        scratch_shapes=[
            pltpu.VMEM((4 * len(sources), TILE, TILE), BF16),
            pltpu.VMEM((n_back + 1, TILE, TILE), F32),
        ],
        compiler_params=PARAMS,
        name="tiles_backward",
    )(scalar(steps), scalar(ids), scalar(picked), near(held), *[near(values) for values in sources])


def pair_kernel(kept, got, first, *others):
    first[...] = kept[0] + got[0].astype(F32)
    for k, other in enumerate(others):
        other[...] = (kept[k + 1] + got[k + 1].astype(F32)).astype(BF16)


def pair_sum(kept, got):
    shape = kept.shape[1:]
    n = kept.shape[0] - 1
    return pl.pallas_call(
        pair_kernel,
        out_shape=[pltpu.VMEM(shape, F32)] + [pltpu.VMEM(shape, BF16)] * n,
        in_specs=[VMEM] * 2,
        out_specs=[VMEM] * (n + 1),
        compiler_params=PARAMS,
        name="pair_sum",
    )(near(kept), near(got))


def own_kernel(first, a, b, c, total, sent):
    value = first[...] + a[...].astype(F32) + b[...].astype(F32) + c[...].astype(F32)
    total[...] = value
    sent[...] = value.astype(BF16)


def own_sum(first, others):
    return pl.pallas_call(
        own_kernel,
        out_shape=[pltpu.VMEM(first.shape, F32), pltpu.VMEM(first.shape, BF16)],
        in_specs=[VMEM] * 4,
        out_specs=[VMEM] * 2,
        compiler_params=PARAMS,
        name="own_sum",
    )(near(first), *[near(values) for values in others])


def middle_kernel(own, other, weight, bias, cotangent, activations, back, back_sent, grads):
    blocks = own.shape[0]
    rows = blocks * TILE
    sums = (own[...] + other[...].astype(F32)).astype(BF16).reshape(rows, TILE)
    preact = jnp.dot(sums, weight[...], preferred_element_type=F32) + bias[...]
    sigma = jax.nn.sigmoid(preact)
    activations[...] = (preact * sigma).astype(BF16)
    grad = cotangent[...].astype(F32) * (sigma * (1.0 + preact * (1.0 - sigma)))
    grad_pre = grad.astype(BF16)
    grads[0:TILE] = lax.dot_general(
        sums, grad_pre, (((0,), (0,)), ((), ())), preferred_element_type=F32
    )
    total = jnp.sum(grad_pre.astype(F32), axis=0, keepdims=True)
    grads[TILE : TILE + 8] = jnp.broadcast_to(total, (8, TILE))
    for b in range(blocks):
        value = lax.dot_general(
            weight[...],
            grad_pre[b * TILE : (b + 1) * TILE],
            (((1,), (1,)), ((), ())),
            preferred_element_type=F32,
        )
        back[b] = value
        back_sent[b] = value.astype(BF16)


def middle(own, other, weight, bias, cotangent):
    return pl.pallas_call(
        middle_kernel,
        out_shape=[
            jax.ShapeDtypeStruct(cotangent.shape, BF16),
            pltpu.VMEM(own.shape, F32),
            pltpu.VMEM(own.shape, BF16),
            pltpu.VMEM((TILE + 8, TILE), F32),
        ],
        in_specs=[VMEM] * 5,
        out_specs=[VMEM] * 4,
        compiler_params=PARAMS,
        name="middle",
    )(near(own), near(other), near(weight), near(bias), near(cotangent))


def message_kernel(ids, back, other, grads, more, message):
    rows = back.shape[0] * TILE
    value = back[...] + other[...].astype(F32)
    message[0:rows] = value.astype(BF16).reshape(rows, TILE)
    half = pl.ds((ids[1] & 1) * (TILE // 2), TILE // 2)
    message[rows : rows + TILE // 2] = (grads[half] + more[half]).astype(BF16)
    rest = grads[TILE : TILE + 8] + more[TILE : TILE + 8]
    rest = jnp.concatenate([rest, rest], 0)
    line = iota(rest.shape, 0)
    terms = jnp.zeros(rest.shape, F32)
    for k in range(3):
        term = rest.astype(BF16).astype(F32)
        terms = jnp.where(line == k, term, terms)
        rest = rest - term
    message[rows + TILE // 2 : rows + TILE // 2 + 16] = terms.astype(BF16)


def message(ids, back, other, grads, more):
    rows = back.shape[0] * TILE + TILE // 2 + 16
    return pl.pallas_call(
        message_kernel,
        out_shape=pltpu.VMEM((rows, TILE), BF16),
        in_specs=[SMEM] + [VMEM] * 4,
        out_specs=VMEM,
        compiler_params=PARAMS,
        name="message",
    )(scalar(ids), near(back), near(other), near(grads), near(more))


def grad_kernel(ids, *refs):
    messages, grads = refs[:-1], refs[-1]
    last = messages[0].shape[0] - 16
    for k in range(2):
        weight = jnp.zeros((TILE // 2, TILE), F32)
        for one in messages[k::2]:
            weight = weight + one[last - TILE // 2 : last].astype(F32)
        grads[pl.ds(jnp.bitwise_xor(ids[1] & 1, k) * (TILE // 2), TILE // 2)] = weight
    bias = jnp.zeros((16, TILE), F32)
    for one in messages[0::2]:
        bias = bias + one[last : last + 16].astype(F32)
    grads[TILE : TILE + 8] = jnp.broadcast_to(jnp.sum(bias, axis=0, keepdims=True), (8, TILE))


def grad_sum(ids, messages):
    return pl.pallas_call(
        grad_kernel,
        out_shape=pltpu.VMEM((TILE + 8, TILE), F32),
        in_specs=[SMEM] + [VMEM] * len(messages),
        out_specs=VMEM,
        compiler_params=PARAMS,
        name="grad_sum",
    )(scalar(ids), *[near(one) for one in messages])


def line_kernel(kept, a, b, c, own, own_sent, other_sent):
    blocks = own.shape[0]
    value = kept[...] + a[...].astype(F32) + b[...].astype(F32) + c[...].astype(F32)
    own[...] = value[:blocks]
    own_sent[...] = value[:blocks].astype(BF16)
    other_sent[...] = value[blocks:].astype(BF16)


def line_sum(kept, others):
    shape = (kept.shape[0] // 2, TILE, TILE)
    return pl.pallas_call(
        line_kernel,
        out_shape=[pltpu.VMEM(shape, F32), pltpu.VMEM(shape, BF16), pltpu.VMEM(shape, BF16)],
        in_specs=[VMEM] * 4,
        out_specs=[VMEM] * 3,
        compiler_params=PARAMS,
        name="line_sum",
    )(near(kept), *[near(values) for values in others])


def finish_kernel(ids, own, beside, opposite, corner, grads, more, features, weight, bias):
    blocks = own.shape[0]
    for b in range(blocks):
        mine = own[b] + beside[b].astype(F32)
        other = opposite[b].astype(F32) + corner[b].astype(F32)
        features[pl.ds((ids[0] * blocks + b) * TILE, TILE)] = mine.T
        features[pl.ds(((1 - ids[0]) * blocks + b) * TILE, TILE)] = other.T
    weight[...] = grads[0:TILE] + more[0:TILE]
    bias[...] = grads[TILE : TILE + 1] + more[TILE : TILE + 1]


def finish(ids, own, beside, opposite, corner, grads, more):
    return pl.pallas_call(
        finish_kernel,
        out_shape=[
            jax.ShapeDtypeStruct((2 * own.shape[0] * TILE, TILE), F32),
            jax.ShapeDtypeStruct((TILE, TILE), F32),
            jax.ShapeDtypeStruct((1, TILE), F32),
        ],
        in_specs=[SMEM] + [VMEM] * 6,
        out_specs=[VMEM] * 3,
        compiler_params=PARAMS,
        name="finish",
    )(scalar(ids), near(own), near(beside), near(opposite), near(corner), near(grads), near(more))


def local(
    features, weight, hidden_bias, adjacency_tiles, tile_rows, tile_columns, tile_count, cotangent
):
    tiles = adjacency_tiles[0, 0]
    n_row, n_col = lax.axis_size("row"), lax.axis_size("col")
    own_rows, fin = features.shape
    blocks = own_rows // TILE
    n_out, n_back = blocks * n_col, blocks // 2 * n_row
    half = lax.axis_index("feat")
    ids = jnp.stack([half, lax.axis_index("col"), lax.axis_index("row")]).astype(jnp.int32)

    mine = lax.dynamic_slice_in_dim(features, half * (own_rows // 2), own_rows // 2, 0)
    lists = pick(tile_count, ids, tile_rows, tile_columns, n_out, n_back)
    beside, lists = lax.optimization_barrier((swap(mine, "row", 1), lists))
    fetched, forward, steps, ids, slots = lists
    pair = join(mine, beside)
    sources = [swap(pair, "row", mask) for mask in range(2, n_row, 2)]
    early = early_tiles(steps, fetched, tiles)
    early, sources = lax.optimization_barrier((early, sources))

    held, kept, sent = tiles_forward(steps, ids, fetched, forward, tiles, early, [pair, *sources], n_out)
    first, *others = pair_sum(kept, swap(sent, "col", 1))
    others = [swap(other, "col", 2 * k + 2) for k, other in enumerate(others)]
    own, sent = own_sum(first, others)
    sent, slots = lax.optimization_barrier((sent, slots))
    ready = prepare(
        ids, tile_rows, tile_columns, slots, forward.shape[1], n_back, weight, hidden_bias[None], cotangent
    )
    other, ready = lax.optimization_barrier((swap(sent, "feat", 1), ready))
    backward, steps, weight, bias, cotangent = ready
    activations, back, back_sent, grads = middle(own, other, weight, bias, cotangent)

    grads = grads + swap(grads, "col", 1)
    back_other, more = lax.optimization_barrier((swap(back_sent, "feat", 1), swap(grads, "row", 1)))
    mine = message(ids, back, back_other, grads, more)
    across = [swap(mine, "col", mask) for mask in (2, 6, 4)]
    beside = swap(mine, "col", 1)
    across = lax.optimization_barrier(across)
    corners = [swap(values, "col", 1) for values in across]
    sources = [mine, beside, across[0], corners[0], across[2], corners[2], across[1], corners[1]]
    grads = grad_sum(ids, sources)
    more = swap(grads, "row", 2)
    kept, *others = tiles_backward(steps, ids, backward, held, sources, n_back)
    others, more = lax.optimization_barrier((others, more))
    grads = grads + more

    others = [swap(other, "row", 2 * k + 2) for k, other in enumerate(others)]
    others, more = lax.optimization_barrier((others, swap(grads, "row", 4)))
    own, own_sent, other_sent = line_sum(kept, others)
    opposite = swap(own_sent, "feat", 1)
    corner = swap(other_sent, ("row", "feat"), 3)
    beside = swap(other_sent, "row", 1)
    grad_features, grad_weight, grad_bias = finish(ids, own, beside, opposite, corner, grads, more)
    return (activations, grad_features, grad_weight, grad_bias[0])


def solution(mesh):
    placed = (
        P(("col", "row"), None),
        P(None, "feat"),
        P("feat"),
        P("row", "col", None, None, None),
        P("row", "col", None),
        P("row", "col", None),
        P("row", "col"),
        P(("row", "col"), "feat"),
    )
    return jax.shard_map(
        local,
        mesh=mesh,
        in_specs=placed,
        out_specs=(P(("row", "col"), "feat"), P(("col", "row"), None), P(None, "feat"), P("feat")),
        check_vma=False,
    )
```

```python
import functools

import jax
import jax.numpy as jnp
from jax import lax
from jax.experimental import pallas as pl
from jax.experimental.pallas import tpu as pltpu
from jax.sharding import PartitionSpec as P

F32 = jnp.float32
BF16 = jnp.bfloat16
TILE = 128
PER = 32
FORWARD = 2
BACKWARD = 4
SPARE = 1023
EARLY = 4
VMEM = pl.BlockSpec(memory_space=pltpu.VMEM)
SMEM = pl.BlockSpec(memory_space=pltpu.SMEM)
ANY = pl.BlockSpec(memory_space=pl.ANY)
PARAMS = pltpu.CompilerParams(vmem_limit_bytes=8 * 1024 * 1024)
PICK_PARAMS = pltpu.CompilerParams(vmem_limit_bytes=16 * 1024 * 1024)


def swap(values, axis, mask):
    size = lax.axis_size(axis)
    return lax.ppermute(values, axis, [(i, i ^ mask) for i in range(size)])


def swap_line(values, axis):
    second = swap(values[1], axis, 4)
    return [swap(values[0], axis, 2), second, swap(values[2], axis, 6)]


def near(values):
    return pltpu.with_memory_space_constraint(values, pltpu.VMEM)


def scalar(values):
    return pltpu.with_memory_space_constraint(values, pltpu.SMEM)


def far(values):
    return pltpu.with_memory_space_constraint(values, pltpu.HBM)


def iota(shape, dim):
    return lax.broadcasted_iota(jnp.int32, shape, dim)


def order(key, used, source, item, n_keys, length, width):
    n = key.shape[1]
    hit = ((iota((n_keys, n), 0) == key) & used).astype(F32)
    upto = (iota((n, n), 0) <= iota((n, n), 1)).astype(BF16)
    rank = jnp.dot(hit.astype(BF16), upto, preferred_element_type=F32)
    groups = jnp.floor((rank[:, n - 1 :] + (width - 1)) * (1.0 / width))
    below = (iota((n_keys, n_keys), 0) >= iota((n_keys, n_keys), 1)).astype(BF16)
    high = jnp.floor(groups * (1.0 / 128))
    lane = iota((n_keys, TILE), 1)
    parts = jnp.where(lane == 0, groups - high * 128, jnp.where(lane == 1, high, 0.0))
    ends = jnp.dot(below, parts.astype(BF16), preferred_element_type=F32)
    end = ends[:, 0:1] + ends[:, 1:2] * 128
    first = (end - groups) * width
    slot = jnp.sum(hit * (first + rank - 1.0), axis=0, keepdims=True)
    slot = jnp.where(used, slot.astype(jnp.int32), -1)
    at = (iota((length, n), 0) == slot).astype(F32).astype(BF16)
    line = iota((8, n), 0)
    values = jnp.where(line == 2, source, 1)
    values = jnp.where(line == 0, item & 255, jnp.where(line == 1, item >> 8, values))
    found = lax.dot_general(
        values.astype(F32).astype(BF16), at, (((1,), (1,)), ((), ())), preferred_element_type=F32
    ).astype(jnp.int32)
    passed = (end * width).astype(jnp.int32) <= iota((n_keys, length), 1)
    target = jnp.sum(passed.astype(F32), axis=0, keepdims=True).astype(jnp.int32)
    items = jnp.where(found[3:4] > 0, found[0:1] + found[1:2] * 256, -1)
    steps = (jnp.max(end).astype(jnp.int32) * width + PER - 1) // PER
    return items, found[2:3], target, steps, slot


def pick_kernel(n_out, count, ids, rows, columns, *refs):
    fetched, forward, steps, same_ids, slots = refs[:5]
    row_copy, column_copy, fetched_copy, forward_copy, arrived = refs[5:]
    copies = [
        pltpu.make_async_copy(rows.at[0], row_copy, arrived.at[0]),
        pltpu.make_async_copy(columns.at[0], column_copy, arrived.at[1]),
    ]
    for copy in copies:
        copy.start()
    for k in range(3):
        same_ids[k] = ids[k]
    for copy in copies:
        copy.wait()
    row, column = row_copy[...], column_copy[...]
    index = iota(row.shape, 1)
    length = forward.shape[1]
    used = (index < count[0, 0]) & (((column >> 1) & 1) == ids[0])
    source = jnp.bitwise_xor(column >> 2, ids[2]) * 2 + (column & 1)
    items, source, target, n_steps, slot = order(row, used, source, index, n_out, length, FORWARD)
    fetched_copy[...] = jnp.maximum(items, 0)
    here = jnp.where(items >= 0, iota(items.shape, 1), SPARE)
    forward_copy[...] = here + source * 1024 + target * 65536
    copies = [
        pltpu.make_async_copy(fetched_copy, fetched, arrived.at[0]),
        pltpu.make_async_copy(forward_copy, forward, arrived.at[1]),
    ]
    for copy in copies:
        copy.start()
    slots[...] = slot
    steps[0] = n_steps
    for copy in copies:
        copy.wait()


def pick(count, ids, rows, columns, n_out, n_back):
    length = rows.shape[-1] + max(n_out * (FORWARD - 1), n_back * (BACKWARD - 1)) + PER
    length = -(-length // TILE) * TILE
    listed = (1, length)
    return pl.pallas_call(
        functools.partial(pick_kernel, n_out),
        out_shape=[
            pltpu.SMEM(listed, jnp.int32),
            pltpu.SMEM(listed, jnp.int32),
            pltpu.SMEM((1,), jnp.int32),
            pltpu.SMEM((3,), jnp.int32),
            pltpu.VMEM(rows.shape[1:], jnp.int32),
        ],
        in_specs=[SMEM, SMEM, ANY, ANY],
        out_specs=[SMEM, SMEM, SMEM, SMEM, VMEM],
        scratch_shapes=[
            pltpu.VMEM(rows.shape[1:], jnp.int32),
            pltpu.VMEM(rows.shape[1:], jnp.int32),
            pltpu.VMEM(listed, jnp.int32),
            pltpu.VMEM(listed, jnp.int32),
            pltpu.SemaphoreType.DMA((2,)),
        ],
        compiler_params=PICK_PARAMS,
        name="pick_tiles",
    )(count, ids, far(rows), far(columns))


def start_fetch(tiles, fetched, held, arrived, g, carry):
    for j in range(PER):
        source = tiles.at[fetched[0, g * PER + j]]
        pltpu.make_async_copy(source, held.at[g * PER + j], arrived.at[g]).start()
    return carry


def end_fetch(tiles, held, arrived, g, carry):
    block = held.at[pl.ds(g * PER, PER)]
    pltpu.make_async_copy(tiles.at[pl.ds(0, PER)], block, arrived.at[g]).wait()
    return carry


def early_kernel(steps, fetched, tiles, early, arrived):
    count = jnp.minimum(steps[0], EARLY)
    lax.fori_loop(0, count, functools.partial(start_fetch, tiles, fetched, early, arrived), 0)
    early[early.shape[0] - 1] = jnp.zeros((TILE, TILE), BF16)
    lax.fori_loop(0, count, functools.partial(end_fetch, tiles, early, arrived), 0)


def early_tiles(steps, fetched, tiles):
    return pl.pallas_call(
        early_kernel,
        out_shape=pltpu.VMEM((EARLY * PER + 1, TILE, TILE), BF16),
        in_specs=[SMEM, SMEM, ANY],
        out_specs=VMEM,
        scratch_shapes=[pltpu.SemaphoreType.DMA((EARLY,))],
        compiler_params=PARAMS,
        name="early_tiles",
    )(scalar(steps), scalar(fetched), far(tiles))


def prepare_kernel(n_back, ids, rows, columns, slots, weight, bias, cotangent, *refs):
    backward, steps, weight_copy, bias_copy, cotangent_copy = refs[:5]
    row_copy, column_copy, backward_copy, arrived = refs[5:]
    pairs = [
        (rows.at[0], row_copy),
        (columns.at[0], column_copy),
        (weight, weight_copy),
        (bias, bias_copy),
        (cotangent, cotangent_copy),
    ]
    copies = [
        pltpu.make_async_copy(source, target, arrived.at[k])
        for k, (source, target) in enumerate(pairs)
    ]
    for copy in copies:
        copy.start()
    for copy in copies:
        copy.wait()
    row, column, slot = row_copy[...], column_copy[...], slots[...]
    length = backward.shape[1]
    place = (column >> 2) * 2 + (column & 1)
    source = jnp.bitwise_xor(row >> 2, ids[1]) * 4 + (row & 3)
    used = slot >= 0
    items, source, target, n_steps, slot = order(
        place, used, source, slot, n_back, length, BACKWARD
    )
    here = jnp.where(items >= 0, items, SPARE)
    backward_copy[...] = here + source * 1024 + target * 65536
    copy = pltpu.make_async_copy(backward_copy, backward, arrived.at[5])
    copy.start()
    steps[0] = n_steps
    copy.wait()


def prepare(ids, rows, columns, slots, length, n_back, weight, bias, cotangent):
    return pl.pallas_call(
        functools.partial(prepare_kernel, n_back),
        out_shape=[
            pltpu.SMEM((1, length), jnp.int32),
            pltpu.SMEM((1,), jnp.int32),
            pltpu.VMEM(weight.shape, weight.dtype),
            pltpu.VMEM(bias.shape, bias.dtype),
            pltpu.VMEM(cotangent.shape, cotangent.dtype),
        ],
        in_specs=[SMEM, ANY, ANY, VMEM, ANY, ANY, ANY],
        out_specs=[SMEM, SMEM, VMEM, VMEM, VMEM],
        scratch_shapes=[
            pltpu.VMEM(rows.shape[1:], jnp.int32),
            pltpu.VMEM(rows.shape[1:], jnp.int32),
            pltpu.VMEM((1, length), jnp.int32),
            pltpu.SemaphoreType.DMA((6,)),
        ],
        compiler_params=PICK_PARAMS,
        name="prepare",
    )(scalar(ids), far(rows), far(columns), near(slots), far(weight), far(bias), far(cotangent))


def join_kernel(a, b, out):
    rows = a.shape[0]
    out[0:rows] = a[...]
    out[rows : 2 * rows] = b[...]


def join(a, b):
    return pl.pallas_call(
        join_kernel,
        out_shape=pltpu.VMEM((2 * a.shape[0], a.shape[1]), a.dtype),
        in_specs=[VMEM] * 2,
        out_specs=VMEM,
        compiler_params=PARAMS,
        name="join",
    )(near(a), near(b))


def add_products(flipped, g, picked, held, source, total):
    last = held.shape[0] - 1
    width = BACKWARD if flipped else FORWARD
    places = []
    products = []
    for at in range(0, PER, width):
        codes = [picked[0, g * PER + at + j] for j in range(width)]
        places.append(codes[0] >> 16)
        mine = [held[jnp.minimum(code & 1023, last)] for code in codes]
        other = [source[(code >> 10) & 63] for code in codes]
        left, right = (other, mine) if flipped else (mine, other)
        products.append(
            jnp.dot(
                jnp.concatenate(left, 1), jnp.concatenate(right, 0), preferred_element_type=F32
            )
        )
    for place, product in zip(places, products):
        total[place] += product


def forward_kernel(steps, ids, fetched, picked, tiles, early, *refs):
    sources, (held, kept, sent, gathered, total, arrived) = refs[:-6], refs[-6:]
    count = steps[0]
    start = functools.partial(start_fetch, tiles, fetched, held, arrived)
    lax.fori_loop(EARLY, jnp.maximum(count, EARLY), start, 0)
    moved = pltpu.make_async_copy(
        early.at[pl.ds(0, EARLY * PER)], held.at[pl.ds(0, EARLY * PER)], arrived.at[0]
    )
    moved.start()
    held[held.shape[0] - 1] = jnp.zeros((TILE, TILE), BF16)
    total[...] = jnp.zeros_like(total)
    for m, source in enumerate(sources):
        gathered[4 * m : 4 * m + 4] = source[...].reshape(4, TILE, TILE)

    def early_step(g, carry):
        add_products(False, g, picked, early, gathered, total)
        return carry

    def step(g, carry):
        end_fetch(tiles, held, arrived, g, 0)
        add_products(False, g, picked, held, gathered, total)
        return carry

    lax.fori_loop(0, jnp.minimum(count, EARLY), early_step, 0)
    lax.fori_loop(EARLY, jnp.maximum(count, EARLY), step, 0)
    moved.wait()
    for k in range(kept.shape[0]):
        own = jnp.bitwise_xor(ids[1], 2 * k)
        kept[k] = total[pl.ds(own * 4, 4)]
        sent[k] = total[pl.ds(jnp.bitwise_xor(own, 1) * 4, 4)].astype(BF16)


def tiles_forward(steps, ids, fetched, picked, tiles, early, sources, n_out):
    shape = (n_out // 8, 4, TILE, TILE)
    length = -(-(tiles.shape[0] + n_out * (FORWARD - 1)) // PER) * PER
    return pl.pallas_call(
        forward_kernel,
        out_shape=[
            pltpu.VMEM((length + 1, TILE, TILE), BF16),
            pltpu.VMEM(shape, F32),
            pltpu.VMEM(shape, BF16),
        ],
        in_specs=[SMEM, SMEM, SMEM, SMEM, ANY, VMEM] + [VMEM] * len(sources),
        out_specs=[VMEM] * 3,
        scratch_shapes=[
            pltpu.VMEM((4 * len(sources), TILE, TILE), BF16),
            pltpu.VMEM((n_out + 1, TILE, TILE), F32),
            pltpu.SemaphoreType.DMA((length // PER,)),
        ],
        compiler_params=PARAMS,
        name="tiles_forward",
    )(
        scalar(steps),
        scalar(ids),
        scalar(fetched),
        scalar(picked),
        far(tiles),
        near(early),
        *[near(values) for values in sources],
    )


def write_terms(values, message, row):
    rest = jnp.concatenate([values, values], 0)
    line = iota(rest.shape, 0)
    terms = jnp.zeros(rest.shape, F32)
    for k in range(3):
        term = rest.astype(BF16).astype(F32)
        terms = jnp.where(line == k, term, terms)
        rest = rest - term
    message[row : row + 16] = terms.astype(BF16)


def read_terms(messages, row):
    terms = jnp.zeros((16, TILE), F32)
    for one in messages:
        terms = terms + one[row : row + 16].astype(F32)
    return jnp.broadcast_to(jnp.sum(terms, axis=0, keepdims=True), (8, TILE))


def backward_kernel(steps, ids, picked, held, *refs):
    messages, outs, (gathered, total) = refs[:-7], refs[-7:-2], refs[-2:]
    kept, grads, outs = outs[0], outs[1], (outs[0], *outs[2:])
    total[...] = jnp.zeros_like(total)
    rows = 4 * TILE
    for m, one in enumerate(messages):
        gathered[4 * m : 4 * m + 4] = one[0:rows].reshape(4, TILE, TILE)

    for k in range(2):
        weight = jnp.zeros((TILE // 2, TILE), F32)
        for one in messages[k::2]:
            weight = weight + one[rows : rows + TILE // 2].astype(F32)
        grads[pl.ds(jnp.bitwise_xor(ids[1] & 1, k) * (TILE // 2), TILE // 2)] = weight
    bias = read_terms(messages[0::2], rows + TILE // 2)
    grads[TILE : TILE + 8] = bias
    for out in outs[1:]:
        out[rows : rows + TILE] = grads[0:TILE].astype(BF16)
        write_terms(bias, out, rows + TILE)

    def step(g, carry):
        add_products(True, g, picked, held, gathered, total)
        return carry

    lax.fori_loop(0, steps[0], step, 0)
    for k, out in enumerate(outs):
        for z in range(2):
            block = total[pl.ds(jnp.bitwise_xor(ids[2], 2 * k + z) * 2, 2)]
            out[2 * z * TILE : 2 * (z + 1) * TILE] = block.reshape(2 * TILE, TILE).astype(out.dtype)


def tiles_backward(steps, ids, picked, held, sources, n_back):
    rows = n_back // 4 * TILE
    return pl.pallas_call(
        backward_kernel,
        out_shape=[pltpu.VMEM((rows, TILE), F32), pltpu.VMEM((TILE + 8, TILE), F32)]
        + [pltpu.VMEM((rows + TILE + 16, TILE), BF16)] * 3,
        in_specs=[SMEM, SMEM, SMEM] + [VMEM] * (1 + len(sources)),
        out_specs=[VMEM] * 5,
        scratch_shapes=[
            pltpu.VMEM((4 * len(sources), TILE, TILE), BF16),
            pltpu.VMEM((n_back + 1, TILE, TILE), F32),
        ],
        compiler_params=PARAMS,
        name="tiles_backward",
    )(scalar(steps), scalar(ids), scalar(picked), near(held), *[near(values) for values in sources])


def pair_kernel(kept, got, first, *others):
    first[...] = kept[0] + got[0].astype(F32)
    for k, other in enumerate(others):
        other[...] = (kept[k + 1] + got[k + 1].astype(F32)).astype(BF16)


def pair_sum(kept, got):
    shape = kept.shape[1:]
    n = kept.shape[0] - 1
    return pl.pallas_call(
        pair_kernel,
        out_shape=[pltpu.VMEM(shape, F32)] + [pltpu.VMEM(shape, BF16)] * n,
        in_specs=[VMEM] * 2,
        out_specs=[VMEM] * (n + 1),
        compiler_params=PARAMS,
        name="pair_sum",
    )(near(kept), near(got))


def own_kernel(first, a, b, c, total, sent):
    value = first[...] + a[...].astype(F32) + b[...].astype(F32) + c[...].astype(F32)
    total[...] = value
    sent[...] = value.astype(BF16)


def own_sum(first, others):
    return pl.pallas_call(
        own_kernel,
        out_shape=[pltpu.VMEM(first.shape, F32), pltpu.VMEM(first.shape, BF16)],
        in_specs=[VMEM] * 4,
        out_specs=[VMEM] * 2,
        compiler_params=PARAMS,
        name="own_sum",
    )(near(first), *[near(values) for values in others])


def middle_kernel(own, other, weight, bias, cotangent, activations, back, back_sent, grads):
    blocks = own.shape[0]
    rows = blocks * TILE
    sums = (own[...] + other[...].astype(F32)).astype(BF16).reshape(rows, TILE)
    preact = jnp.dot(sums, weight[...], preferred_element_type=F32) + bias[...]
    sigma = jax.nn.sigmoid(preact)
    activations[...] = (preact * sigma).astype(BF16)
    grad = cotangent[...].astype(F32) * (sigma * (1.0 + preact * (1.0 - sigma)))
    grad_pre = grad.astype(BF16)
    grads[0:TILE] = lax.dot_general(
        sums, grad_pre, (((0,), (0,)), ((), ())), preferred_element_type=F32
    )
    total = jnp.sum(grad_pre.astype(F32), axis=0, keepdims=True)
    grads[TILE : TILE + 8] = jnp.broadcast_to(total, (8, TILE))
    for b in range(blocks):
        value = lax.dot_general(
            weight[...],
            grad_pre[b * TILE : (b + 1) * TILE],
            (((1,), (1,)), ((), ())),
            preferred_element_type=F32,
        )
        back[b] = value
        back_sent[b] = value.astype(BF16)


def middle(own, other, weight, bias, cotangent):
    return pl.pallas_call(
        middle_kernel,
        out_shape=[
            jax.ShapeDtypeStruct(cotangent.shape, BF16),
            pltpu.VMEM(own.shape, F32),
            pltpu.VMEM(own.shape, BF16),
            pltpu.VMEM((TILE + 8, TILE), F32),
        ],
        in_specs=[VMEM] * 5,
        out_specs=[VMEM] * 4,
        compiler_params=PARAMS,
        name="middle",
    )(near(own), near(other), near(weight), near(bias), near(cotangent))


def message_kernel(ids, back, other, grads, more, message):
    rows = back.shape[0] * TILE
    value = back[...] + other[...].astype(F32)
    message[0:rows] = value.astype(BF16).reshape(rows, TILE)
    half = pl.ds((ids[1] & 1) * (TILE // 2), TILE // 2)
    message[rows : rows + TILE // 2] = (grads[half] + more[half]).astype(BF16)
    write_terms(grads[TILE : TILE + 8] + more[TILE : TILE + 8], message, rows + TILE // 2)


def message(ids, back, other, grads, more):
    rows = back.shape[0] * TILE + TILE // 2 + 16
    return pl.pallas_call(
        message_kernel,
        out_shape=pltpu.VMEM((rows, TILE), BF16),
        in_specs=[SMEM] + [VMEM] * 4,
        out_specs=VMEM,
        compiler_params=PARAMS,
        name="message",
    )(scalar(ids), near(back), near(other), near(grads), near(more))


def line_kernel(kept, grads, a, b, c, own, own_grads, own_sent, other_sent, other_message):
    rows = own.shape[0]
    value = kept[...]
    weight = grads[0:TILE]
    for one in (a, b, c):
        value = value + one[0 : 2 * rows].astype(F32)
        weight = weight + one[2 * rows : 2 * rows + TILE].astype(F32)
    bias = grads[TILE : TILE + 8] + read_terms((a, b, c), 2 * rows + TILE)
    own[...] = value[:rows]
    own_sent[...] = value[:rows].astype(BF16)
    other = value[rows:].astype(BF16)
    other_sent[...] = other
    own_grads[0:TILE] = weight
    own_grads[TILE : TILE + 8] = bias
    other_message[0:rows] = other
    other_message[rows : rows + TILE] = weight.astype(BF16)
    write_terms(bias, other_message, rows + TILE)


def line_sum(kept, grads, messages):
    rows = kept.shape[0] // 2
    return pl.pallas_call(
        line_kernel,
        out_shape=[
            pltpu.VMEM((rows, TILE), F32),
            pltpu.VMEM(grads.shape, F32),
            pltpu.VMEM((rows, TILE), BF16),
            pltpu.VMEM((rows, TILE), BF16),
            pltpu.VMEM((rows + TILE + 16, TILE), BF16),
        ],
        in_specs=[VMEM] * 5,
        out_specs=[VMEM] * 5,
        compiler_params=PARAMS,
        name="line_sum",
    )(near(kept), near(grads), *[near(one) for one in messages])


def finish_kernel(ids, own, grads, beside, opposite, corner, features, weight, bias):
    rows = own.shape[0]
    for b in range(rows // TILE):
        block = pl.ds(b * TILE, TILE)
        mine = own[block] + beside[block].astype(F32)
        other = opposite[block].astype(F32) + corner[block].astype(F32)
        features[pl.ds(ids[0] * rows + b * TILE, TILE)] = mine.T
        features[pl.ds((1 - ids[0]) * rows + b * TILE, TILE)] = other.T
    weight[...] = grads[0:TILE] + beside[rows : rows + TILE].astype(F32)
    bias[...] = (grads[TILE : TILE + 8] + read_terms((beside,), rows + TILE))[0:1]


def finish(ids, own, grads, beside, opposite, corner):
    return pl.pallas_call(
        finish_kernel,
        out_shape=[
            jax.ShapeDtypeStruct((2 * own.shape[0], TILE), F32),
            jax.ShapeDtypeStruct((TILE, TILE), F32),
            jax.ShapeDtypeStruct((1, TILE), F32),
        ],
        in_specs=[SMEM] + [VMEM] * 5,
        out_specs=[VMEM] * 3,
        compiler_params=PARAMS,
        name="finish",
    )(scalar(ids), near(own), near(grads), near(beside), near(opposite), near(corner))


def local(
    features, weight, hidden_bias, adjacency_tiles, tile_rows, tile_columns, tile_count, cotangent
):
    tiles = adjacency_tiles[0, 0]
    n_row, n_col = lax.axis_size("row"), lax.axis_size("col")
    own_rows, fin = features.shape
    blocks = own_rows // TILE
    n_out, n_back = blocks * n_col, blocks // 2 * n_row
    half = lax.axis_index("feat")
    ids = jnp.stack([half, lax.axis_index("col"), lax.axis_index("row")]).astype(jnp.int32)

    mine = lax.dynamic_slice_in_dim(features, half * (own_rows // 2), own_rows // 2, 0)
    lists = pick(tile_count, ids, tile_rows, tile_columns, n_out, n_back)
    beside, lists = lax.optimization_barrier((swap(mine, "row", 1), lists))
    fetched, forward, steps, ids, slots = lists
    pair = join(mine, beside)
    sources = [swap(pair, "row", mask) for mask in range(2, n_row, 2)]
    early = early_tiles(steps, fetched, tiles)
    early, sources = lax.optimization_barrier((early, sources))

    held, kept, sent = tiles_forward(steps, ids, fetched, forward, tiles, early, [pair, *sources], n_out)
    first, *others = pair_sum(kept, swap(sent, "col", 1))
    others = swap_line(others, "col")
    own, sent = own_sum(first, others)
    sent, slots = lax.optimization_barrier((sent, slots))
    ready = prepare(
        ids, tile_rows, tile_columns, slots, forward.shape[1], n_back, weight, hidden_bias[None], cotangent
    )
    other, ready = lax.optimization_barrier((swap(sent, "feat", 1), ready))
    backward, steps, weight, bias, cotangent = ready
    activations, back, back_sent, grads = middle(own, other, weight, bias, cotangent)

    back_other, more = lax.optimization_barrier((swap(back_sent, "feat", 1), swap(grads, "col", 1)))
    mine = message(ids, back, back_other, grads, more)
    across = [swap(mine, "col", mask) for mask in (2, 6, 4)]
    beside = swap(mine, "col", 1)
    across = lax.optimization_barrier(across)
    corners = [swap(values, "col", 1) for values in across]
    sources = [mine, beside, across[0], corners[0], across[2], corners[2], across[1], corners[1]]
    kept, grads, *others = tiles_backward(steps, ids, backward, held, sources, n_back)

    others = swap_line(others, "row")
    own, grads, own_sent, other_sent, other_message = line_sum(kept, grads, others)
    opposite = swap(own_sent, "feat", 1)
    corner = swap(other_sent, ("row", "feat"), 3)
    beside = swap(other_message, "row", 1)
    grad_features, grad_weight, grad_bias = finish(ids, own, grads, beside, opposite, corner)
    return (activations, grad_features, grad_weight, grad_bias[0])


def solution(mesh):
    placed = (
        P(("col", "row"), None),
        P(None, "feat"),
        P("feat"),
        P("row", "col", None, None, None),
        P("row", "col", None),
        P("row", "col", None),
        P("row", "col"),
        P(("row", "col"), "feat"),
    )
    return jax.shard_map(
        local,
        mesh=mesh,
        in_specs=placed,
        out_specs=(P(("row", "col"), "feat"), P(("col", "row"), None), P(None, "feat"), P("feat")),
        check_vma=False,
    )
```

```python
import functools

import jax
import jax.numpy as jnp
from jax import lax
from jax.experimental import pallas as pl
from jax.experimental.pallas import tpu as pltpu
from jax.sharding import PartitionSpec as P

F32 = jnp.float32
BF16 = jnp.bfloat16
TILE = 128
PER = 32
MERGED = 5
FORWARD = 2
BACKWARD = 4
SPARE = 1023
EARLY = 5
VMEM = pl.BlockSpec(memory_space=pltpu.VMEM)
SMEM = pl.BlockSpec(memory_space=pltpu.SMEM)
ANY = pl.BlockSpec(memory_space=pl.ANY)
PARAMS = pltpu.CompilerParams(vmem_limit_bytes=8 * 1024 * 1024)
PICK_PARAMS = pltpu.CompilerParams(vmem_limit_bytes=16 * 1024 * 1024)


def swap(values, axis, mask):
    size = lax.axis_size(axis)
    return lax.ppermute(values, axis, [(i, i ^ mask) for i in range(size)])


def swap_line(values, axis):
    second = swap(values[1], axis, 4)
    return [swap(values[0], axis, 2), second, swap(values[2], axis, 6)]


def near(values):
    return pltpu.with_memory_space_constraint(values, pltpu.VMEM)


def scalar(values):
    return pltpu.with_memory_space_constraint(values, pltpu.SMEM)


def far(values):
    return pltpu.with_memory_space_constraint(values, pltpu.HBM)


def iota(shape, dim):
    return lax.broadcasted_iota(jnp.int32, shape, dim)


def order(key, used, source, item, n_keys, length, width):
    n = key.shape[1]
    hit = ((iota((n_keys, n), 0) == key) & used).astype(F32)
    upto = (iota((n, n), 0) <= iota((n, n), 1)).astype(BF16)
    rank = jnp.dot(hit.astype(BF16), upto, preferred_element_type=F32)
    groups = jnp.floor((rank[:, n - 1 :] + (width - 1)) * (1.0 / width))
    below = (iota((n_keys, n_keys), 0) >= iota((n_keys, n_keys), 1)).astype(BF16)
    high = jnp.floor(groups * (1.0 / 128))
    lane = iota((n_keys, TILE), 1)
    parts = jnp.where(lane == 0, groups - high * 128, jnp.where(lane == 1, high, 0.0))
    ends = jnp.dot(below, parts.astype(BF16), preferred_element_type=F32)
    end = ends[:, 0:1] + ends[:, 1:2] * 128
    first = (end - groups) * width
    slot = jnp.sum(hit * (first + rank - 1.0), axis=0, keepdims=True)
    slot = jnp.where(used, slot.astype(jnp.int32), -1)
    at = (iota((length, n), 0) == slot).astype(F32).astype(BF16)
    line = iota((8, n), 0)
    values = jnp.where(line == 2, source, 1)
    values = jnp.where(line == 0, item & 255, jnp.where(line == 1, item >> 8, values))
    found = lax.dot_general(
        values.astype(F32).astype(BF16), at, (((1,), (1,)), ((), ())), preferred_element_type=F32
    ).astype(jnp.int32)
    passed = (end * width).astype(jnp.int32) <= iota((n_keys, length), 1)
    target = jnp.sum(passed.astype(F32), axis=0, keepdims=True).astype(jnp.int32)
    items = jnp.where(found[3:4] > 0, found[0:1] + found[1:2] * 256, -1)
    steps = (jnp.max(end).astype(jnp.int32) * width + PER - 1) // PER
    return items, found[2:3], target, steps, slot


def pick_kernel(n_out, count, ids, rows, columns, *refs):
    fetched, forward, steps, same_ids, slots = refs[:5]
    row_copy, column_copy, fetched_copy, forward_copy, arrived = refs[5:]
    copies = [
        pltpu.make_async_copy(rows.at[0], row_copy, arrived.at[0]),
        pltpu.make_async_copy(columns.at[0], column_copy, arrived.at[1]),
    ]
    for copy in copies:
        copy.start()
    for k in range(3):
        same_ids[k] = ids[k]
    for copy in copies:
        copy.wait()
    row, column = row_copy[...], column_copy[...]
    index = iota(row.shape, 1)
    length = forward.shape[1]
    used = (index < count[0, 0]) & (((column >> 1) & 1) == ids[0])
    source = jnp.bitwise_xor(column >> 2, ids[2]) * 2 + (column & 1)
    items, source, target, n_steps, slot = order(row, used, source, index, n_out, length, FORWARD)
    fetched_copy[...] = jnp.maximum(items, 0)
    here = jnp.where(items >= 0, iota(items.shape, 1), SPARE)
    forward_copy[...] = here + source * 1024 + target * 65536
    copies = [
        pltpu.make_async_copy(fetched_copy, fetched, arrived.at[0]),
        pltpu.make_async_copy(forward_copy, forward, arrived.at[1]),
    ]
    for copy in copies:
        copy.start()
    slots[...] = slot
    steps[0] = n_steps
    for copy in copies:
        copy.wait()


def pick(count, ids, rows, columns, n_out, n_back):
    length = rows.shape[-1] + max(n_out * (FORWARD - 1), n_back * (BACKWARD - 1)) + PER
    length = -(-length // TILE) * TILE
    listed = (1, length)
    return pl.pallas_call(
        functools.partial(pick_kernel, n_out),
        out_shape=[
            pltpu.SMEM(listed, jnp.int32),
            pltpu.SMEM(listed, jnp.int32),
            pltpu.SMEM((1,), jnp.int32),
            pltpu.SMEM((3,), jnp.int32),
            pltpu.VMEM(rows.shape[1:], jnp.int32),
        ],
        in_specs=[SMEM, SMEM, ANY, ANY],
        out_specs=[SMEM, SMEM, SMEM, SMEM, VMEM],
        scratch_shapes=[
            pltpu.VMEM(rows.shape[1:], jnp.int32),
            pltpu.VMEM(rows.shape[1:], jnp.int32),
            pltpu.VMEM(listed, jnp.int32),
            pltpu.VMEM(listed, jnp.int32),
            pltpu.SemaphoreType.DMA((2,)),
        ],
        compiler_params=PICK_PARAMS,
        name="pick_tiles",
    )(count, ids, far(rows), far(columns))


def start_fetch(tiles, fetched, held, arrived, g, carry):
    for j in range(PER):
        source = tiles.at[fetched[0, g * PER + j]]
        pltpu.make_async_copy(source, held.at[g * PER + j], arrived.at[g]).start()
    return carry


def end_fetch(tiles, held, arrived, g, carry):
    block = held.at[pl.ds(g * PER, PER)]
    pltpu.make_async_copy(tiles.at[pl.ds(0, PER)], block, arrived.at[g]).wait()
    return carry


def early_kernel(steps, fetched, tiles, early, arrived):
    count = jnp.minimum(steps[0], EARLY)
    lax.fori_loop(0, count, functools.partial(start_fetch, tiles, fetched, early, arrived), 0)
    early[early.shape[0] - 1] = jnp.zeros((TILE, TILE), BF16)
    lax.fori_loop(0, count, functools.partial(end_fetch, tiles, early, arrived), 0)


def early_tiles(steps, fetched, tiles):
    return pl.pallas_call(
        early_kernel,
        out_shape=pltpu.VMEM((EARLY * PER + 1, TILE, TILE), BF16),
        in_specs=[SMEM, SMEM, ANY],
        out_specs=VMEM,
        scratch_shapes=[pltpu.SemaphoreType.DMA((EARLY,))],
        compiler_params=PARAMS,
        name="early_tiles",
    )(scalar(steps), scalar(fetched), far(tiles))


def prepare_kernel(n_back, ids, rows, columns, slots, weight, bias, cotangent, *refs):
    backward, steps, weight_copy, bias_copy, cotangent_copy = refs[:5]
    row_copy, column_copy, backward_copy, arrived = refs[5:]
    pairs = [
        (rows.at[0], row_copy),
        (columns.at[0], column_copy),
        (weight, weight_copy),
        (bias, bias_copy),
        (cotangent, cotangent_copy),
    ]
    copies = [
        pltpu.make_async_copy(source, target, arrived.at[k])
        for k, (source, target) in enumerate(pairs)
    ]
    for copy in copies:
        copy.start()
    for copy in copies:
        copy.wait()
    row, column, slot = row_copy[...], column_copy[...], slots[...]
    length = backward.shape[1]
    place = (column >> 2) * 2 + (column & 1)
    source = jnp.bitwise_xor(row >> 2, ids[1]) * 4 + (row & 3)
    used = slot >= 0
    items, source, target, n_steps, slot = order(
        place, used, source, slot, n_back, length, BACKWARD
    )
    here = jnp.where(items >= 0, items, SPARE)
    backward_copy[...] = here + source * 1024 + target * 65536
    copy = pltpu.make_async_copy(backward_copy, backward, arrived.at[5])
    copy.start()
    steps[0] = n_steps
    copy.wait()


def prepare(ids, rows, columns, slots, length, n_back, weight, bias, cotangent):
    return pl.pallas_call(
        functools.partial(prepare_kernel, n_back),
        out_shape=[
            pltpu.SMEM((1, length), jnp.int32),
            pltpu.SMEM((1,), jnp.int32),
            pltpu.VMEM(weight.shape, weight.dtype),
            pltpu.VMEM(bias.shape, bias.dtype),
            pltpu.VMEM(cotangent.shape, cotangent.dtype),
        ],
        in_specs=[SMEM, ANY, ANY, VMEM, ANY, ANY, ANY],
        out_specs=[SMEM, SMEM, VMEM, VMEM, VMEM],
        scratch_shapes=[
            pltpu.VMEM(rows.shape[1:], jnp.int32),
            pltpu.VMEM(rows.shape[1:], jnp.int32),
            pltpu.VMEM((1, length), jnp.int32),
            pltpu.SemaphoreType.DMA((6,)),
        ],
        compiler_params=PICK_PARAMS,
        name="prepare",
    )(scalar(ids), far(rows), far(columns), near(slots), far(weight), far(bias), far(cotangent))


def join_kernel(a, b, out):
    rows = a.shape[0]
    out[0:rows] = a[...]
    out[rows : 2 * rows] = b[...]


def join(a, b):
    return pl.pallas_call(
        join_kernel,
        out_shape=pltpu.VMEM((2 * a.shape[0], a.shape[1]), a.dtype),
        in_specs=[VMEM] * 2,
        out_specs=VMEM,
        compiler_params=PARAMS,
        name="join",
    )(near(a), near(b))


def add_products(flipped, first, picked, held, source, total):
    last = held.shape[0] - 1
    width = BACKWARD if flipped else FORWARD
    places = []
    products = []
    for at in range(0, PER, width):
        codes = [picked[0, first + at + j] for j in range(width)]
        places.append(codes[0] >> 16)
        mine = [held[jnp.minimum(code & 1023, last)] for code in codes]
        other = [source[(code >> 10) & 63] for code in codes]
        left, right = (other, mine) if flipped else (mine, other)
        products.append(
            jnp.dot(
                jnp.concatenate(left, 1), jnp.concatenate(right, 0), preferred_element_type=F32
            )
        )
    for place, product in zip(places, products):
        total[place] += product


def run_steps(first, last, step):
    passes = (last - first) // MERGED

    def merged(k, carry):
        for j in range(MERGED):
            step(first + k * MERGED + j)
        return carry

    def single(g, carry):
        step(g)
        return carry

    lax.fori_loop(0, passes, merged, 0)
    lax.fori_loop(first + passes * MERGED, last, single, 0)


def forward_kernel(steps, ids, fetched, picked, tiles, early, *refs):
    sources, (held, kept, sent, gathered, total, arrived) = refs[:-6], refs[-6:]
    count = steps[0]
    start = functools.partial(start_fetch, tiles, fetched, held, arrived)
    lax.fori_loop(EARLY, jnp.maximum(count, EARLY), start, 0)
    moved = pltpu.make_async_copy(
        early.at[pl.ds(0, EARLY * PER)], held.at[pl.ds(0, EARLY * PER)], arrived.at[0]
    )
    moved.start()
    held[held.shape[0] - 1] = jnp.zeros((TILE, TILE), BF16)
    total[...] = jnp.zeros_like(total)
    for m, source in enumerate(sources):
        gathered[4 * m : 4 * m + 4] = source[...].reshape(4, TILE, TILE)

    def early_step(g):
        add_products(False, g * PER, picked, early, gathered, total)

    def step(g):
        end_fetch(tiles, held, arrived, g, 0)
        add_products(False, g * PER, picked, held, gathered, total)

    run_steps(0, jnp.minimum(count, EARLY), early_step)
    run_steps(EARLY, jnp.maximum(count, EARLY), step)
    moved.wait()
    for k in range(kept.shape[0]):
        own = jnp.bitwise_xor(ids[1], 2 * k)
        kept[k] = total[pl.ds(own * 4, 4)]
        sent[k] = total[pl.ds(jnp.bitwise_xor(own, 1) * 4, 4)].astype(BF16)


def tiles_forward(steps, ids, fetched, picked, tiles, early, sources, n_out):
    shape = (n_out // 8, 4, TILE, TILE)
    length = -(-(tiles.shape[0] + n_out * (FORWARD - 1)) // PER) * PER
    return pl.pallas_call(
        forward_kernel,
        out_shape=[
            pltpu.VMEM((length + 1, TILE, TILE), BF16),
            pltpu.VMEM(shape, F32),
            pltpu.VMEM(shape, BF16),
        ],
        in_specs=[SMEM, SMEM, SMEM, SMEM, ANY, VMEM] + [VMEM] * len(sources),
        out_specs=[VMEM] * 3,
        scratch_shapes=[
            pltpu.VMEM((4 * len(sources), TILE, TILE), BF16),
            pltpu.VMEM((n_out + 1, TILE, TILE), F32),
            pltpu.SemaphoreType.DMA((length // PER,)),
        ],
        compiler_params=PARAMS,
        name="tiles_forward",
    )(
        scalar(steps),
        scalar(ids),
        scalar(fetched),
        scalar(picked),
        far(tiles),
        near(early),
        *[near(values) for values in sources],
    )


def write_terms(values, message, row):
    rest = jnp.concatenate([values, values], 0)
    line = iota(rest.shape, 0)
    terms = jnp.zeros(rest.shape, F32)
    for k in range(3):
        term = rest.astype(BF16).astype(F32)
        terms = jnp.where(line == k, term, terms)
        rest = rest - term
    message[row : row + 16] = terms.astype(BF16)


def read_terms(messages, row):
    terms = jnp.zeros((16, TILE), F32)
    for one in messages:
        terms = terms + one[row : row + 16].astype(F32)
    return jnp.broadcast_to(jnp.sum(terms, axis=0, keepdims=True), (8, TILE))


def backward_kernel(steps, ids, picked, held, *refs):
    messages, outs, (gathered, total) = refs[:-7], refs[-7:-2], refs[-2:]
    kept, grads, outs = outs[0], outs[1], (outs[0], *outs[2:])
    total[...] = jnp.zeros_like(total)
    rows = 4 * TILE
    for m, one in enumerate(messages):
        gathered[4 * m : 4 * m + 4] = one[0:rows].reshape(4, TILE, TILE)

    for k in range(2):
        weight = jnp.zeros((TILE // 2, TILE), F32)
        for one in messages[k::2]:
            weight = weight + one[rows : rows + TILE // 2].astype(F32)
        grads[pl.ds(jnp.bitwise_xor(ids[1] & 1, k) * (TILE // 2), TILE // 2)] = weight
    bias = read_terms(messages[0::2], rows + TILE // 2)
    grads[TILE : TILE + 8] = bias
    for out in outs[1:]:
        out[rows : rows + TILE] = grads[0:TILE].astype(BF16)
        write_terms(bias, out, rows + TILE)

    run_steps(0, steps[0], lambda g: add_products(True, g * PER, picked, held, gathered, total))
    for k, out in enumerate(outs):
        for z in range(2):
            block = total[pl.ds(jnp.bitwise_xor(ids[2], 2 * k + z) * 2, 2)]
            out[2 * z * TILE : 2 * (z + 1) * TILE] = block.reshape(2 * TILE, TILE).astype(out.dtype)


def tiles_backward(steps, ids, picked, held, sources, n_back):
    rows = n_back // 4 * TILE
    return pl.pallas_call(
        backward_kernel,
        out_shape=[pltpu.VMEM((rows, TILE), F32), pltpu.VMEM((TILE + 8, TILE), F32)]
        + [pltpu.VMEM((rows + TILE + 16, TILE), BF16)] * 3,
        in_specs=[SMEM, SMEM, SMEM] + [VMEM] * (1 + len(sources)),
        out_specs=[VMEM] * 5,
        scratch_shapes=[
            pltpu.VMEM((4 * len(sources), TILE, TILE), BF16),
            pltpu.VMEM((n_back + 1, TILE, TILE), F32),
        ],
        compiler_params=PARAMS,
        name="tiles_backward",
    )(scalar(steps), scalar(ids), scalar(picked), near(held), *[near(values) for values in sources])


def pair_kernel(kept, got, first, *others):
    first[...] = kept[0] + got[0].astype(F32)
    for k, other in enumerate(others):
        other[...] = (kept[k + 1] + got[k + 1].astype(F32)).astype(BF16)


def pair_sum(kept, got):
    shape = kept.shape[1:]
    n = kept.shape[0] - 1
    return pl.pallas_call(
        pair_kernel,
        out_shape=[pltpu.VMEM(shape, F32)] + [pltpu.VMEM(shape, BF16)] * n,
        in_specs=[VMEM] * 2,
        out_specs=[VMEM] * (n + 1),
        compiler_params=PARAMS,
        name="pair_sum",
    )(near(kept), near(got))


def own_kernel(first, a, b, c, total, sent):
    value = first[...] + a[...].astype(F32) + b[...].astype(F32) + c[...].astype(F32)
    total[...] = value
    sent[...] = value.astype(BF16)


def own_sum(first, others):
    return pl.pallas_call(
        own_kernel,
        out_shape=[pltpu.VMEM(first.shape, F32), pltpu.VMEM(first.shape, BF16)],
        in_specs=[VMEM] * 4,
        out_specs=[VMEM] * 2,
        compiler_params=PARAMS,
        name="own_sum",
    )(near(first), *[near(values) for values in others])


def middle_kernel(own, other, weight, bias, cotangent, activations, back, back_sent, grads):
    blocks = own.shape[0]
    rows = blocks * TILE
    sums = (own[...] + other[...].astype(F32)).astype(BF16).reshape(rows, TILE)
    preact = jnp.dot(sums, weight[...], preferred_element_type=F32) + bias[...]
    sigma = jax.nn.sigmoid(preact)
    activations[...] = (preact * sigma).astype(BF16)
    grad = cotangent[...].astype(F32) * (sigma * (1.0 + preact * (1.0 - sigma)))
    grad_pre = grad.astype(BF16)
    grads[0:TILE] = lax.dot_general(
        sums, grad_pre, (((0,), (0,)), ((), ())), preferred_element_type=F32
    )
    total = jnp.sum(grad_pre.astype(F32), axis=0, keepdims=True)
    grads[TILE : TILE + 8] = jnp.broadcast_to(total, (8, TILE))
    for b in range(blocks):
        value = lax.dot_general(
            weight[...],
            grad_pre[b * TILE : (b + 1) * TILE],
            (((1,), (1,)), ((), ())),
            preferred_element_type=F32,
        )
        back[b] = value
        back_sent[b] = value.astype(BF16)


def middle(own, other, weight, bias, cotangent):
    return pl.pallas_call(
        middle_kernel,
        out_shape=[
            jax.ShapeDtypeStruct(cotangent.shape, BF16),
            pltpu.VMEM(own.shape, F32),
            pltpu.VMEM(own.shape, BF16),
            pltpu.VMEM((TILE + 8, TILE), F32),
        ],
        in_specs=[VMEM] * 5,
        out_specs=[VMEM] * 4,
        compiler_params=PARAMS,
        name="middle",
    )(near(own), near(other), near(weight), near(bias), near(cotangent))


def message_kernel(ids, back, other, grads, more, message):
    rows = back.shape[0] * TILE
    value = back[...] + other[...].astype(F32)
    message[0:rows] = value.astype(BF16).reshape(rows, TILE)
    half = pl.ds((ids[1] & 1) * (TILE // 2), TILE // 2)
    message[rows : rows + TILE // 2] = (grads[half] + more[half]).astype(BF16)
    write_terms(grads[TILE : TILE + 8] + more[TILE : TILE + 8], message, rows + TILE // 2)


def message(ids, back, other, grads, more):
    rows = back.shape[0] * TILE + TILE // 2 + 16
    return pl.pallas_call(
        message_kernel,
        out_shape=pltpu.VMEM((rows, TILE), BF16),
        in_specs=[SMEM] + [VMEM] * 4,
        out_specs=VMEM,
        compiler_params=PARAMS,
        name="message",
    )(scalar(ids), near(back), near(other), near(grads), near(more))


def line_kernel(kept, grads, a, b, c, own, own_grads, own_sent, other_sent, other_message):
    rows = own.shape[0]
    value = kept[...]
    weight = grads[0:TILE]
    for one in (a, b, c):
        value = value + one[0 : 2 * rows].astype(F32)
        weight = weight + one[2 * rows : 2 * rows + TILE].astype(F32)
    bias = grads[TILE : TILE + 8] + read_terms((a, b, c), 2 * rows + TILE)
    own[...] = value[:rows]
    own_sent[...] = value[:rows].astype(BF16)
    other = value[rows:].astype(BF16)
    other_sent[...] = other
    own_grads[0:TILE] = weight
    own_grads[TILE : TILE + 8] = bias
    other_message[0:rows] = other
    other_message[rows : rows + TILE] = weight.astype(BF16)
    write_terms(bias, other_message, rows + TILE)


def line_sum(kept, grads, messages):
    rows = kept.shape[0] // 2
    return pl.pallas_call(
        line_kernel,
        out_shape=[
            pltpu.VMEM((rows, TILE), F32),
            pltpu.VMEM(grads.shape, F32),
            pltpu.VMEM((rows, TILE), BF16),
            pltpu.VMEM((rows, TILE), BF16),
            pltpu.VMEM((rows + TILE + 16, TILE), BF16),
        ],
        in_specs=[VMEM] * 5,
        out_specs=[VMEM] * 5,
        compiler_params=PARAMS,
        name="line_sum",
    )(near(kept), near(grads), *[near(one) for one in messages])


def finish_kernel(ids, own, grads, beside, opposite, corner, features, weight, bias):
    rows = own.shape[0]
    for b in range(rows // TILE):
        block = pl.ds(b * TILE, TILE)
        mine = own[block] + beside[block].astype(F32)
        other = opposite[block].astype(F32) + corner[block].astype(F32)
        features[pl.ds(ids[0] * rows + b * TILE, TILE)] = mine.T
        features[pl.ds((1 - ids[0]) * rows + b * TILE, TILE)] = other.T
    weight[...] = grads[0:TILE] + beside[rows : rows + TILE].astype(F32)
    bias[...] = (grads[TILE : TILE + 8] + read_terms((beside,), rows + TILE))[0:1]


def finish(ids, own, grads, beside, opposite, corner):
    return pl.pallas_call(
        finish_kernel,
        out_shape=[
            jax.ShapeDtypeStruct((2 * own.shape[0], TILE), F32),
            jax.ShapeDtypeStruct((TILE, TILE), F32),
            jax.ShapeDtypeStruct((1, TILE), F32),
        ],
        in_specs=[SMEM] + [VMEM] * 5,
        out_specs=[VMEM] * 3,
        compiler_params=PARAMS,
        name="finish",
    )(scalar(ids), near(own), near(grads), near(beside), near(opposite), near(corner))


def local(
    features, weight, hidden_bias, adjacency_tiles, tile_rows, tile_columns, tile_count, cotangent
):
    tiles = adjacency_tiles[0, 0]
    n_row, n_col = lax.axis_size("row"), lax.axis_size("col")
    own_rows, fin = features.shape
    blocks = own_rows // TILE
    n_out, n_back = blocks * n_col, blocks // 2 * n_row
    half = lax.axis_index("feat")
    ids = jnp.stack([half, lax.axis_index("col"), lax.axis_index("row")]).astype(jnp.int32)

    mine = lax.dynamic_slice_in_dim(features, half * (own_rows // 2), own_rows // 2, 0)
    lists = pick(tile_count, ids, tile_rows, tile_columns, n_out, n_back)
    beside, lists = lax.optimization_barrier((swap(mine, "row", 1), lists))
    fetched, forward, steps, ids, slots = lists
    pair = join(mine, beside)
    sources = [swap(pair, "row", mask) for mask in range(2, n_row, 2)]
    early = early_tiles(steps, fetched, tiles)
    early, sources = lax.optimization_barrier((early, sources))

    held, kept, sent = tiles_forward(steps, ids, fetched, forward, tiles, early, [pair, *sources], n_out)
    first, *others = pair_sum(kept, swap(sent, "col", 1))
    others = swap_line(others, "col")
    own, sent = own_sum(first, others)
    sent, slots = lax.optimization_barrier((sent, slots))
    ready = prepare(
        ids, tile_rows, tile_columns, slots, forward.shape[1], n_back, weight, hidden_bias[None], cotangent
    )
    other, ready = lax.optimization_barrier((swap(sent, "feat", 1), ready))
    backward, steps, weight, bias, cotangent = ready
    activations, back, back_sent, grads = middle(own, other, weight, bias, cotangent)

    back_other, more = lax.optimization_barrier((swap(back_sent, "feat", 1), swap(grads, "col", 1)))
    mine = message(ids, back, back_other, grads, more)
    across = [swap(mine, "col", mask) for mask in (2, 6, 4)]
    beside = swap(mine, "col", 1)
    across = lax.optimization_barrier(across)
    corners = [swap(values, "col", 1) for values in across]
    sources = [mine, beside, across[0], corners[0], across[2], corners[2], across[1], corners[1]]
    kept, grads, *others = tiles_backward(steps, ids, backward, held, sources, n_back)

    others = swap_line(others, "row")
    own, grads, own_sent, other_sent, other_message = line_sum(kept, grads, others)
    opposite = swap(own_sent, "feat", 1)
    corner = swap(other_sent, ("row", "feat"), 3)
    beside = swap(other_message, "row", 1)
    grad_features, grad_weight, grad_bias = finish(ids, own, grads, beside, opposite, corner)
    return (activations, grad_features, grad_weight, grad_bias[0])


def solution(mesh):
    placed = (
        P(("col", "row"), None),
        P(None, "feat"),
        P("feat"),
        P("row", "col", None, None, None),
        P("row", "col", None),
        P("row", "col", None),
        P("row", "col"),
        P(("row", "col"), "feat"),
    )
    return jax.shard_map(
        local,
        mesh=mesh,
        in_specs=placed,
        out_specs=(P(("row", "col"), "feat"), P(("col", "row"), None), P(None, "feat"), P("feat")),
        check_vma=False,
    )
```

```python
import functools

import jax
import jax.numpy as jnp
from jax import lax
from jax.experimental import pallas as pl
from jax.experimental.pallas import tpu as pltpu
from jax.sharding import PartitionSpec as P

F32 = jnp.float32
BF16 = jnp.bfloat16
TILE = 128
PER = 32
MERGED = 5
FORWARD = 2
BACKWARD = 4
SPARE = 1023
EARLY = 5
VMEM = pl.BlockSpec(memory_space=pltpu.VMEM)
SMEM = pl.BlockSpec(memory_space=pltpu.SMEM)
ANY = pl.BlockSpec(memory_space=pl.ANY)
PARAMS = pltpu.CompilerParams(vmem_limit_bytes=8 * 1024 * 1024)
PICK_PARAMS = pltpu.CompilerParams(vmem_limit_bytes=16 * 1024 * 1024)


def swap(values, axis, mask):
    size = lax.axis_size(axis)
    return lax.ppermute(values, axis, [(i, i ^ mask) for i in range(size)])


def swap_line(values, axis):
    return [swap(one, axis, mask) for one, mask in zip(values, (4, 2, 6))]


def near(values):
    return pltpu.with_memory_space_constraint(values, pltpu.VMEM)


def scalar(values):
    return pltpu.with_memory_space_constraint(values, pltpu.SMEM)


def far(values):
    return pltpu.with_memory_space_constraint(values, pltpu.HBM)


def iota(shape, dim):
    return lax.broadcasted_iota(jnp.int32, shape, dim)


def order(key, used, source, item, n_keys, length, width):
    n = key.shape[1]
    hit = ((iota((n_keys, n), 0) == key) & used).astype(F32)
    upto = (iota((n, n), 0) <= iota((n, n), 1)).astype(BF16)
    rank = jnp.dot(hit.astype(BF16), upto, preferred_element_type=F32)
    groups = jnp.floor((rank[:, n - 1 :] + (width - 1)) * (1.0 / width))
    below = (iota((n_keys, n_keys), 0) >= iota((n_keys, n_keys), 1)).astype(BF16)
    high = jnp.floor(groups * (1.0 / 128))
    lane = iota((n_keys, TILE), 1)
    parts = jnp.where(lane == 0, groups - high * 128, jnp.where(lane == 1, high, 0.0))
    ends = jnp.dot(below, parts.astype(BF16), preferred_element_type=F32)
    end = ends[:, 0:1] + ends[:, 1:2] * 128
    first = (end - groups) * width
    slot = jnp.sum(hit * (first + rank - 1.0), axis=0, keepdims=True)
    slot = jnp.where(used, slot.astype(jnp.int32), -1)
    at = (iota((length, n), 0) == slot).astype(F32).astype(BF16)
    line = iota((8, n), 0)
    values = jnp.where(line == 2, source, 1)
    values = jnp.where(line == 0, item & 255, jnp.where(line == 1, item >> 8, values))
    found = lax.dot_general(
        values.astype(F32).astype(BF16), at, (((1,), (1,)), ((), ())), preferred_element_type=F32
    ).astype(jnp.int32)
    passed = (end * width).astype(jnp.int32) <= iota((n_keys, length), 1)
    target = jnp.sum(passed.astype(F32), axis=0, keepdims=True).astype(jnp.int32)
    items = jnp.where(found[3:4] > 0, found[0:1] + found[1:2] * 256, -1)
    steps = (jnp.max(end).astype(jnp.int32) * width + PER - 1) // PER
    return items, found[2:3], target, steps, slot


def pick_kernel(n_out, ids, rows, columns, *refs):
    fetched, forward, steps, same_ids, slots = refs[:5]
    row_copy, column_copy, fetched_copy, forward_copy, arrived = refs[5:]
    copies = [
        pltpu.make_async_copy(rows.at[0], row_copy, arrived.at[0]),
        pltpu.make_async_copy(columns.at[0], column_copy, arrived.at[1]),
    ]
    for copy in copies:
        copy.start()
    for k in range(3):
        same_ids[k] = ids[k]
    for copy in copies:
        copy.wait()
    row, column = row_copy[...], column_copy[...]
    index = iota(row.shape, 1)
    length = forward.shape[1]
    used = (index < ids[3]) & (((column >> 1) & 1) == ids[0])
    source = jnp.bitwise_xor(column >> 2, ids[2]) * 2 + (column & 1)
    items, source, target, n_steps, slot = order(row, used, source, index, n_out, length, FORWARD)
    fetched_copy[...] = jnp.maximum(items, 0)
    here = jnp.where(items >= 0, iota(items.shape, 1), SPARE)
    forward_copy[...] = here + source * 1024 + target * 65536
    copies = [
        pltpu.make_async_copy(fetched_copy, fetched, arrived.at[0]),
        pltpu.make_async_copy(forward_copy, forward, arrived.at[1]),
    ]
    for copy in copies:
        copy.start()
    slots[...] = slot
    steps[0] = n_steps
    for copy in copies:
        copy.wait()


def pick(ids, rows, columns, n_out, n_back):
    length = rows.shape[-1] + max(n_out * (FORWARD - 1), n_back * (BACKWARD - 1)) + PER
    length = -(-length // TILE) * TILE
    listed = (1, length)
    return pl.pallas_call(
        functools.partial(pick_kernel, n_out),
        out_shape=[
            pltpu.SMEM(listed, jnp.int32),
            pltpu.SMEM(listed, jnp.int32),
            pltpu.SMEM((1,), jnp.int32),
            pltpu.SMEM((3,), jnp.int32),
            pltpu.VMEM(rows.shape[1:], jnp.int32),
        ],
        in_specs=[SMEM, ANY, ANY],
        out_specs=[SMEM, SMEM, SMEM, SMEM, VMEM],
        scratch_shapes=[
            pltpu.VMEM(rows.shape[1:], jnp.int32),
            pltpu.VMEM(rows.shape[1:], jnp.int32),
            pltpu.VMEM(listed, jnp.int32),
            pltpu.VMEM(listed, jnp.int32),
            pltpu.SemaphoreType.DMA((2,)),
        ],
        compiler_params=PICK_PARAMS,
        name="pick_tiles",
    )(ids, far(rows), far(columns))


def start_fetch(tiles, fetched, held, arrived, g, carry):
    for j in range(PER):
        source = tiles.at[fetched[0, g * PER + j]]
        pltpu.make_async_copy(source, held.at[g * PER + j], arrived.at[g]).start()
    return carry


def end_fetch(tiles, held, arrived, g, carry):
    block = held.at[pl.ds(g * PER, PER)]
    pltpu.make_async_copy(tiles.at[pl.ds(0, PER)], block, arrived.at[g]).wait()
    return carry


def early_kernel(steps, fetched, tiles, early, arrived):
    count = jnp.minimum(steps[0], EARLY)
    lax.fori_loop(0, count, functools.partial(start_fetch, tiles, fetched, early, arrived), 0)
    early[early.shape[0] - 1] = jnp.zeros((TILE, TILE), BF16)
    lax.fori_loop(0, count, functools.partial(end_fetch, tiles, early, arrived), 0)


def early_tiles(steps, fetched, tiles):
    return pl.pallas_call(
        early_kernel,
        out_shape=pltpu.VMEM((EARLY * PER + 1, TILE, TILE), BF16),
        in_specs=[SMEM, SMEM, ANY],
        out_specs=VMEM,
        scratch_shapes=[pltpu.SemaphoreType.DMA((EARLY,))],
        compiler_params=PARAMS,
        name="early_tiles",
    )(scalar(steps), scalar(fetched), far(tiles))


def prepare_kernel(n_back, ids, rows, columns, slots, weight, bias, cotangent, *refs):
    backward, steps, weight_copy, bias_copy, cotangent_copy = refs[:5]
    row_copy, column_copy, backward_copy, arrived = refs[5:]
    pairs = [
        (rows.at[0], row_copy),
        (columns.at[0], column_copy),
        (weight, weight_copy),
        (bias, bias_copy),
        (cotangent, cotangent_copy),
    ]
    copies = [
        pltpu.make_async_copy(source, target, arrived.at[k])
        for k, (source, target) in enumerate(pairs)
    ]
    for copy in copies:
        copy.start()
    for copy in copies:
        copy.wait()
    row, column, slot = row_copy[...], column_copy[...], slots[...]
    length = backward.shape[1]
    place = (column >> 2) * 2 + (column & 1)
    source = jnp.bitwise_xor(row >> 2, ids[1]) * 4 + (row & 3)
    used = slot >= 0
    items, source, target, n_steps, slot = order(
        place, used, source, slot, n_back, length, BACKWARD
    )
    here = jnp.where(items >= 0, items, SPARE)
    backward_copy[...] = here + source * 1024 + target * 65536
    copy = pltpu.make_async_copy(backward_copy, backward, arrived.at[5])
    copy.start()
    steps[0] = n_steps
    copy.wait()


def prepare(ids, rows, columns, slots, length, n_back, weight, bias, cotangent):
    return pl.pallas_call(
        functools.partial(prepare_kernel, n_back),
        out_shape=[
            pltpu.SMEM((1, length), jnp.int32),
            pltpu.SMEM((1,), jnp.int32),
            pltpu.VMEM(weight.shape, weight.dtype),
            pltpu.VMEM(bias.shape, bias.dtype),
            pltpu.VMEM(cotangent.shape, cotangent.dtype),
        ],
        in_specs=[SMEM, ANY, ANY, VMEM, ANY, ANY, ANY],
        out_specs=[SMEM, SMEM, VMEM, VMEM, VMEM],
        scratch_shapes=[
            pltpu.VMEM(rows.shape[1:], jnp.int32),
            pltpu.VMEM(rows.shape[1:], jnp.int32),
            pltpu.VMEM((1, length), jnp.int32),
            pltpu.SemaphoreType.DMA((6,)),
        ],
        compiler_params=PICK_PARAMS,
        name="prepare",
    )(scalar(ids), far(rows), far(columns), near(slots), far(weight), far(bias), far(cotangent))


def join_kernel(a, b, out):
    rows = a.shape[0]
    out[0:rows] = a[...]
    out[rows : 2 * rows] = b[...]


def join(a, b):
    return pl.pallas_call(
        join_kernel,
        out_shape=pltpu.VMEM((2 * a.shape[0], a.shape[1]), a.dtype),
        in_specs=[VMEM] * 2,
        out_specs=VMEM,
        compiler_params=PARAMS,
        name="join",
    )(near(a), near(b))


def add_products(flipped, first, picked, held, source, total):
    last = held.shape[0] - 1
    width = BACKWARD if flipped else FORWARD
    places = []
    products = []
    for at in range(0, PER, width):
        codes = [picked[0, first + at + j] for j in range(width)]
        places.append(codes[0] >> 16)
        mine = [held[jnp.minimum(code & 1023, last)] for code in codes]
        other = [source[(code >> 10) & 63] for code in codes]
        left, right = (other, mine) if flipped else (mine, other)
        products.append(
            jnp.dot(
                jnp.concatenate(left, 1), jnp.concatenate(right, 0), preferred_element_type=F32
            )
        )
    for place, product in zip(places, products):
        total[place] += product


def run_steps(first, last, step):
    passes = (last - first) // MERGED

    def merged(k, carry):
        for j in range(MERGED):
            step(first + k * MERGED + j)
        return carry

    def single(g, carry):
        step(g)
        return carry

    lax.fori_loop(0, passes, merged, 0)
    lax.fori_loop(first + passes * MERGED, last, single, 0)


def forward_kernel(steps, ids, fetched, picked, tiles, early, *refs):
    sources, (held, kept, sent, gathered, total, arrived) = refs[:-6], refs[-6:]
    count = steps[0]
    start = functools.partial(start_fetch, tiles, fetched, held, arrived)
    lax.fori_loop(EARLY, jnp.maximum(count, EARLY), start, 0)
    moved = pltpu.make_async_copy(
        early.at[pl.ds(0, EARLY * PER)], held.at[pl.ds(0, EARLY * PER)], arrived.at[0]
    )
    moved.start()
    held[held.shape[0] - 1] = jnp.zeros((TILE, TILE), BF16)
    total[...] = jnp.zeros_like(total)
    for m, source in enumerate(sources):
        gathered[4 * m : 4 * m + 4] = source[...].reshape(4, TILE, TILE)

    def early_step(g):
        add_products(False, g * PER, picked, early, gathered, total)

    def step(g):
        end_fetch(tiles, held, arrived, g, 0)
        add_products(False, g * PER, picked, held, gathered, total)

    run_steps(0, jnp.minimum(count, EARLY), early_step)
    run_steps(EARLY, jnp.maximum(count, EARLY), step)
    moved.wait()
    for k in range(kept.shape[0]):
        own = jnp.bitwise_xor(ids[1], 2 * k)
        kept[k] = total[pl.ds(own * 4, 4)]
        sent[k] = total[pl.ds(jnp.bitwise_xor(own, 1) * 4, 4)].astype(BF16)


def tiles_forward(steps, ids, fetched, picked, tiles, early, sources, n_out):
    shape = (n_out // 8, 4, TILE, TILE)
    length = -(-(tiles.shape[0] + n_out * (FORWARD - 1)) // PER) * PER
    return pl.pallas_call(
        forward_kernel,
        out_shape=[
            pltpu.VMEM((length + 1, TILE, TILE), BF16),
            pltpu.VMEM(shape, F32),
            pltpu.VMEM(shape, BF16),
        ],
        in_specs=[SMEM, SMEM, SMEM, SMEM, ANY, VMEM] + [VMEM] * len(sources),
        out_specs=[VMEM] * 3,
        scratch_shapes=[
            pltpu.VMEM((4 * len(sources), TILE, TILE), BF16),
            pltpu.VMEM((n_out + 1, TILE, TILE), F32),
            pltpu.SemaphoreType.DMA((length // PER,)),
        ],
        compiler_params=PARAMS,
        name="tiles_forward",
    )(
        scalar(steps),
        scalar(ids),
        scalar(fetched),
        scalar(picked),
        far(tiles),
        near(early),
        *[near(values) for values in sources],
    )


def write_terms(values, message, row):
    rest = jnp.concatenate([values, values], 0)
    line = iota(rest.shape, 0)
    terms = jnp.zeros(rest.shape, F32)
    for k in range(3):
        term = rest.astype(BF16).astype(F32)
        terms = jnp.where(line == k, term, terms)
        rest = rest - term
    message[row : row + 16] = terms.astype(BF16)


def read_terms(messages, row):
    terms = jnp.zeros((16, TILE), F32)
    for one in messages:
        terms = terms + one[row : row + 16].astype(F32)
    return jnp.broadcast_to(jnp.sum(terms, axis=0, keepdims=True), (8, TILE))


def backward_kernel(steps, ids, picked, held, *refs):
    messages, outs, (gathered, total) = refs[:-7], refs[-7:-2], refs[-2:]
    kept, grads, outs = outs[0], outs[1], (outs[0], *outs[2:])
    total[...] = jnp.zeros_like(total)
    rows = 4 * TILE
    for m, one in enumerate(messages):
        gathered[4 * m : 4 * m + 4] = one[0:rows].reshape(4, TILE, TILE)

    for k in range(2):
        weight = jnp.zeros((TILE // 2, TILE), F32)
        for one in messages[k::2]:
            weight = weight + one[rows : rows + TILE // 2].astype(F32)
        grads[pl.ds(jnp.bitwise_xor(ids[1] & 1, k) * (TILE // 2), TILE // 2)] = weight
    bias = read_terms(messages[0::2], rows + TILE // 2)
    grads[TILE : TILE + 8] = bias
    for out in outs[1:]:
        out[rows : rows + TILE] = grads[0:TILE].astype(BF16)
        write_terms(bias, out, rows + TILE)

    run_steps(0, steps[0], lambda g: add_products(True, g * PER, picked, held, gathered, total))
    for k, out in zip((0, 2, 1, 3), outs):
        for z in range(2):
            block = total[pl.ds(jnp.bitwise_xor(ids[2], 2 * k + z) * 2, 2)]
            out[2 * z * TILE : 2 * (z + 1) * TILE] = block.reshape(2 * TILE, TILE).astype(out.dtype)


def tiles_backward(steps, ids, picked, held, sources, n_back):
    rows = n_back // 4 * TILE
    return pl.pallas_call(
        backward_kernel,
        out_shape=[pltpu.VMEM((rows, TILE), F32), pltpu.VMEM((TILE + 8, TILE), F32)]
        + [pltpu.VMEM((rows + TILE + 16, TILE), BF16)] * 3,
        in_specs=[SMEM, SMEM, SMEM] + [VMEM] * (1 + len(sources)),
        out_specs=[VMEM] * 5,
        scratch_shapes=[
            pltpu.VMEM((4 * len(sources), TILE, TILE), BF16),
            pltpu.VMEM((n_back + 1, TILE, TILE), F32),
        ],
        compiler_params=PARAMS,
        name="tiles_backward",
    )(scalar(steps), scalar(ids), scalar(picked), near(held), *[near(values) for values in sources])


def pair_kernel(kept, got, first, *others):
    first[...] = kept[0] + got[0].astype(F32)
    for k, other in zip((2, 1, 3), others):
        other[...] = (kept[k] + got[k].astype(F32)).astype(BF16)


def pair_sum(kept, got):
    shape = kept.shape[1:]
    n = kept.shape[0] - 1
    return pl.pallas_call(
        pair_kernel,
        out_shape=[pltpu.VMEM(shape, F32)] + [pltpu.VMEM(shape, BF16)] * n,
        in_specs=[VMEM] * 2,
        out_specs=[VMEM] * (n + 1),
        compiler_params=PARAMS,
        name="pair_sum",
    )(near(kept), near(got))


def own_kernel(first, a, b, c, total, sent):
    value = first[...] + a[...].astype(F32) + b[...].astype(F32) + c[...].astype(F32)
    total[...] = value
    sent[...] = value.astype(BF16)


def own_sum(first, others):
    return pl.pallas_call(
        own_kernel,
        out_shape=[pltpu.VMEM(first.shape, F32), pltpu.VMEM(first.shape, BF16)],
        in_specs=[VMEM] * 4,
        out_specs=[VMEM] * 2,
        compiler_params=PARAMS,
        name="own_sum",
    )(near(first), *[near(values) for values in others])


def middle_kernel(own, other, weight, bias, cotangent, activations, back, back_sent, grads):
    blocks = own.shape[0]
    rows = blocks * TILE
    sums = (own[...] + other[...].astype(F32)).astype(BF16).reshape(rows, TILE)
    preact = jnp.dot(sums, weight[...], preferred_element_type=F32) + bias[...]
    sigma = jax.nn.sigmoid(preact)
    activations[...] = (preact * sigma).astype(BF16)
    grad = cotangent[...].astype(F32) * (sigma * (1.0 + preact * (1.0 - sigma)))
    grad_pre = grad.astype(BF16)
    grads[0:TILE] = lax.dot_general(
        sums, grad_pre, (((0,), (0,)), ((), ())), preferred_element_type=F32
    )
    total = jnp.sum(grad_pre.astype(F32), axis=0, keepdims=True)
    grads[TILE : TILE + 8] = jnp.broadcast_to(total, (8, TILE))
    for b in range(blocks):
        value = lax.dot_general(
            weight[...],
            grad_pre[b * TILE : (b + 1) * TILE],
            (((1,), (1,)), ((), ())),
            preferred_element_type=F32,
        )
        back[b] = value
        back_sent[b] = value.astype(BF16)


def middle(own, other, weight, bias, cotangent):
    return pl.pallas_call(
        middle_kernel,
        out_shape=[
            jax.ShapeDtypeStruct(cotangent.shape, BF16),
            pltpu.VMEM(own.shape, F32),
            pltpu.VMEM(own.shape, BF16),
            pltpu.VMEM((TILE + 8, TILE), F32),
        ],
        in_specs=[VMEM] * 5,
        out_specs=[VMEM] * 4,
        compiler_params=PARAMS,
        name="middle",
    )(near(own), near(other), near(weight), near(bias), near(cotangent))


def message_kernel(ids, back, other, grads, more, message):
    rows = back.shape[0] * TILE
    value = back[...] + other[...].astype(F32)
    message[0:rows] = value.astype(BF16).reshape(rows, TILE)
    half = pl.ds((ids[1] & 1) * (TILE // 2), TILE // 2)
    message[rows : rows + TILE // 2] = (grads[half] + more[half]).astype(BF16)
    write_terms(grads[TILE : TILE + 8] + more[TILE : TILE + 8], message, rows + TILE // 2)


def message(ids, back, other, grads, more):
    rows = back.shape[0] * TILE + TILE // 2 + 16
    return pl.pallas_call(
        message_kernel,
        out_shape=pltpu.VMEM((rows, TILE), BF16),
        in_specs=[SMEM] + [VMEM] * 4,
        out_specs=VMEM,
        compiler_params=PARAMS,
        name="message",
    )(scalar(ids), near(back), near(other), near(grads), near(more))


def line_kernel(kept, grads, a, b, c, own_sent, other_sent, other_message, own, own_grads):
    rows = own.shape[0]
    value = kept[...]
    weight = grads[0:TILE]
    for one in (a, b, c):
        value = value + one[0 : 2 * rows].astype(F32)
        weight = weight + one[2 * rows : 2 * rows + TILE].astype(F32)
    bias = grads[TILE : TILE + 8] + read_terms((a, b, c), 2 * rows + TILE)
    own[...] = value[:rows]
    own_sent[...] = value[:rows].astype(BF16)
    other = value[rows:].astype(BF16)
    other_sent[...] = other
    own_grads[0:TILE] = weight
    own_grads[TILE : TILE + 8] = bias
    other_message[0:rows] = other
    other_message[rows : rows + TILE] = weight.astype(BF16)
    write_terms(bias, other_message, rows + TILE)


def line_sum(kept, grads, messages):
    rows = kept.shape[0] // 2
    return pl.pallas_call(
        line_kernel,
        out_shape=[
            pltpu.VMEM((rows, TILE), BF16),
            pltpu.VMEM((rows, TILE), BF16),
            pltpu.VMEM((rows + TILE + 16, TILE), BF16),
            pltpu.VMEM((rows, TILE), F32),
            pltpu.VMEM(grads.shape, F32),
        ],
        in_specs=[VMEM] * 5,
        out_specs=[VMEM] * 5,
        compiler_params=PARAMS,
        name="line_sum",
    )(near(kept), near(grads), *[near(one) for one in messages])


def finish_kernel(ids, own, grads, opposite, corner, beside, features, weight, bias):
    rows = own.shape[0]
    for b in range(rows // TILE):
        block = pl.ds(b * TILE, TILE)
        mine = own[block] + beside[block].astype(F32)
        other = opposite[block].astype(F32) + corner[block].astype(F32)
        features[pl.ds(ids[0] * rows + b * TILE, TILE)] = mine.T
        features[pl.ds((1 - ids[0]) * rows + b * TILE, TILE)] = other.T
    weight[...] = grads[0:TILE] + beside[rows : rows + TILE].astype(F32)
    bias[...] = (grads[TILE : TILE + 8] + read_terms((beside,), rows + TILE))[0:1]


def finish(ids, own, grads, opposite, corner, beside):
    return pl.pallas_call(
        finish_kernel,
        out_shape=[
            jax.ShapeDtypeStruct((2 * own.shape[0], TILE), F32),
            jax.ShapeDtypeStruct((TILE, TILE), F32),
            jax.ShapeDtypeStruct((1, TILE), F32),
        ],
        in_specs=[SMEM] + [VMEM] * 5,
        out_specs=[VMEM] * 3,
        compiler_params=PARAMS,
        name="finish",
    )(scalar(ids), near(own), near(grads), near(opposite), near(corner), near(beside))


def local(
    features, weight, hidden_bias, adjacency_tiles, tile_rows, tile_columns, tile_count, cotangent
):
    tiles = adjacency_tiles[0, 0]
    n_row, n_col = lax.axis_size("row"), lax.axis_size("col")
    own_rows, fin = features.shape
    blocks = own_rows // TILE
    n_out, n_back = blocks * n_col, blocks // 2 * n_row
    half = lax.axis_index("feat")
    places = [half, lax.axis_index("col"), lax.axis_index("row"), tile_count[0, 0]]
    ids = jnp.stack(places).astype(jnp.int32)

    mine = lax.dynamic_slice_in_dim(features, half * (own_rows // 2), own_rows // 2, 0)
    mine, ids = lax.optimization_barrier((mine, ids))
    lists = pick(ids, tile_rows, tile_columns, n_out, n_back)
    beside, lists = lax.optimization_barrier((swap(mine, "row", 1), lists))
    fetched, forward, steps, ids, slots = lists
    pair = join(mine, beside)
    second, first, third = swap_line([pair] * 3, "row")
    early = early_tiles(steps, fetched, tiles)
    early, first, third, second = lax.optimization_barrier((early, first, third, second))

    held, kept, sent = tiles_forward(steps, ids, fetched, forward, tiles, early, [pair, first, second, third], n_out)
    first, *others = pair_sum(kept, swap(sent, "col", 1))
    others = swap_line(others, "col")
    own, sent = own_sum(first, others)
    sent, slots = lax.optimization_barrier((sent, slots))
    ready = prepare(
        ids, tile_rows, tile_columns, slots, forward.shape[1], n_back, weight, hidden_bias[None], cotangent
    )
    other, ready = lax.optimization_barrier((swap(sent, "feat", 1), ready))
    backward, steps, weight, bias, cotangent = ready
    activations, back, back_sent, grads = middle(own, other, weight, bias, cotangent)

    back_other, more = lax.optimization_barrier((swap(back_sent, "feat", 1), swap(grads, "col", 1)))
    mine = message(ids, back, back_other, grads, more)
    across = [swap(mine, "col", mask) for mask in (2, 6, 4)]
    beside = swap(mine, "col", 1)
    across = lax.optimization_barrier(across)
    corners = [swap(values, "col", 1) for values in across]
    sources = [mine, beside, across[0], corners[0], across[2], corners[2], across[1], corners[1]]
    kept, grads, *others = tiles_backward(steps, ids, backward, held, sources, n_back)

    others = swap_line(others, "row")
    own_sent, other_sent, other_message, own, grads = line_sum(kept, grads, others)
    opposite = swap(own_sent, "feat", 1)
    corner = swap(other_sent, ("row", "feat"), 3)
    beside = swap(other_message, "row", 1)
    grad_features, grad_weight, grad_bias = finish(ids, own, grads, opposite, corner, beside)
    return (activations, grad_features, grad_weight, grad_bias[0])


def solution(mesh):
    placed = (
        P(("col", "row"), None),
        P(None, "feat"),
        P("feat"),
        P("row", "col", None, None, None),
        P("row", "col", None),
        P("row", "col", None),
        P("row", "col"),
        P(("row", "col"), "feat"),
    )
    return jax.shard_map(
        local,
        mesh=mesh,
        in_specs=placed,
        out_specs=(P(("row", "col"), "feat"), P(("col", "row"), None), P(None, "feat"), P("feat")),
        check_vma=False,
    )
```

```python
import functools

import jax
import jax.numpy as jnp
from jax import lax
from jax.experimental import pallas as pl
from jax.experimental.pallas import tpu as pltpu
from jax.sharding import PartitionSpec as P

F32 = jnp.float32
BF16 = jnp.bfloat16
TILE = 128
PER = 32
MERGED = 5
FORWARD = 2
BACKWARD = 4
SPARE = 1023
EARLY = 5
VMEM = pl.BlockSpec(memory_space=pltpu.VMEM)
SMEM = pl.BlockSpec(memory_space=pltpu.SMEM)
ANY = pl.BlockSpec(memory_space=pl.ANY)
PARAMS = pltpu.CompilerParams(vmem_limit_bytes=8 * 1024 * 1024)
PICK_PARAMS = pltpu.CompilerParams(vmem_limit_bytes=16 * 1024 * 1024)


def swap(values, axis, mask):
    size = lax.axis_size(axis)
    return lax.ppermute(values, axis, [(i, i ^ mask) for i in range(size)])


def swap_line(values, axis):
    return [swap(one, axis, mask) for one, mask in zip(values, (4, 2, 6))]


def near(values):
    return pltpu.with_memory_space_constraint(values, pltpu.VMEM)


def scalar(values):
    return pltpu.with_memory_space_constraint(values, pltpu.SMEM)


def far(values):
    return pltpu.with_memory_space_constraint(values, pltpu.HBM)


def iota(shape, dim):
    return lax.broadcasted_iota(jnp.int32, shape, dim)


def order(key, used, source, item, n_keys, length, width, split=0):
    n = key.shape[1]
    hit = ((iota((n_keys, n), 0) == key) & used).astype(F32)
    upto = (iota((n, n), 0) <= iota((n, n), 1)).astype(BF16)
    rank = jnp.dot(hit.astype(BF16), upto, preferred_element_type=F32)
    groups = jnp.floor((rank[:, n - 1 :] + (width - 1)) * (1.0 / width))
    below = (iota((n_keys, n_keys), 0) >= iota((n_keys, n_keys), 1)).astype(BF16)
    groups = jnp.broadcast_to(groups, (n_keys, TILE))
    high = jnp.floor(groups * (1.0 / 128))
    low = groups - high * 128
    end = jnp.dot(below, low.astype(BF16), preferred_element_type=F32)
    end = end + jnp.dot(below, high.astype(BF16), preferred_element_type=F32) * 128
    n_first = 0
    if split:
        part = iota((n_keys, TILE), 0) < split
        before = jnp.where(part, end, 0.0)
        n_first = (jnp.max(before).astype(jnp.int32) * width + PER - 1) // PER
        before = jnp.max(before, axis=0, keepdims=True)
        steps = jnp.floor((before * width + (PER - 1)) * (1.0 / PER))
        end = end + jnp.where(part, 0.0, steps * (PER // width) - before)
    groups, end = groups[:, :1], end[:, :1]
    first = (end - groups) * width
    slot = jnp.sum(hit * (first + rank - 1.0), axis=0, keepdims=True)
    slot = jnp.where(used, slot.astype(jnp.int32), -1)
    at = (iota((length, n), 0) == slot).astype(F32).astype(BF16)
    line = iota((8, n), 0)
    values = jnp.where(line == 2, source, 1)
    values = jnp.where(line == 0, item & 255, jnp.where(line == 1, item >> 8, values))
    found = lax.dot_general(
        values.astype(F32).astype(BF16), at, (((1,), (1,)), ((), ())), preferred_element_type=F32
    ).astype(jnp.int32)
    passed = (end * width).astype(jnp.int32) <= iota((n_keys, length), 1)
    target = jnp.sum(passed.astype(F32), axis=0, keepdims=True).astype(jnp.int32)
    items = jnp.where(found[3:4] > 0, found[0:1] + found[1:2] * 256, -1)
    steps = (jnp.max(end).astype(jnp.int32) * width + PER - 1) // PER
    return items, found[2:3], target, steps, slot, n_first


def pick_kernel(n_out, ids, rows, columns, *refs):
    fetched, forward, steps, same_ids, slots, fetched_copy, forward_copy, arrived = refs
    for k in range(3):
        same_ids[k] = ids[k]
    row, column = rows[0], columns[0]
    index = iota(row.shape, 1)
    length = forward.shape[1]
    used = (index < ids[3]) & (((column >> 1) & 1) == ids[0])
    source = jnp.bitwise_xor(column >> 2, ids[2]) * 2 + (column & 1)
    items, source, target, n_steps, slot, _ = order(
        row, used, source, index, n_out, length, FORWARD
    )
    fetched_copy[...] = jnp.maximum(items, 0)
    here = jnp.where(items >= 0, iota(items.shape, 1), SPARE)
    forward_copy[...] = here + source * 1024 + target * 65536
    copies = [
        pltpu.make_async_copy(fetched_copy, fetched, arrived.at[0]),
        pltpu.make_async_copy(forward_copy, forward, arrived.at[1]),
    ]
    for copy in copies:
        copy.start()
    slots[...] = slot
    steps[0] = n_steps
    for copy in copies:
        copy.wait()


def pick(ids, rows, columns, n_out, n_back):
    length = rows.shape[-1] + max(n_out * (FORWARD - 1), n_back * (BACKWARD - 1)) + 2 * PER
    length = -(-length // TILE) * TILE
    listed = (1, length)
    return pl.pallas_call(
        functools.partial(pick_kernel, n_out),
        out_shape=[
            pltpu.SMEM(listed, jnp.int32),
            pltpu.SMEM(listed, jnp.int32),
            pltpu.SMEM((1,), jnp.int32),
            pltpu.SMEM((3,), jnp.int32),
            pltpu.VMEM(rows.shape[1:], jnp.int32),
        ],
        in_specs=[SMEM, VMEM, VMEM],
        out_specs=[SMEM, SMEM, SMEM, SMEM, VMEM],
        scratch_shapes=[
            pltpu.VMEM(listed, jnp.int32),
            pltpu.VMEM(listed, jnp.int32),
            pltpu.SemaphoreType.DMA((2,)),
        ],
        compiler_params=PICK_PARAMS,
        name="pick_tiles",
    )(ids, far(rows), far(columns))


def start_fetch(tiles, fetched, held, arrived, g, carry):
    for j in range(PER):
        source = tiles.at[fetched[0, g * PER + j]]
        pltpu.make_async_copy(source, held.at[g * PER + j], arrived.at[g]).start()
    return carry


def end_fetch(tiles, held, arrived, g, carry):
    block = held.at[pl.ds(g * PER, PER)]
    pltpu.make_async_copy(tiles.at[pl.ds(0, PER)], block, arrived.at[g]).wait()
    return carry


def early_kernel(steps, fetched, tiles, early, arrived):
    count = jnp.minimum(steps[0], EARLY)
    lax.fori_loop(0, count, functools.partial(start_fetch, tiles, fetched, early, arrived), 0)
    early[early.shape[0] - 1] = jnp.zeros((TILE, TILE), BF16)
    lax.fori_loop(0, count, functools.partial(end_fetch, tiles, early, arrived), 0)


def early_tiles(steps, fetched, tiles):
    return pl.pallas_call(
        early_kernel,
        out_shape=pltpu.VMEM((EARLY * PER + 1, TILE, TILE), BF16),
        in_specs=[SMEM, SMEM, ANY],
        out_specs=VMEM,
        scratch_shapes=[pltpu.SemaphoreType.DMA((EARLY,))],
        compiler_params=PARAMS,
        name="early_tiles",
    )(scalar(steps), scalar(fetched), far(tiles))


def prepare_kernel(n_back, ids, rows, columns, slots, weight, bias, cotangent, *refs):
    backward, steps, weight_copy, bias_copy, cotangent_copy = refs[:5]
    row_copy, column_copy, backward_copy, arrived = refs[5:]
    pairs = [
        (rows.at[0], row_copy),
        (columns.at[0], column_copy),
        (weight, weight_copy),
        (bias, bias_copy),
        (cotangent, cotangent_copy),
    ]
    copies = [
        pltpu.make_async_copy(source, target, arrived.at[k])
        for k, (source, target) in enumerate(pairs)
    ]
    for copy in copies:
        copy.start()
    for copy in copies:
        copy.wait()
    row, column, slot = row_copy[...], column_copy[...], slots[...]
    length = backward.shape[1]
    owner = jnp.bitwise_xor(column >> 2, ids[2])
    chip = owner >> 1
    chip = jnp.where(chip == 2, 0, jnp.where(chip == 1, 1, jnp.where(chip == 3, 2, 3)))
    place = chip * 4 + (owner & 1) * 2 + (column & 1)
    source = jnp.bitwise_xor(row >> 2, ids[1]) * 4 + (row & 3)
    used = slot >= 0
    items, source, target, n_steps, slot, n_first = order(
        place, used, source, slot, n_back, length, BACKWARD, 4
    )
    here = jnp.where(items >= 0, items, SPARE)
    backward_copy[...] = here + source * 1024 + target * 65536
    copy = pltpu.make_async_copy(backward_copy, backward, arrived.at[5])
    copy.start()
    steps[0] = n_first
    steps[1] = n_steps
    copy.wait()


def prepare(ids, rows, columns, slots, length, n_back, weight, bias, cotangent):
    return pl.pallas_call(
        functools.partial(prepare_kernel, n_back),
        out_shape=[
            pltpu.SMEM((1, length), jnp.int32),
            pltpu.SMEM((2,), jnp.int32),
            pltpu.VMEM(weight.shape, weight.dtype),
            pltpu.VMEM(bias.shape, bias.dtype),
            pltpu.VMEM(cotangent.shape, cotangent.dtype),
        ],
        in_specs=[SMEM, ANY, ANY, VMEM, ANY, ANY, ANY],
        out_specs=[SMEM, SMEM, VMEM, VMEM, VMEM],
        scratch_shapes=[
            pltpu.VMEM(rows.shape[1:], jnp.int32),
            pltpu.VMEM(rows.shape[1:], jnp.int32),
            pltpu.VMEM((1, length), jnp.int32),
            pltpu.SemaphoreType.DMA((6,)),
        ],
        compiler_params=PICK_PARAMS,
        name="prepare",
    )(scalar(ids), far(rows), far(columns), near(slots), far(weight), far(bias), far(cotangent))


def join_kernel(a, b, out):
    rows = a.shape[0]
    out[0:rows] = a[...]
    out[rows : 2 * rows] = b[...]


def join(a, b):
    return pl.pallas_call(
        join_kernel,
        out_shape=pltpu.VMEM((2 * a.shape[0], a.shape[1]), a.dtype),
        in_specs=[VMEM] * 2,
        out_specs=VMEM,
        compiler_params=PARAMS,
        name="join",
    )(near(a), near(b))


def add_products(flipped, first, picked, held, source, total):
    last = held.shape[0] - 1
    width = BACKWARD if flipped else FORWARD
    places = []
    products = []
    for at in range(0, PER, width):
        codes = [picked[0, first + at + j] for j in range(width)]
        places.append(codes[0] >> 16)
        mine = [held[jnp.minimum(code & 1023, last)] for code in codes]
        other = [source[(code >> 10) & 63] for code in codes]
        left, right = (other, mine) if flipped else (mine, other)
        products.append(
            jnp.dot(
                jnp.concatenate(left, 1), jnp.concatenate(right, 0), preferred_element_type=F32
            )
        )
    for place, product in zip(places, products):
        total[place] += product


def run_steps(first, last, step):
    passes = (last - first) // MERGED

    def merged(k, carry):
        for j in range(MERGED):
            step(first + k * MERGED + j)
        return carry

    def single(g, carry):
        step(g)
        return carry

    lax.fori_loop(0, passes, merged, 0)
    lax.fori_loop(first + passes * MERGED, last, single, 0)


def forward_kernel(steps, ids, fetched, picked, tiles, early, *refs):
    sources, (held, kept, sent, gathered, total, arrived) = refs[:-6], refs[-6:]
    count = steps[0]
    start = functools.partial(start_fetch, tiles, fetched, held, arrived)
    lax.fori_loop(EARLY, jnp.maximum(count, EARLY), start, 0)
    moved = pltpu.make_async_copy(
        early.at[pl.ds(0, EARLY * PER)], held.at[pl.ds(0, EARLY * PER)], arrived.at[0]
    )
    moved.start()
    held[held.shape[0] - 1] = jnp.zeros((TILE, TILE), BF16)
    total[...] = jnp.zeros_like(total)
    for m, source in enumerate(sources):
        gathered[4 * m : 4 * m + 4] = source[...].reshape(4, TILE, TILE)

    def early_step(g):
        add_products(False, g * PER, picked, early, gathered, total)

    def step(g):
        end_fetch(tiles, held, arrived, g, 0)
        add_products(False, g * PER, picked, held, gathered, total)

    run_steps(0, jnp.minimum(count, EARLY), early_step)
    run_steps(EARLY, jnp.maximum(count, EARLY), step)
    moved.wait()
    for k in range(kept.shape[0]):
        own = jnp.bitwise_xor(ids[1], 2 * k)
        kept[k] = total[pl.ds(own * 4, 4)]
        sent[k] = total[pl.ds(jnp.bitwise_xor(own, 1) * 4, 4)].astype(BF16)


def tiles_forward(steps, ids, fetched, picked, tiles, early, sources, n_out):
    shape = (n_out // 8, 4, TILE, TILE)
    length = -(-(tiles.shape[0] + n_out * (FORWARD - 1)) // PER) * PER
    return pl.pallas_call(
        forward_kernel,
        out_shape=[
            pltpu.VMEM((length + 1, TILE, TILE), BF16),
            pltpu.VMEM(shape, F32),
            pltpu.VMEM(shape, BF16),
        ],
        in_specs=[SMEM, SMEM, SMEM, SMEM, ANY, VMEM] + [VMEM] * len(sources),
        out_specs=[VMEM] * 3,
        scratch_shapes=[
            pltpu.VMEM((4 * len(sources), TILE, TILE), BF16),
            pltpu.VMEM((n_out + 1, TILE, TILE), F32),
            pltpu.SemaphoreType.DMA((length // PER,)),
        ],
        compiler_params=PARAMS,
        name="tiles_forward",
    )(
        scalar(steps),
        scalar(ids),
        scalar(fetched),
        scalar(picked),
        far(tiles),
        near(early),
        *[near(values) for values in sources],
    )


def write_terms(values, message, row):
    rest = jnp.concatenate([values, values], 0)
    line = iota(rest.shape, 0)
    terms = jnp.zeros(rest.shape, F32)
    for k in range(3):
        term = rest.astype(BF16).astype(F32)
        terms = jnp.where(line == k, term, terms)
        rest = rest - term
    message[row : row + 16] = terms.astype(BF16)


def read_terms(messages, row):
    terms = jnp.zeros((16, TILE), F32)
    for one in messages:
        terms = terms + one[row : row + 16].astype(F32)
    return jnp.broadcast_to(jnp.sum(terms, axis=0, keepdims=True), (8, TILE))


def first_kernel(steps, ids, picked, held, *refs):
    messages, (gathered, grads, out, total) = refs[:-4], refs[-4:]
    total[...] = jnp.zeros_like(total)
    rows = 4 * TILE
    for m, one in enumerate(messages):
        gathered[4 * m : 4 * m + 4] = one[0:rows].reshape(4, TILE, TILE)

    for k in range(2):
        weight = jnp.zeros((TILE // 2, TILE), F32)
        for one in messages[k::2]:
            weight = weight + one[rows : rows + TILE // 2].astype(F32)
        grads[pl.ds(jnp.bitwise_xor(ids[1] & 1, k) * (TILE // 2), TILE // 2)] = weight
    bias = read_terms(messages[0::2], rows + TILE // 2)
    grads[TILE : TILE + 8] = bias
    out[rows : rows + TILE] = grads[0:TILE].astype(BF16)
    write_terms(bias, out, rows + TILE)
    run_steps(0, steps[0], lambda g: add_products(True, g * PER, picked, held, gathered, total))
    out[0:rows] = total[0:4].reshape(rows, TILE).astype(BF16)


def tiles_first(steps, ids, picked, held, sources):
    rows = 4 * TILE
    return pl.pallas_call(
        first_kernel,
        out_shape=[
            pltpu.VMEM((4 * len(sources), TILE, TILE), BF16),
            pltpu.VMEM((TILE + 8, TILE), F32),
            pltpu.VMEM((rows + TILE + 16, TILE), BF16),
        ],
        in_specs=[SMEM, SMEM, SMEM] + [VMEM] * (1 + len(sources)),
        out_specs=[VMEM] * 3,
        scratch_shapes=[pltpu.VMEM((5, TILE, TILE), F32)],
        compiler_params=PARAMS,
        name="tiles_first",
    )(scalar(steps), scalar(ids), scalar(picked), near(held), *[near(values) for values in sources])


def second_kernel(steps, picked, held, gathered, grads, kept, second, third, total):
    total[...] = jnp.zeros_like(total)
    rows = 4 * TILE
    for out in (second, third):
        out[rows : rows + TILE] = grads[0:TILE].astype(BF16)
        write_terms(grads[TILE : TILE + 8], out, rows + TILE)
    run_steps(steps[0], steps[1], lambda g: add_products(True, g * PER, picked, held, gathered, total))
    for k, out in enumerate((second, third, kept)):
        out[0:rows] = total[4 * k + 4 : 4 * k + 8].reshape(rows, TILE).astype(out.dtype)


def tiles_second(steps, picked, held, gathered, grads, n_back):
    rows = 4 * TILE
    return pl.pallas_call(
        second_kernel,
        out_shape=[pltpu.VMEM((rows, TILE), F32)]
        + [pltpu.VMEM((rows + TILE + 16, TILE), BF16)] * 2,
        in_specs=[SMEM, SMEM] + [VMEM] * 3,
        out_specs=[VMEM] * 3,
        scratch_shapes=[pltpu.VMEM((n_back + 1, TILE, TILE), F32)],
        compiler_params=PARAMS,
        cost_estimate=pl.CostEstimate(
            flops=held.shape[0] * 2 * TILE**3,
            bytes_accessed=held.shape[0] * 2 * TILE**2,
            transcendentals=0,
        ),
        name="tiles_second",
    )(scalar(steps), scalar(picked), near(held), near(gathered), near(grads))


def pair_kernel(kept, got, first, *others):
    first[...] = kept[0] + got[0].astype(F32)
    for k, other in zip((2, 1, 3), others):
        other[...] = (kept[k] + got[k].astype(F32)).astype(BF16)


def pair_sum(kept, got):
    shape = kept.shape[1:]
    n = kept.shape[0] - 1
    return pl.pallas_call(
        pair_kernel,
        out_shape=[pltpu.VMEM(shape, F32)] + [pltpu.VMEM(shape, BF16)] * n,
        in_specs=[VMEM] * 2,
        out_specs=[VMEM] * (n + 1),
        compiler_params=PARAMS,
        name="pair_sum",
    )(near(kept), near(got))


def own_kernel(first, a, b, c, total, sent):
    value = first[...] + a[...].astype(F32) + b[...].astype(F32) + c[...].astype(F32)
    total[...] = value
    sent[...] = value.astype(BF16)


def own_sum(first, others):
    return pl.pallas_call(
        own_kernel,
        out_shape=[pltpu.VMEM(first.shape, F32), pltpu.VMEM(first.shape, BF16)],
        in_specs=[VMEM] * 4,
        out_specs=[VMEM] * 2,
        compiler_params=PARAMS,
        name="own_sum",
    )(near(first), *[near(values) for values in others])


def middle_kernel(own, other, weight, bias, cotangent, activations, back, back_sent, grads):
    blocks = own.shape[0]
    rows = blocks * TILE
    sums = (own[...] + other[...].astype(F32)).astype(BF16).reshape(rows, TILE)
    preact = jnp.dot(sums, weight[...], preferred_element_type=F32) + bias[...]
    sigma = jax.nn.sigmoid(preact)
    activations[...] = (preact * sigma).astype(BF16)
    grad = cotangent[...].astype(F32) * (sigma * (1.0 + preact * (1.0 - sigma)))
    grad_pre = grad.astype(BF16)
    grads[0:TILE] = lax.dot_general(
        sums, grad_pre, (((0,), (0,)), ((), ())), preferred_element_type=F32
    )
    total = jnp.sum(grad_pre.astype(F32), axis=0, keepdims=True)
    grads[TILE : TILE + 8] = jnp.broadcast_to(total, (8, TILE))
    for b in range(blocks):
        value = lax.dot_general(
            weight[...],
            grad_pre[b * TILE : (b + 1) * TILE],
            (((1,), (1,)), ((), ())),
            preferred_element_type=F32,
        )
        back[b] = value
        back_sent[b] = value.astype(BF16)


def middle(own, other, weight, bias, cotangent):
    return pl.pallas_call(
        middle_kernel,
        out_shape=[
            jax.ShapeDtypeStruct(cotangent.shape, BF16),
            pltpu.VMEM(own.shape, F32),
            pltpu.VMEM(own.shape, BF16),
            pltpu.VMEM((TILE + 8, TILE), F32),
        ],
        in_specs=[VMEM] * 5,
        out_specs=[VMEM] * 4,
        compiler_params=PARAMS,
        name="middle",
    )(near(own), near(other), near(weight), near(bias), near(cotangent))


def message_kernel(ids, back, other, grads, more, message):
    rows = back.shape[0] * TILE
    value = back[...] + other[...].astype(F32)
    message[0:rows] = value.astype(BF16).reshape(rows, TILE)
    half = pl.ds((ids[1] & 1) * (TILE // 2), TILE // 2)
    message[rows : rows + TILE // 2] = (grads[half] + more[half]).astype(BF16)
    write_terms(grads[TILE : TILE + 8] + more[TILE : TILE + 8], message, rows + TILE // 2)


def message(ids, back, other, grads, more):
    rows = back.shape[0] * TILE + TILE // 2 + 16
    return pl.pallas_call(
        message_kernel,
        out_shape=pltpu.VMEM((rows, TILE), BF16),
        in_specs=[SMEM] + [VMEM] * 4,
        out_specs=VMEM,
        compiler_params=PARAMS,
        name="message",
    )(scalar(ids), near(back), near(other), near(grads), near(more))


def near_kernel(kept, grads, a, value, sums):
    rows = kept.shape[0]
    value[...] = kept[...] + a[0:rows].astype(F32)
    sums[0:TILE] = grads[0:TILE] + a[rows : rows + TILE].astype(F32)
    sums[TILE : TILE + 8] = grads[TILE : TILE + 8] + read_terms((a,), rows + TILE)


def first_sum(kept, grads, message):
    return pl.pallas_call(
        near_kernel,
        out_shape=[pltpu.VMEM(kept.shape, F32), pltpu.VMEM(grads.shape, F32)],
        in_specs=[VMEM] * 3,
        out_specs=[VMEM] * 2,
        compiler_params=PARAMS,
        name="first_sum",
    )(near(kept), near(grads), near(message))


def line_kernel(kept, grads, a, b, own_sent, other_sent, other_message, own, own_grads):
    rows = own.shape[0]
    value = kept[...]
    weight = grads[0:TILE]
    for one in (a, b):
        value = value + one[0 : 2 * rows].astype(F32)
        weight = weight + one[2 * rows : 2 * rows + TILE].astype(F32)
    bias = grads[TILE : TILE + 8] + read_terms((a, b), 2 * rows + TILE)
    own[...] = value[:rows]
    own_sent[...] = value[:rows].astype(BF16)
    other = value[rows:].astype(BF16)
    other_sent[...] = other
    own_grads[0:TILE] = weight
    own_grads[TILE : TILE + 8] = bias
    other_message[0:rows] = other
    other_message[rows : rows + TILE] = weight.astype(BF16)
    write_terms(bias, other_message, rows + TILE)


def line_sum(kept, grads, messages):
    rows = kept.shape[0] // 2
    return pl.pallas_call(
        line_kernel,
        out_shape=[
            pltpu.VMEM((rows, TILE), BF16),
            pltpu.VMEM((rows, TILE), BF16),
            pltpu.VMEM((rows + TILE + 16, TILE), BF16),
            pltpu.VMEM((rows, TILE), F32),
            pltpu.VMEM(grads.shape, F32),
        ],
        in_specs=[VMEM] * 4,
        out_specs=[VMEM] * 5,
        compiler_params=PARAMS,
        name="line_sum",
    )(near(kept), near(grads), *[near(one) for one in messages])


def finish_kernel(ids, own, grads, opposite, corner, beside, features, weight, bias):
    rows = own.shape[0]
    for b in range(rows // TILE):
        block = pl.ds(b * TILE, TILE)
        mine = own[block] + beside[block].astype(F32)
        other = opposite[block].astype(F32) + corner[block].astype(F32)
        features[pl.ds(ids[0] * rows + b * TILE, TILE)] = mine.T
        features[pl.ds((1 - ids[0]) * rows + b * TILE, TILE)] = other.T
    weight[...] = grads[0:TILE] + beside[rows : rows + TILE].astype(F32)
    bias[...] = (grads[TILE : TILE + 8] + read_terms((beside,), rows + TILE))[0:1]


def finish(ids, own, grads, opposite, corner, beside):
    return pl.pallas_call(
        finish_kernel,
        out_shape=[
            jax.ShapeDtypeStruct((2 * own.shape[0], TILE), F32),
            jax.ShapeDtypeStruct((TILE, TILE), F32),
            jax.ShapeDtypeStruct((1, TILE), F32),
        ],
        in_specs=[SMEM] + [VMEM] * 5,
        out_specs=[VMEM] * 3,
        compiler_params=PARAMS,
        name="finish",
    )(scalar(ids), near(own), near(grads), near(opposite), near(corner), near(beside))


def local(
    features, weight, hidden_bias, adjacency_tiles, tile_rows, tile_columns, tile_count, cotangent
):
    tiles = adjacency_tiles[0, 0]
    n_row, n_col = lax.axis_size("row"), lax.axis_size("col")
    own_rows, fin = features.shape
    blocks = own_rows // TILE
    n_out, n_back = blocks * n_col, blocks // 2 * n_row
    half = lax.axis_index("feat")
    places = [half, lax.axis_index("col"), lax.axis_index("row"), tile_count[0, 0]]
    ids = jnp.stack(places).astype(jnp.int32)

    mine = lax.dynamic_slice_in_dim(features, half * (own_rows // 2), own_rows // 2, 0)
    mine, ids = lax.optimization_barrier((mine, ids))
    lists = pick(ids, tile_rows, tile_columns, n_out, n_back)
    beside, lists = lax.optimization_barrier((swap(mine, "row", 1), lists))
    fetched, forward, steps, ids, slots = lists
    pair = join(mine, beside)
    second, first, third = swap_line([pair] * 3, "row")
    early = early_tiles(steps, fetched, tiles)
    early, first, third, second = lax.optimization_barrier((early, first, third, second))

    held, kept, sent = tiles_forward(steps, ids, fetched, forward, tiles, early, [pair, first, second, third], n_out)
    first, *others = pair_sum(kept, swap(sent, "col", 1))
    others = swap_line(others, "col")
    own, sent = own_sum(first, others)
    sent, slots = lax.optimization_barrier((sent, slots))
    ready = prepare(
        ids, tile_rows, tile_columns, slots, forward.shape[1], n_back, weight, hidden_bias[None], cotangent
    )
    other, ready = lax.optimization_barrier((swap(sent, "feat", 1), ready))
    backward, steps, weight, bias, cotangent = ready
    activations, back, back_sent, grads = middle(own, other, weight, bias, cotangent)

    back_other, more = lax.optimization_barrier((swap(back_sent, "feat", 1), swap(grads, "col", 1)))
    mine = message(ids, back, back_other, grads, more)
    across = [swap(mine, "col", mask) for mask in (2, 6, 4)]
    beside = swap(mine, "col", 1)
    across = lax.optimization_barrier(across)
    corners = [swap(values, "col", 1) for values in across]
    sources = [mine, beside, across[0], corners[0], across[2], corners[2], across[1], corners[1]]
    gathered, grads, first = tiles_first(steps, ids, backward, held, sources)

    first = swap(first, "row", 4)
    kept, second, third = tiles_second(steps, backward, held, gathered, grads, n_back)
    others = [swap(second, "row", 2), swap(third, "row", 6)]
    kept, grads = first_sum(kept, grads, first)
    own_sent, other_sent, other_message, own, grads = line_sum(kept, grads, others)
    opposite = swap(own_sent, "feat", 1)
    corner = swap(other_sent, ("row", "feat"), 3)
    beside = swap(other_message, "row", 1)
    grad_features, grad_weight, grad_bias = finish(ids, own, grads, opposite, corner, beside)
    return (activations, grad_features, grad_weight, grad_bias[0])


def solution(mesh):
    placed = (
        P(("col", "row"), None),
        P(None, "feat"),
        P("feat"),
        P("row", "col", None, None, None),
        P("row", "col", None),
        P("row", "col", None),
        P("row", "col"),
        P(("row", "col"), "feat"),
    )
    return jax.shard_map(
        local,
        mesh=mesh,
        in_specs=placed,
        out_specs=(P(("row", "col"), "feat"), P(("col", "row"), None), P(None, "feat"), P("feat")),
        check_vma=False,
    )
```

```python
import functools

import jax
import jax.numpy as jnp
from jax import lax
from jax.experimental import pallas as pl
from jax.experimental.pallas import tpu as pltpu
from jax.sharding import PartitionSpec as P

F32 = jnp.float32
BF16 = jnp.bfloat16
TILE = 128
PER = 32
MERGED = 5
FORWARD = 2
BACKWARD = 4
SPARE = 1023
EARLY = 5
VMEM = pl.BlockSpec(memory_space=pltpu.VMEM)
SMEM = pl.BlockSpec(memory_space=pltpu.SMEM)
ANY = pl.BlockSpec(memory_space=pl.ANY)
PARAMS = pltpu.CompilerParams(vmem_limit_bytes=8 * 1024 * 1024)
PICK_PARAMS = pltpu.CompilerParams(vmem_limit_bytes=16 * 1024 * 1024)


def swap(values, axis, mask):
    size = lax.axis_size(axis)
    return lax.ppermute(values, axis, [(i, i ^ mask) for i in range(size)])


def swap_line(values, axis):
    return [swap(one, axis, mask) for one, mask in zip(values, (4, 2, 6))]


def near(values):
    return pltpu.with_memory_space_constraint(values, pltpu.VMEM)


def scalar(values):
    return pltpu.with_memory_space_constraint(values, pltpu.SMEM)


def far(values):
    return pltpu.with_memory_space_constraint(values, pltpu.HBM)


def iota(shape, dim):
    return lax.broadcasted_iota(jnp.int32, shape, dim)


def order(key, used, source, item, n_keys, length, width, split=0):
    n = key.shape[1]
    hit = ((iota((n_keys, n), 0) == key) & used).astype(F32)
    upto = (iota((n, n), 0) <= iota((n, n), 1)).astype(BF16)
    rank = jnp.dot(hit.astype(BF16), upto, preferred_element_type=F32)
    groups = jnp.floor((rank[:, n - 1 :] + (width - 1)) * (1.0 / width))
    below = (iota((n_keys, n_keys), 0) >= iota((n_keys, n_keys), 1)).astype(BF16)
    groups = jnp.broadcast_to(groups, (n_keys, TILE))
    high = jnp.floor(groups * (1.0 / 128))
    low = groups - high * 128
    end = jnp.dot(below, low.astype(BF16), preferred_element_type=F32)
    end = end + jnp.dot(below, high.astype(BF16), preferred_element_type=F32) * 128
    n_first = 0
    if split:
        part = iota((n_keys, TILE), 0) < split
        before = jnp.where(part, end, 0.0)
        n_first = (jnp.max(before).astype(jnp.int32) * width + PER - 1) // PER
        before = jnp.max(before, axis=0, keepdims=True)
        steps = jnp.floor((before * width + (PER - 1)) * (1.0 / PER))
        end = end + jnp.where(part, 0.0, steps * (PER // width) - before)
    groups, end = groups[:, :1], end[:, :1]
    first = (end - groups) * width
    slot = jnp.sum(hit * (first + rank - 1.0), axis=0, keepdims=True)
    slot = jnp.where(used, slot.astype(jnp.int32), -1)
    at = (iota((length, n), 0) == slot).astype(F32).astype(BF16)
    line = iota((8, n), 0)
    values = jnp.where(line == 2, source, 1)
    values = jnp.where(line == 0, item & 255, jnp.where(line == 1, item >> 8, values))
    found = lax.dot_general(
        values.astype(F32).astype(BF16), at, (((1,), (1,)), ((), ())), preferred_element_type=F32
    ).astype(jnp.int32)
    passed = (end * width).astype(jnp.int32) <= iota((n_keys, length), 1)
    target = jnp.sum(passed.astype(F32), axis=0, keepdims=True).astype(jnp.int32)
    items = jnp.where(found[3:4] > 0, found[0:1] + found[1:2] * 256, -1)
    steps = (jnp.max(end).astype(jnp.int32) * width + PER - 1) // PER
    return items, found[2:3], target, steps, slot, n_first


def pick_kernel(n_out, ids, rows, columns, *refs):
    fetched, forward, steps, same_ids, slots, fetched_copy, forward_copy, arrived = refs
    for k in range(3):
        same_ids[k] = ids[k]
    row, column = rows[0], columns[0]
    index = iota(row.shape, 1)
    length = forward.shape[1]
    used = (index < ids[3]) & (((column >> 1) & 1) == ids[0])
    source = jnp.bitwise_xor(column >> 2, ids[2]) * 2 + (column & 1)
    items, source, target, n_steps, slot, _ = order(
        row, used, source, index, n_out, length, FORWARD
    )
    fetched_copy[...] = jnp.maximum(items, 0)
    here = jnp.where(items >= 0, iota(items.shape, 1), SPARE)
    forward_copy[...] = here + source * 1024 + target * 65536
    copies = [
        pltpu.make_async_copy(fetched_copy, fetched, arrived.at[0]),
        pltpu.make_async_copy(forward_copy, forward, arrived.at[1]),
    ]
    for copy in copies:
        copy.start()
    slots[...] = slot
    steps[0] = n_steps
    for copy in copies:
        copy.wait()


def pick(ids, rows, columns, n_out, n_back):
    length = rows.shape[-1] + max(n_out * (FORWARD - 1), n_back * (BACKWARD - 1)) + 2 * PER
    length = -(-length // TILE) * TILE
    listed = (1, length)
    return pl.pallas_call(
        functools.partial(pick_kernel, n_out),
        out_shape=[
            pltpu.SMEM(listed, jnp.int32),
            pltpu.SMEM(listed, jnp.int32),
            pltpu.SMEM((1,), jnp.int32),
            pltpu.SMEM((3,), jnp.int32),
            pltpu.VMEM(rows.shape[1:], jnp.int32),
        ],
        in_specs=[SMEM, VMEM, VMEM],
        out_specs=[SMEM, SMEM, SMEM, SMEM, VMEM],
        scratch_shapes=[
            pltpu.VMEM(listed, jnp.int32),
            pltpu.VMEM(listed, jnp.int32),
            pltpu.SemaphoreType.DMA((2,)),
        ],
        compiler_params=PICK_PARAMS,
        name="pick_tiles",
    )(ids, far(rows), far(columns))


def start_fetch(tiles, fetched, held, arrived, g, carry):
    for j in range(PER):
        source = tiles.at[fetched[0, g * PER + j]]
        pltpu.make_async_copy(source, held.at[g * PER + j], arrived.at[g]).start()
    return carry


def end_fetch(tiles, held, arrived, g, carry):
    block = held.at[pl.ds(g * PER, PER)]
    pltpu.make_async_copy(tiles.at[pl.ds(0, PER)], block, arrived.at[g]).wait()
    return carry


def early_kernel(steps, fetched, tiles, early, arrived):
    count = jnp.minimum(steps[0], EARLY)
    lax.fori_loop(0, count, functools.partial(start_fetch, tiles, fetched, early, arrived), 0)
    early[early.shape[0] - 1] = jnp.zeros((TILE, TILE), BF16)
    lax.fori_loop(0, count, functools.partial(end_fetch, tiles, early, arrived), 0)


def early_tiles(steps, fetched, tiles):
    return pl.pallas_call(
        early_kernel,
        out_shape=pltpu.VMEM((EARLY * PER + 1, TILE, TILE), BF16),
        in_specs=[SMEM, SMEM, ANY],
        out_specs=VMEM,
        scratch_shapes=[pltpu.SemaphoreType.DMA((EARLY,))],
        compiler_params=PARAMS,
        name="early_tiles",
    )(scalar(steps), scalar(fetched), far(tiles))


def prepare_kernel(n_back, ids, rows, columns, slots, weight, bias, cotangent, *refs):
    backward, steps, weight_copy, bias_copy, cotangent_copy = refs[:5]
    row_copy, column_copy, backward_copy, arrived = refs[5:]
    pairs = [
        (rows.at[0], row_copy),
        (columns.at[0], column_copy),
        (weight, weight_copy),
        (bias, bias_copy),
        (cotangent, cotangent_copy),
    ]
    copies = [
        pltpu.make_async_copy(source, target, arrived.at[k])
        for k, (source, target) in enumerate(pairs)
    ]
    for copy in copies:
        copy.start()
    for copy in copies:
        copy.wait()
    row, column, slot = row_copy[...], column_copy[...], slots[...]
    length = backward.shape[1]
    owner = jnp.bitwise_xor(column >> 2, ids[2])
    chip = owner >> 1
    chip = jnp.where(chip == 2, 0, jnp.where(chip == 1, 1, jnp.where(chip == 3, 2, 3)))
    place = chip * 4 + (owner & 1) * 2 + (column & 1)
    source = jnp.bitwise_xor(row >> 2, ids[1]) * 4 + (row & 3)
    used = slot >= 0
    items, source, target, n_steps, slot, n_first = order(
        place, used, source, slot, n_back, length, BACKWARD, 4
    )
    here = jnp.where(items >= 0, items, SPARE)
    backward_copy[...] = here + source * 1024 + target * 65536
    copy = pltpu.make_async_copy(backward_copy, backward, arrived.at[5])
    copy.start()
    steps[0] = n_first
    steps[1] = n_steps
    copy.wait()


def prepare(ids, rows, columns, slots, length, n_back, weight, bias, cotangent):
    return pl.pallas_call(
        functools.partial(prepare_kernel, n_back),
        out_shape=[
            pltpu.SMEM((1, length), jnp.int32),
            pltpu.SMEM((2,), jnp.int32),
            pltpu.VMEM(weight.shape, weight.dtype),
            pltpu.VMEM(bias.shape, bias.dtype),
            pltpu.VMEM(cotangent.shape, cotangent.dtype),
        ],
        in_specs=[SMEM, ANY, ANY, VMEM, ANY, ANY, ANY],
        out_specs=[SMEM, SMEM, VMEM, VMEM, VMEM],
        scratch_shapes=[
            pltpu.VMEM(rows.shape[1:], jnp.int32),
            pltpu.VMEM(rows.shape[1:], jnp.int32),
            pltpu.VMEM((1, length), jnp.int32),
            pltpu.SemaphoreType.DMA((6,)),
        ],
        compiler_params=PICK_PARAMS,
        name="prepare",
    )(scalar(ids), far(rows), far(columns), near(slots), far(weight), far(bias), far(cotangent))


def join_kernel(a, b, out):
    rows = a.shape[0]
    out[0:rows] = a[...]
    out[rows : 2 * rows] = b[...]


def join(a, b):
    return pl.pallas_call(
        join_kernel,
        out_shape=pltpu.VMEM((2 * a.shape[0], a.shape[1]), a.dtype),
        in_specs=[VMEM] * 2,
        out_specs=VMEM,
        compiler_params=PARAMS,
        name="join",
    )(near(a), near(b))


def add_products(flipped, first, picked, held, source, total):
    last = held.shape[0] - 1
    width = BACKWARD if flipped else FORWARD
    places = []
    products = []
    for at in range(0, PER, width):
        codes = [picked[0, first + at + j] for j in range(width)]
        places.append(codes[0] >> 16)
        mine = [held[jnp.minimum(code & 1023, last)] for code in codes]
        other = [source[(code >> 10) & 63] for code in codes]
        left, right = (other, mine) if flipped else (mine, other)
        products.append(
            jnp.dot(
                jnp.concatenate(left, 1), jnp.concatenate(right, 0), preferred_element_type=F32
            )
        )
    for place, product in zip(places, products):
        total[place] += product


def run_steps(first, last, step):
    passes = (last - first) // MERGED

    def merged(k, carry):
        for j in range(MERGED):
            step(first + k * MERGED + j)
        return carry

    def single(g, carry):
        step(g)
        return carry

    lax.fori_loop(0, passes, merged, 0)
    lax.fori_loop(first + passes * MERGED, last, single, 0)


def forward_kernel(steps, ids, fetched, picked, tiles, early, *refs):
    sources, (held, kept, distant, sent, gathered, total, arrived) = refs[:-7], refs[-7:]
    count = steps[0]
    start = functools.partial(start_fetch, tiles, fetched, held, arrived)
    lax.fori_loop(EARLY, jnp.maximum(count, EARLY), start, 0)
    moved = pltpu.make_async_copy(
        early.at[pl.ds(0, EARLY * PER)], held.at[pl.ds(0, EARLY * PER)], arrived.at[0]
    )
    moved.start()
    held[held.shape[0] - 1] = jnp.zeros((TILE, TILE), BF16)
    total[...] = jnp.zeros_like(total)
    for m, source in enumerate(sources):
        gathered[4 * m : 4 * m + 4] = source[...].reshape(4, TILE, TILE)

    def early_step(g):
        add_products(False, g * PER, picked, early, gathered, total)

    def step(g):
        end_fetch(tiles, held, arrived, g, 0)
        add_products(False, g * PER, picked, held, gathered, total)

    run_steps(0, jnp.minimum(count, EARLY), early_step)
    run_steps(EARLY, jnp.maximum(count, EARLY), step)
    moved.wait()
    for k in range(kept.shape[0]):
        own = jnp.bitwise_xor(ids[1], 2 * k)
        kept[k] = total[pl.ds(own * 4, 4)]
        value = total[pl.ds(jnp.bitwise_xor(own, 1) * 4, 4)].astype(BF16)
        if k == 2:
            distant[...] = value
        else:
            sent[min(k, 2)] = value


def tiles_forward(steps, ids, fetched, picked, tiles, early, sources, n_out):
    shape = (n_out // 8, 4, TILE, TILE)
    length = -(-(tiles.shape[0] + n_out * (FORWARD - 1)) // PER) * PER
    return pl.pallas_call(
        forward_kernel,
        out_shape=[
            pltpu.VMEM((length + 1, TILE, TILE), BF16),
            pltpu.VMEM(shape, F32),
            pltpu.VMEM(shape[1:], BF16),
            pltpu.VMEM((shape[0] - 1, *shape[1:]), BF16),
        ],
        in_specs=[SMEM, SMEM, SMEM, SMEM, ANY, VMEM] + [VMEM] * len(sources),
        out_specs=[VMEM] * 4,
        scratch_shapes=[
            pltpu.VMEM((4 * len(sources), TILE, TILE), BF16),
            pltpu.VMEM((n_out + 1, TILE, TILE), F32),
            pltpu.SemaphoreType.DMA((length // PER,)),
        ],
        compiler_params=PARAMS,
        name="tiles_forward",
    )(
        scalar(steps),
        scalar(ids),
        scalar(fetched),
        scalar(picked),
        far(tiles),
        near(early),
        *[near(values) for values in sources],
    )


def write_terms(values, message, row):
    rest = jnp.concatenate([values, values], 0)
    line = iota(rest.shape, 0)
    terms = jnp.zeros(rest.shape, F32)
    for k in range(3):
        term = rest.astype(BF16).astype(F32)
        terms = jnp.where(line == k, term, terms)
        rest = rest - term
    message[row : row + 16] = terms.astype(BF16)


def read_terms(messages, row):
    terms = jnp.zeros((16, TILE), F32)
    for one in messages:
        terms = terms + one[row : row + 16].astype(F32)
    return jnp.broadcast_to(jnp.sum(terms, axis=0, keepdims=True), (8, TILE))


def first_kernel(steps, ids, picked, held, *refs):
    messages, (gathered, grads, out, total) = refs[:-4], refs[-4:]
    total[...] = jnp.zeros_like(total)
    rows = 4 * TILE
    for m, one in enumerate(messages):
        gathered[4 * m : 4 * m + 4] = one[0:rows].reshape(4, TILE, TILE)

    for k in range(2):
        weight = jnp.zeros((TILE // 2, TILE), F32)
        for one in messages[k::2]:
            weight = weight + one[rows : rows + TILE // 2].astype(F32)
        grads[pl.ds(jnp.bitwise_xor(ids[1] & 1, k) * (TILE // 2), TILE // 2)] = weight
    bias = read_terms(messages[0::2], rows + TILE // 2)
    grads[TILE : TILE + 8] = bias
    out[rows : rows + TILE] = grads[0:TILE].astype(BF16)
    write_terms(bias, out, rows + TILE)
    run_steps(0, steps[0], lambda g: add_products(True, g * PER, picked, held, gathered, total))
    out[0:rows] = total[0:4].reshape(rows, TILE).astype(BF16)


def tiles_first(steps, ids, picked, held, sources):
    rows = 4 * TILE
    return pl.pallas_call(
        first_kernel,
        out_shape=[
            pltpu.VMEM((4 * len(sources), TILE, TILE), BF16),
            pltpu.VMEM((TILE + 8, TILE), F32),
            pltpu.VMEM((rows + TILE + 16, TILE), BF16),
        ],
        in_specs=[SMEM, SMEM, SMEM] + [VMEM] * (1 + len(sources)),
        out_specs=[VMEM] * 3,
        scratch_shapes=[pltpu.VMEM((5, TILE, TILE), F32)],
        compiler_params=PARAMS,
        name="tiles_first",
    )(scalar(steps), scalar(ids), scalar(picked), near(held), *[near(values) for values in sources])


def second_kernel(steps, picked, held, gathered, grads, kept, second, third, total):
    total[...] = jnp.zeros_like(total)
    rows = 4 * TILE
    for out in (second, third):
        out[rows : rows + TILE] = grads[0:TILE].astype(BF16)
        write_terms(grads[TILE : TILE + 8], out, rows + TILE)
    run_steps(steps[0], steps[1], lambda g: add_products(True, g * PER, picked, held, gathered, total))
    for k, out in enumerate((second, third, kept)):
        out[0:rows] = total[4 * k + 4 : 4 * k + 8].reshape(rows, TILE).astype(out.dtype)


def tiles_second(steps, picked, held, gathered, grads, n_back):
    rows = 4 * TILE
    return pl.pallas_call(
        second_kernel,
        out_shape=[pltpu.VMEM((rows, TILE), F32)]
        + [pltpu.VMEM((rows + TILE + 16, TILE), BF16)] * 2,
        in_specs=[SMEM, SMEM] + [VMEM] * 3,
        out_specs=[VMEM] * 3,
        scratch_shapes=[pltpu.VMEM((n_back + 1, TILE, TILE), F32)],
        compiler_params=PARAMS,
        cost_estimate=pl.CostEstimate(
            flops=held.shape[0] * 2 * TILE**3,
            bytes_accessed=held.shape[0] * 2 * TILE**2,
            transcendentals=0,
        ),
        name="tiles_second",
    )(scalar(steps), scalar(picked), near(held), near(gathered), near(grads))


def distant_kernel(kept, got, out):
    out[...] = (kept[2] + got[...].astype(F32)).astype(BF16)


def distant_sum(kept, got):
    return pl.pallas_call(
        distant_kernel,
        out_shape=pltpu.VMEM(got.shape, BF16),
        in_specs=[VMEM] * 2,
        out_specs=VMEM,
        compiler_params=PARAMS,
        name="distant_sum",
    )(near(kept), near(got))


def pair_kernel(kept, got, first, second, third):
    first[...] = kept[0] + got[0].astype(F32)
    second[...] = (kept[1] + got[1].astype(F32)).astype(BF16)
    third[...] = (kept[3] + got[2].astype(F32)).astype(BF16)


def pair_sum(kept, got):
    shape = kept.shape[1:]
    return pl.pallas_call(
        pair_kernel,
        out_shape=[pltpu.VMEM(shape, F32)] + [pltpu.VMEM(shape, BF16)] * 2,
        in_specs=[VMEM] * 2,
        out_specs=[VMEM] * 3,
        compiler_params=PARAMS,
        name="pair_sum",
    )(near(kept), near(got))


def own_kernel(first, a, b, c, total, sent):
    value = first[...] + a[...].astype(F32) + b[...].astype(F32) + c[...].astype(F32)
    total[...] = value
    sent[...] = value.astype(BF16)


def own_sum(first, others):
    return pl.pallas_call(
        own_kernel,
        out_shape=[pltpu.VMEM(first.shape, F32), pltpu.VMEM(first.shape, BF16)],
        in_specs=[VMEM] * 4,
        out_specs=[VMEM] * 2,
        compiler_params=PARAMS,
        name="own_sum",
    )(near(first), *[near(values) for values in others])


def middle_kernel(own, other, weight, bias, cotangent, activations, back, back_sent, grads):
    blocks = own.shape[0]
    rows = blocks * TILE
    sums = (own[...] + other[...].astype(F32)).astype(BF16).reshape(rows, TILE)
    preact = jnp.dot(sums, weight[...], preferred_element_type=F32) + bias[...]
    sigma = jax.nn.sigmoid(preact)
    activations[...] = (preact * sigma).astype(BF16)
    grad = cotangent[...].astype(F32) * (sigma * (1.0 + preact * (1.0 - sigma)))
    grad_pre = grad.astype(BF16)
    grads[0:TILE] = lax.dot_general(
        sums, grad_pre, (((0,), (0,)), ((), ())), preferred_element_type=F32
    )
    total = jnp.sum(grad_pre.astype(F32), axis=0, keepdims=True)
    grads[TILE : TILE + 8] = jnp.broadcast_to(total, (8, TILE))
    for b in range(blocks):
        value = lax.dot_general(
            weight[...],
            grad_pre[b * TILE : (b + 1) * TILE],
            (((1,), (1,)), ((), ())),
            preferred_element_type=F32,
        )
        back[b] = value
        back_sent[b] = value.astype(BF16)


def middle(own, other, weight, bias, cotangent):
    return pl.pallas_call(
        middle_kernel,
        out_shape=[
            jax.ShapeDtypeStruct(cotangent.shape, BF16),
            pltpu.VMEM(own.shape, F32),
            pltpu.VMEM(own.shape, BF16),
            pltpu.VMEM((TILE + 8, TILE), F32),
        ],
        in_specs=[VMEM] * 5,
        out_specs=[VMEM] * 4,
        compiler_params=PARAMS,
        name="middle",
    )(near(own), near(other), near(weight), near(bias), near(cotangent))


def message_kernel(ids, back, other, grads, more, message):
    rows = back.shape[0] * TILE
    value = back[...] + other[...].astype(F32)
    message[0:rows] = value.astype(BF16).reshape(rows, TILE)
    half = pl.ds((ids[1] & 1) * (TILE // 2), TILE // 2)
    message[rows : rows + TILE // 2] = (grads[half] + more[half]).astype(BF16)
    write_terms(grads[TILE : TILE + 8] + more[TILE : TILE + 8], message, rows + TILE // 2)


def message(ids, back, other, grads, more):
    rows = back.shape[0] * TILE + TILE // 2 + 16
    return pl.pallas_call(
        message_kernel,
        out_shape=pltpu.VMEM((rows, TILE), BF16),
        in_specs=[SMEM] + [VMEM] * 4,
        out_specs=VMEM,
        compiler_params=PARAMS,
        name="message",
    )(scalar(ids), near(back), near(other), near(grads), near(more))


def near_kernel(kept, grads, a, value, sums):
    rows = kept.shape[0]
    value[...] = kept[...] + a[0:rows].astype(F32)
    sums[0:TILE] = grads[0:TILE] + a[rows : rows + TILE].astype(F32)
    sums[TILE : TILE + 8] = grads[TILE : TILE + 8] + read_terms((a,), rows + TILE)


def first_sum(kept, grads, message):
    return pl.pallas_call(
        near_kernel,
        out_shape=[pltpu.VMEM(kept.shape, F32), pltpu.VMEM(grads.shape, F32)],
        in_specs=[VMEM] * 3,
        out_specs=[VMEM] * 2,
        compiler_params=PARAMS,
        name="first_sum",
    )(near(kept), near(grads), near(message))


def line_kernel(kept, grads, a, b, own_sent, other_sent, other_message, own, own_grads):
    rows = own.shape[0]
    value = kept[...]
    weight = grads[0:TILE]
    for one in (a, b):
        value = value + one[0 : 2 * rows].astype(F32)
        weight = weight + one[2 * rows : 2 * rows + TILE].astype(F32)
    bias = grads[TILE : TILE + 8] + read_terms((a, b), 2 * rows + TILE)
    own[...] = value[:rows]
    own_sent[...] = value[:rows].astype(BF16)
    other = value[rows:].astype(BF16)
    other_sent[...] = other
    own_grads[0:TILE] = weight
    own_grads[TILE : TILE + 8] = bias
    other_message[0:rows] = other
    other_message[rows : rows + TILE] = weight.astype(BF16)
    write_terms(bias, other_message, rows + TILE)


def line_sum(kept, grads, messages):
    rows = kept.shape[0] // 2
    return pl.pallas_call(
        line_kernel,
        out_shape=[
            pltpu.VMEM((rows, TILE), BF16),
            pltpu.VMEM((rows, TILE), BF16),
            pltpu.VMEM((rows + TILE + 16, TILE), BF16),
            pltpu.VMEM((rows, TILE), F32),
            pltpu.VMEM(grads.shape, F32),
        ],
        in_specs=[VMEM] * 4,
        out_specs=[VMEM] * 5,
        compiler_params=PARAMS,
        name="line_sum",
    )(near(kept), near(grads), *[near(one) for one in messages])


def finish_kernel(ids, own, grads, opposite, corner, beside, features, weight, bias):
    rows = own.shape[0]
    for b in range(rows // TILE):
        block = pl.ds(b * TILE, TILE)
        mine = own[block] + beside[block].astype(F32)
        other = opposite[block].astype(F32) + corner[block].astype(F32)
        features[pl.ds(ids[0] * rows + b * TILE, TILE)] = mine.T
        features[pl.ds((1 - ids[0]) * rows + b * TILE, TILE)] = other.T
    weight[...] = grads[0:TILE] + beside[rows : rows + TILE].astype(F32)
    bias[...] = (grads[TILE : TILE + 8] + read_terms((beside,), rows + TILE))[0:1]


def finish(ids, own, grads, opposite, corner, beside):
    return pl.pallas_call(
        finish_kernel,
        out_shape=[
            jax.ShapeDtypeStruct((2 * own.shape[0], TILE), F32),
            jax.ShapeDtypeStruct((TILE, TILE), F32),
            jax.ShapeDtypeStruct((1, TILE), F32),
        ],
        in_specs=[SMEM] + [VMEM] * 5,
        out_specs=[VMEM] * 3,
        compiler_params=PARAMS,
        name="finish",
    )(scalar(ids), near(own), near(grads), near(opposite), near(corner), near(beside))


def local(
    features, weight, hidden_bias, adjacency_tiles, tile_rows, tile_columns, tile_count, cotangent
):
    tiles = adjacency_tiles[0, 0]
    n_row, n_col = lax.axis_size("row"), lax.axis_size("col")
    own_rows, fin = features.shape
    blocks = own_rows // TILE
    n_out, n_back = blocks * n_col, blocks // 2 * n_row
    half = lax.axis_index("feat")
    places = [half, lax.axis_index("col"), lax.axis_index("row"), tile_count[0, 0]]
    ids = jnp.stack(places).astype(jnp.int32)

    mine = lax.dynamic_slice_in_dim(features, half * (own_rows // 2), own_rows // 2, 0)
    mine, ids = lax.optimization_barrier((mine, ids))
    lists = pick(ids, tile_rows, tile_columns, n_out, n_back)
    beside, lists = lax.optimization_barrier((swap(mine, "row", 1), lists))
    fetched, forward, steps, ids, slots = lists
    pair = join(mine, beside)
    second, first, third = swap_line([pair] * 3, "row")
    early = early_tiles(steps, fetched, tiles)
    early, first, third, second = lax.optimization_barrier((early, first, third, second))

    held, kept, distant, sent = tiles_forward(steps, ids, fetched, forward, tiles, early, [pair, first, second, third], n_out)
    distant = distant_sum(kept, swap(distant, "col", 1))
    first, second, third = pair_sum(kept, swap(sent, "col", 1))
    others = swap_line([distant, second, third], "col")
    own, sent = own_sum(first, others)
    sent, slots = lax.optimization_barrier((sent, slots))
    ready = prepare(
        ids, tile_rows, tile_columns, slots, forward.shape[1], n_back, weight, hidden_bias[None], cotangent
    )
    other, ready = lax.optimization_barrier((swap(sent, "feat", 1), ready))
    backward, steps, weight, bias, cotangent = ready
    activations, back, back_sent, grads = middle(own, other, weight, bias, cotangent)

    back_other, more = lax.optimization_barrier((swap(back_sent, "feat", 1), swap(grads, "col", 1)))
    mine = message(ids, back, back_other, grads, more)
    across = [swap(mine, "col", mask) for mask in (2, 6, 4)]
    beside = swap(mine, "col", 1)
    across = lax.optimization_barrier(across)
    corners = [swap(values, "col", 1) for values in across]
    sources = [mine, beside, across[0], corners[0], across[2], corners[2], across[1], corners[1]]
    gathered, grads, first = tiles_first(steps, ids, backward, held, sources)

    first = swap(first, "row", 4)
    kept, second, third = tiles_second(steps, backward, held, gathered, grads, n_back)
    others = [swap(second, "row", 2), swap(third, "row", 6)]
    kept, grads = first_sum(kept, grads, first)
    own_sent, other_sent, other_message, own, grads = line_sum(kept, grads, others)
    opposite = swap(own_sent, "feat", 1)
    corner = swap(other_sent, ("row", "feat"), 3)
    beside = swap(other_message, "row", 1)
    grad_features, grad_weight, grad_bias = finish(ids, own, grads, opposite, corner, beside)
    return (activations, grad_features, grad_weight, grad_bias[0])


def solution(mesh):
    placed = (
        P(("col", "row"), None),
        P(None, "feat"),
        P("feat"),
        P("row", "col", None, None, None),
        P("row", "col", None),
        P("row", "col", None),
        P("row", "col"),
        P(("row", "col"), "feat"),
    )
    return jax.shard_map(
        local,
        mesh=mesh,
        in_specs=placed,
        out_specs=(P(("row", "col"), "feat"), P(("col", "row"), None), P(None, "feat"), P("feat")),
        check_vma=False,
    )
```
